32 devices in a mesh: rep: 2 (over core), fsdp: 16 (over z, y, x).
Axes of the slice: x: 2, y: 2, z: 4, core: 2. Of those that a mesh axis runs over, the one named last changes fastest.
Arguments:
- tokens: bfloat16 [4096, 1024], P(('rep', 'fsdp')), may hold values from -6 to 6
- segment_ids: int32 [32, 128], P(('rep', 'fsdp')), may hold values from 0 to 3, never falling along the last dimension, each value on 1 to 64 neighbouring positions
- norm_gain: float32 [1024], replicated, may hold values from 0.5 to 1.5
- in_weight: bfloat16 [1024, 4384], P('fsdp'), may hold values from -0.1875 to 0.1875
- conv_weight: float32 [4, 2304], replicated, may hold values from -3 to 3
- conv_bias: float32 [2304], replicated, may hold values from -3 to 3
- dt_bias: float32 [32], replicated, may hold values from -7 to -2.5
- a_log: float32 [32], replicated, may hold values from 0 to 2.5
- skip_gain: float32 [32], replicated, may hold values from 0.5 to 1.5
- gate_gain: float32 [2048], replicated, may hold values from 0.5 to 1.5
- out_weight: bfloat16 [2048, 1024], P('fsdp'), may hold values from -0.125 to 0.125
- cotangent: bfloat16 [4096, 1024], P(('rep', 'fsdp')), may hold values from -6 to 6
Outputs:
- block_out: bfloat16 [4096, 1024], P(('rep', 'fsdp'))
- d_tokens: float32 [4096, 1024], P(('rep', 'fsdp'))
- d_norm_gain: float32 [1024], replicated
- d_in_weight: float32 [1024, 4384], P('fsdp')
- d_conv_weight: float32 [4, 2304], replicated
- d_conv_bias: float32 [2304], replicated
- d_dt_bias: float32 [32], replicated
- d_a_log: float32 [32], replicated
- d_skip_gain: float32 [32], replicated
- d_gate_gain: float32 [2048], replicated
- d_out_weight: float32 [2048, 1024], P('fsdp')
The draws below stay inside these ranges and needn't reach their ends.
Inputs may be any that keep to these rules, and one draw needn't show every extreme that they name: `segment_ids`: each row is one packed sequence; its segment numbers start at 0, never fall, rise by at most one from a position to the next, and each segment has at most 64 tokens.
All inputs are finite; a program needn't handle non-finite values.
Results may differ from the reference program's by a relative error of at most 0.0071.
Values may be sent and summed in bfloat16 or wider, within the bound.
No kernel may reach another device: no remote copies, remote signals or barrier semaphores. Data moves between devices by JAX's collectives and lax.ppermute only.
A program may use at most 128 MiB of HBM per device.

```python
import math
import jax
import jax.numpy as jnp
import numpy as np
from jax import lax

D = 1024
HEADS = 32
CONV = 4
BLOCK = 64
SEQ = 128
INNER = 2048
XBC = 2304
PROJ = 4384
SEQUENCES = 32
TOKENS = 4096


def shard_levels(key, dims, cuts, smallest, high):
    level, own = 1.0, jax.random.fold_in(key, 6)
    for axis_at, parts in cuts:
        heights = jnp.exp(jax.random.uniform(jax.random.fold_in(own, axis_at), (parts,), jnp.float32, smallest / len(cuts), high / len(cuts)))
        level = level * jnp.repeat(heights, dims[axis_at] // parts).reshape([-1 if axis == axis_at else 1 for axis in range(len(dims))])
    return level


def length_profile(count, total, bound, lean):
    portions = [(1 << 20) // math.isqrt(grade ** lean) + 1 for grade in range(2, count + 1)]
    surplus, given = total - bound - (count - 1), [1] * (count - 1)
    while surplus > 0:
        movable = [i for i in range(count - 1) if given[i] < bound]
        mass, left = sum([portions[i] for i in movable]), surplus
        for i in movable:
            more = min(bound - given[i], max(1, left * portions[i] // mass), surplus)
            given[i] = given[i] + more
            surplus = surplus - more
    return np.array([bound] + given)


def ragged_sizes(key, amount, total, bound, lean):
    if amount == 2:
        one = jax.random.randint(key, (), max(1, total - bound), min(bound, total - 1) + 1)
        return jnp.stack([one, total - one])
    sizes = jnp.asarray(length_profile(amount, total, bound, lean), jnp.int32)
    pairs = (amount - 1) // 2
    donor, taker = sizes[1:1 + 2 * pairs:2], sizes[2:2 + 2 * pairs:2]
    slack = jnp.minimum(donor - 1, bound - taker)
    shifted = jax.random.randint(jax.random.fold_in(key, 1), (pairs,), 0, 1 << 20) % (slack + 1)
    sizes = sizes.at[1:1 + 2 * pairs:2].set(donor - shifted).at[2:2 + 2 * pairs:2].set(taker + shifted)
    return sizes[jax.random.permutation(jax.random.fold_in(key, 2), amount)]


def normal_values(key, extent, deviation, most, pieces=(), held_as=jnp.bfloat16):
    drawn = deviation * jax.random.normal(key, extent, jnp.float32)
    if pieces:
        drawn = drawn * shard_levels(key, extent, pieces, -0.22, 0.18)
    return jnp.clip(drawn, -most, most).astype(held_as)


def setup_inputs(seed: int = 0) -> dict:
    key_list = jax.random.split(jax.random.key(seed), 13)
    return {
        "tokens": normal_values(key_list[0], (TOKENS, D), 1.0, 6.0, ((0, 32),)),
        "segment_ids": jax.vmap(lambda own: jnp.searchsorted(jnp.cumsum(ragged_sizes(own, 4, SEQ, SEQ // 2, 0)), jnp.arange(SEQ), side="right"))(jax.random.split(key_list[1], SEQUENCES)).reshape((SEQUENCES, SEQ)).astype(jnp.int32),
        "norm_gain": jnp.clip(1.0 + 0.1 * jax.random.normal(key_list[2], (D,), jnp.float32), 0.5, 1.5),
        "in_weight": normal_values(key_list[3], (D, PROJ), D ** -0.5, 0.1875, ((0, 16),)),
        "conv_weight": normal_values(key_list[4], (CONV, XBC), CONV ** -0.5, 3.0, (), jnp.float32),
        "conv_bias": normal_values(key_list[5], (XBC,), 0.3, 3.0, (), jnp.float32),
        "dt_bias": jnp.clip(jax.random.uniform(key_list[6], (HEADS,), jnp.float32, -7.0, -2.5), -7.0, -2.5),
        "a_log": jnp.clip(jax.random.uniform(key_list[7], (HEADS,), jnp.float32, 0.0, 2.5), 0.0, 2.5),
        "skip_gain": jnp.clip(jax.random.uniform(key_list[8], (HEADS,), jnp.float32, 0.5, 1.5), 0.5, 1.5),
        "gate_gain": jnp.clip(1.0 + 0.1 * jax.random.normal(key_list[9], (INNER,), jnp.float32), 0.5, 1.5),
        "out_weight": normal_values(key_list[10], (INNER, D), INNER ** -0.5, 0.125, ((0, 16),)),
        "cotangent": normal_values(key_list[11], (TOKENS, D), 1.0, 6.0, ((0, 32),)),
    }


@jax.custom_vjp
def low(v):
    return lax.optimization_barrier(v.astype(jnp.bfloat16)).astype(jnp.float32)

@jax.custom_vjp
def low_back(v):
    return v

def low_keep(v):
    return (low(v), None)

def low_pass(kept, grad):
    return (grad,)

def back_keep(v):
    return (v, None)

def back_low(kept, grad):
    return (low(grad),)
low.defvjp(low_keep, low_pass)
low_back.defvjp(back_keep, back_low)
epsilon = 1e-05
highest = lax.Precision.HIGHEST

def rms_normed(hidden, gain):
    factor = lax.rsqrt(lax.optimization_barrier(jnp.mean(hidden * hidden, axis=-1, keepdims=True)) + epsilon)
    return hidden * factor * gain

def mixer(projected, segments, conv_weight, conv_bias, dt_bias, a_log, skip_gain, gate_gain):
    seq_count = projected.shape[0]
    seq_len = projected.shape[1]
    inner_dim = gate_gain.shape[0]
    head_count = dt_bias.shape[0]
    conv_dim = conv_bias.shape[0]
    state_dim = (conv_dim - inner_dim) // 2
    head_dim = inner_dim // head_count
    kernel_len = conv_weight.shape[0]
    gate_part = projected[:, :, :inner_dim]
    signal = projected[:, :, inner_dim:inner_dim + conv_dim]
    step_raw = projected[:, :, inner_dim + conv_dim:]
    mixed_conv = conv_bias + conv_weight[kernel_len - 1] * signal
    for offset in range(1, kernel_len):
        earlier = jnp.pad(signal, ((0, 0), (offset, 0), (0, 0)))[:, :seq_len]
        earlier_seg = jnp.pad(segments, ((0, 0), (offset, 0)), constant_values=-1)[:, :seq_len]
        same_doc = (earlier_seg == segments).astype(jnp.float32)[:, :, None]
        mixed_conv = mixed_conv + conv_weight[kernel_len - 1 - offset] * earlier * same_doc
    activated = jax.nn.silu(mixed_conv)
    values = activated[:, :, :inner_dim].reshape(seq_count, seq_len, head_count, head_dim)
    in_state = activated[:, :, inner_dim:inner_dim + state_dim]
    out_state = activated[:, :, inner_dim + state_dim:]
    step_size = jax.nn.softplus(step_raw + dt_bias)
    log_decay = -step_size * jnp.exp(a_log)
    scaled = values * step_size[..., None]
    blocks = seq_len // BLOCK
    total = seq_count * blocks
    seg_block = segments.reshape(total, BLOCK)
    entry_seg = jnp.pad(segments, ((0, 0), (1, 0)), constant_values=-1)[:, :seq_len].reshape(total, BLOCK)[:, 0]
    cumul = jnp.cumsum(log_decay.reshape(total, BLOCK, head_count), axis=1)
    keys_blk = in_state.reshape(total, BLOCK, state_dim)
    query_blk = out_state.reshape(total, BLOCK, state_dim)
    value_blk = scaled.reshape(total, BLOCK, head_count, head_dim)
    scores = jnp.einsum('ktn,ksn->kts', query_blk, keys_blk, precision=highest)
    places = jnp.arange(BLOCK)
    visible = (places[:, None] >= places[None, :])[None] & (seg_block[:, :, None] == seg_block[:, None, :])
    cumul_heads = jnp.swapaxes(cumul, 1, 2)
    spread = cumul_heads[:, :, :, None] - cumul_heads[:, :, None, :]
    visible_heads = visible[:, None]
    weights = jnp.exp(jnp.where(visible_heads, spread, 0.0)) * visible_heads.astype(jnp.float32) * scores[:, None]
    inside = jnp.einsum('khts,kshp->kthp', weights, value_blk, precision=highest)
    same_last = (seg_block == seg_block[:, -1:]).astype(jnp.float32)
    tail_weight = jnp.exp(cumul[:, -1:, :] - cumul) * same_last[:, :, None]
    contrib = jnp.einsum('kshp,ksn->khpn', value_blk * tail_weight[..., None], keys_blk, precision=highest)
    carry_keep = jnp.exp(cumul[:, -1, :]) * (entry_seg == seg_block[:, -1]).astype(jnp.float32)[:, None]
    contrib_seq = jnp.swapaxes(contrib.reshape(seq_count, blocks, head_count, head_dim, state_dim), 0, 1)
    keep_seq = jnp.swapaxes(carry_keep.reshape(seq_count, blocks, head_count), 0, 1)

    def advance(carried, scanned):
        added, factor = scanned
        return (factor[:, :, None, None] * carried + added, carried)
    start_state = jnp.zeros((seq_count, head_count, head_dim, state_dim), jnp.float32)
    final_state, entering = lax.scan(advance, start_state, (contrib_seq, keep_seq))
    entering = jnp.swapaxes(entering, 0, 1).reshape(total, head_count, head_dim, state_dim)
    reach = jnp.exp(cumul) * (seg_block == entry_seg[:, None]).astype(jnp.float32)[:, :, None]
    carried_out = jnp.einsum('ktn,khpn->kthp', query_blk, entering, precision=highest) * reach[..., None]
    result = (inside + carried_out).reshape(seq_count, seq_len, head_count, head_dim) + skip_gain[:, None] * values
    result = result.reshape(seq_count, seq_len, inner_dim) * jax.nn.silu(gate_part)
    return rms_normed(result, gate_gain)

def forward(hidden, segments, params):
    norm_gain, in_weight, conv_weight, conv_bias, dt_bias, a_log, skip_gain, gate_gain, out_weight = params
    seq_count = segments.shape[0]
    seq_len = segments.shape[1]
    normed = low(rms_normed(hidden, norm_gain))
    projected = low_back(jnp.dot(normed, in_weight, precision=highest))
    gated = mixer(projected.reshape(seq_count, seq_len, -1), segments, conv_weight, conv_bias, dt_bias, a_log, skip_gain, gate_gain)
    gated = low(gated.reshape(seq_count * seq_len, -1))
    return hidden + jnp.dot(gated, out_weight, precision=highest)

def reference(tokens, segment_ids, norm_gain, in_weight, conv_weight, conv_bias, dt_bias, a_log, skip_gain, gate_gain, out_weight, cotangent):
    params = tuple((entry.astype(jnp.float32) for entry in (norm_gain, in_weight, conv_weight, conv_bias, dt_bias, a_log, skip_gain, gate_gain, out_weight)))
    seq_total = segment_ids.shape[0]
    group_size = math.gcd(seq_total, max(1, 4096 // SEQ))
    group_count = seq_total // group_size
    model_width = tokens.shape[1]
    inputs = tokens.astype(jnp.float32).reshape(group_count, group_size * SEQ, model_width)
    grads_in = cotangent.astype(jnp.float32).reshape(group_count, group_size * SEQ, model_width)
    seg_groups = segment_ids.reshape(group_count, group_size, SEQ)

    def scan_step(totals, scanned):
        group_tokens, group_segs, group_cot = scanned

        def apply_layer(hidden, weights):
            return forward(hidden, group_segs, weights)
        outcome, pullback = jax.vjp(apply_layer, group_tokens, params)
        d_hidden, d_params = pullback(group_cot)
        return (jax.tree.map(jnp.add, totals, d_params), (outcome.astype(jnp.bfloat16), d_hidden))
    zero_grads = jax.tree.map(jnp.zeros_like, params)
    totals, (outputs, d_hidden) = lax.scan(scan_step, zero_grads, (inputs, seg_groups, grads_in))
    block_out = outputs.reshape(-1, model_width)
    d_tokens = d_hidden.reshape(-1, model_width)
    return (block_out, d_tokens, totals[0], totals[1], totals[2], totals[3], totals[4], totals[5], totals[6], totals[7], totals[8])
```

```python
import functools

import jax
import jax.numpy as jnp
from jax import lax
from jax.experimental import pallas as pl
from jax.experimental.pallas import tpu as pltpu
from jax.sharding import PartitionSpec as P

epsilon = 1e-05
highest = lax.Precision.HIGHEST
f32 = jnp.float32
bf16 = jnp.bfloat16
LANES = 128
VMEM_LIMIT = 50 * 1024 * 1024
BOTH = ("rep", "fsdp")


def exact_dot(a, b, dims=((1,), (0,))):
    return lax.dot_general(a, b, (dims, ((), ())), precision=highest, preferred_element_type=f32)


def low_dot(a, b, dims=((1,), (0,))):
    return lax.dot_general(
        a.astype(bf16), b.astype(bf16), (dims, ((), ())), preferred_element_type=f32
    )


def iota(shape, dim):
    return lax.broadcasted_iota(jnp.int32, shape, dim)


def params(**kw):
    return pltpu.CompilerParams(vmem_limit_bytes=VMEM_LIMIT, **kw)


def in_vmem(n):
    return [pl.BlockSpec(memory_space=pltpu.VMEM)] * n


def in_smem(n):
    return [pl.BlockSpec(memory_space=pltpu.SMEM)] * n


def anywhere(n):
    return [pl.BlockSpec(memory_space=pl.ANY)] * n


def chunk_copies(pos_ref, chunks, whole, sems, inward):
    copies = []
    for at, chunk in enumerate(chunks):
        rows = chunk.shape[0]
        start = pl.multiple_of(pos_ref[at], 16)
        part = whole.at[pl.ds(start, rows)]
        source, target = (chunk, part) if inward else (part, chunk)
        copies.append(pltpu.make_async_copy(source, target, sems.at[at]))
    return copies


def silu_parts(v):
    sig = 1.0 / (1.0 + jnp.exp(-v))
    return sig, v * sig


def conv_block(proj_ref, masks_ref, cw_ref, cb_ref, inner, at):
    signal = proj_ref[:, pl.ds(pl.multiple_of(inner + at * LANES, LANES), LANES)]
    lanes = pl.ds(pl.multiple_of(at * LANES, LANES), LANES)
    taps = cw_ref.shape[0]
    mixed = cb_ref[:, lanes] + cw_ref[taps - 1 : taps, lanes] * signal
    for offset in range(1, taps):
        earlier = pltpu.roll(signal, offset, 0) * masks_ref[offset - 1]
        mixed = mixed + cw_ref[taps - 1 - offset : taps - offset, lanes] * earlier
    return signal, mixed


def decay_prep(proj_ref, heads_ref, inner, head_dim, stepe_ref, cume_ref, cumt_ref):
    tokens, width = proj_ref.shape
    raw = proj_ref[:, width - LANES :] + heads_ref[0:1, :]
    step = jnp.maximum(raw, 0.0) + jnp.log1p(jnp.exp(-jnp.abs(raw)))
    decay = -step * jnp.exp(heads_ref[1:2, :])
    lower = (iota((LANES, LANES), 0) >= iota((LANES, LANES), 1)).astype(f32)
    spread = (
        iota((LANES, inner), 1) // head_dim == iota((LANES, inner), 0)
    ).astype(f32)
    stepe_ref[...] = exact_dot(step, spread)
    for seq in range(tokens // LANES):
        rows = slice(seq * LANES, (seq + 1) * LANES)
        cumul = exact_dot(lower, decay[rows])
        cume_ref[rows, :] = exact_dot(cumul, spread)
        turned = cumul.T
        for pair in range(inner // LANES):
            cumt_ref[pair, 0:2, rows] = turned[2 * pair : 2 * pair + 2]
    return raw, step, decay


def pair_weights(cume_ref, cumt_ref, vis_ref, rows, lanes, pair, half):
    cols = cume_ref[rows, lanes]
    seen = vis_ref[rows, :] > 0.5
    first, second = cumt_ref[pair, 0:1, rows], cumt_ref[pair, 1:2, rows]
    fade_a = jnp.exp(jnp.where(seen, cols[:, 0:1] - first, -1e30))
    fade_b = jnp.exp(jnp.where(seen, cols[:, half : half + 1] - second, -1e30))
    return fade_a, fade_b


def split_heads(block, half):
    lane = iota(block.shape, 1)
    return jnp.concatenate(
        [jnp.where(lane < half, block, 0.0), jnp.where(lane >= half, block, 0.0)], axis=0
    )


def forward_kernel(
    chunk_count, inner, head_dim,
    pos_ref, tok_ref, gain_ref, masks_ref, vis_ref, cw_ref, cb_ref, heads_ref, skip_ref, *rest,
):
    chunks = rest[:chunk_count]
    normed_ref, proj_ref, mixer_ref, sq_ref, w_ref, act_ref, stepe_ref, cume_ref, cumt_ref, score_ref, sems = (
        rest[chunk_count:]
    )
    copies = chunk_copies(pos_ref, chunks, w_ref, sems, True)
    for copy in copies:
        copy.start()
    hidden = tok_ref[...].astype(f32)
    factor = lax.rsqrt(jnp.mean(hidden * hidden, axis=-1, keepdims=True) + epsilon)
    normed_ref[...] = (hidden * factor * gain_ref[...]).astype(bf16)
    for copy in copies:
        copy.wait()
    tokens, width = proj_ref.shape
    for start in range(0, width, 512):
        end = min(start + 512, width)
        proj_ref[:, start:end] = jnp.dot(
            normed_ref[...], w_ref[:, start:end], preferred_element_type=f32
        )
    decay_prep(proj_ref, heads_ref, inner, head_dim, stepe_ref, cume_ref, cumt_ref)

    def convolve(at, _):
        signal, mixed = conv_block(proj_ref, masks_ref, cw_ref, cb_ref, inner, at)
        act_ref[:, pl.ds(pl.multiple_of(at * LANES, LANES), LANES)] = silu_parts(mixed)[1]
        return 0

    lax.fori_loop(0, act_ref.shape[1] // LANES, convolve, 0)
    seqs = tokens // LANES
    for seq in range(seqs):
        rows = slice(seq * LANES, (seq + 1) * LANES)
        keys = act_ref[rows, inner : inner + LANES]
        queries = act_ref[rows, inner + LANES :]
        score_ref[rows, :] = exact_dot(queries, keys, ((1,), (1,)))
    sq_ref[...] = jnp.zeros_like(sq_ref)

    def scan(pair, _):
        lanes = pl.ds(pl.multiple_of(pair * LANES, LANES), LANES)
        skip = skip_ref[:, lanes]
        for seq in range(seqs):
            rows = slice(seq * LANES, (seq + 1) * LANES)
            fade_a, fade_b = pair_weights(cume_ref, cumt_ref, vis_ref, rows, lanes, pair, head_dim)
            score = score_ref[rows, :]
            weights = jnp.concatenate([fade_a * score, fade_b * score], axis=1)
            values = act_ref[rows, lanes]
            scaled = split_heads(values * stepe_ref[rows, lanes], head_dim)
            mixed = low_dot(weights, scaled) + skip * values
            mixer_ref[rows, lanes] = mixed
            product = mixed * silu_parts(proj_ref[rows, lanes])[1]
            sq_ref[rows, :] += product * product
        return 0

    lax.fori_loop(0, inner // LANES, scan, 0)
    total = jnp.sum(sq_ref[...], axis=1, keepdims=True)
    sq_ref[...] = jnp.broadcast_to(total, sq_ref.shape)


def gated_kernel(
    chunk_count, inner, full_inner,
    pos_ref, proj_ref, mixer_ref, sq_ref, gain_ref, cot_ref, *rest,
):
    gated_ref = rest[0]
    chunks = rest[1 : 1 + chunk_count]
    grad_ref, sems = rest[1 + chunk_count :]
    factor = lax.rsqrt(sq_ref[...][:, 0:1] / full_inner + epsilon)
    for start in range(0, inner, LANES):
        lanes = slice(start, start + LANES)
        product = mixer_ref[:, lanes] * silu_parts(proj_ref[:, lanes])[1]
        gated_ref[:, lanes] = (product * factor * gain_ref[:, lanes]).astype(bf16)
    for start in range(0, inner, 256):
        lanes = slice(start, start + 256)
        grad_ref[lanes, :] = low_dot(gated_ref[:, lanes], cot_ref[...], ((0,), (0,))).astype(bf16)
    copies = chunk_copies(pos_ref, chunks, grad_ref, sems, False)
    for copy in copies:
        copy.start()
    for copy in copies:
        copy.wait()


def out_kernel(
    chunk_count, inner,
    pos_ref, proj_ref, mixer_ref, gain_ref, cot_ref, gated_ref, *rest,
):
    chunks = rest[:chunk_count]
    dgated_ref, cross_ref, block_ref, w_ref, sems = rest[chunk_count:]
    copies = chunk_copies(pos_ref, chunks, w_ref, sems, True)
    for copy in copies:
        copy.start()
    for copy in copies:
        copy.wait()
    cross = jnp.zeros(cross_ref.shape, f32)
    for start in range(0, inner, 256):
        lanes = slice(start, start + 256)
        dgated_ref[:, lanes] = low_dot(cot_ref[...], w_ref[lanes, :], ((1,), (1,)))
    for start in range(0, inner, LANES):
        lanes = slice(start, start + LANES)
        product = mixer_ref[:, lanes] * silu_parts(proj_ref[:, lanes])[1]
        cross = cross + product * gain_ref[:, lanes] * dgated_ref[:, lanes]
    cross_ref[...] = jnp.broadcast_to(jnp.sum(cross, axis=1, keepdims=True), cross.shape)
    block_ref[...] = jnp.dot(gated_ref[...], w_ref[...], preferred_element_type=f32)


def backward_kernel(
    chunk_count, inner, head_dim, full_inner,
    pos_ref, normed_ref, proj_ref, mixer_ref, dgated_ref, sq_ref, cross_ref, gain_ref,
    masks_ref, vis_ref, cw_ref, cb_ref, heads_ref, skip_ref, *rest,
):
    dproj_ref, small_ref = rest[:2]
    chunks = rest[2 : 2 + chunk_count]
    (act_ref, stepe_ref, cume_ref, cumt_ref, score_ref, dscore_ref, dact_ref, dstep_ref,
     rowsum_ref, colsum_ref, turned_ref, dskip_ref, grad_ref, sems) = rest[2 + chunk_count :]
    tokens, width = proj_ref.shape
    seqs = tokens // LANES
    raw, step, decay = decay_prep(
        proj_ref, heads_ref, inner, head_dim, stepe_ref, cume_ref, cumt_ref
    )
    small_ref[...] = jnp.zeros_like(small_ref)

    def convolve(at, _):
        signal, mixed = conv_block(proj_ref, masks_ref, cw_ref, cb_ref, inner, at)
        act_ref[:, pl.ds(pl.multiple_of(at * LANES, LANES), LANES)] = silu_parts(mixed)[1]
        return 0

    lax.fori_loop(0, act_ref.shape[1] // LANES, convolve, 0)
    for seq in range(seqs):
        rows = slice(seq * LANES, (seq + 1) * LANES)
        keys = act_ref[rows, inner : inner + LANES]
        queries = act_ref[rows, inner + LANES :]
        score_ref[rows, :] = exact_dot(queries, keys, ((1,), (1,)))
    dscore_ref[...] = jnp.zeros_like(dscore_ref)
    dstep_ref[...] = jnp.zeros_like(dstep_ref)
    rowsum_ref[...] = jnp.zeros_like(rowsum_ref)
    turned_ref[...] = jnp.zeros_like(turned_ref)
    dskip_ref[...] = jnp.zeros_like(dskip_ref)
    factor = lax.rsqrt(sq_ref[...] / full_inner + epsilon)
    pull = factor * factor * factor * cross_ref[...] / full_inner

    def scan(pair, _):
        lanes = pl.ds(pl.multiple_of(pair * LANES, LANES), LANES)
        skip = skip_ref[:, lanes]
        gain = gain_ref[:, lanes]
        collect = (
            iota((LANES, LANES), 0) // head_dim + 2 * pair == iota((LANES, LANES), 1)
        ).astype(f32)
        dgain = jnp.zeros((1, LANES), f32)
        dskip = jnp.zeros((1, LANES), f32)
        for seq in range(seqs):
            rows = slice(seq * LANES, (seq + 1) * LANES)
            gate = proj_ref[rows, lanes]
            sig, gate_act = silu_parts(gate)
            mixed = mixer_ref[rows, lanes]
            product = mixed * gate_act
            dgated = dgated_ref[rows, lanes]
            dproduct = factor[rows] * gain * dgated - product * pull[rows]
            dgain = dgain + jnp.sum(dgated * product * factor[rows], axis=0, keepdims=True)
            dgate = dproduct * mixed * (sig * (1.0 + gate * (1.0 - sig)))
            dproj_ref[rows, lanes] = dgate.astype(bf16)
            dmixed = dproduct * gate_act
            values = act_ref[rows, lanes]
            stepe = stepe_ref[rows, lanes]
            dskip = dskip + jnp.sum(dmixed * values, axis=0, keepdims=True)
            fade_a, fade_b = pair_weights(cume_ref, cumt_ref, vis_ref, rows, lanes, pair, head_dim)
            score = score_ref[rows, :]
            weights_a, weights_b = fade_a * score, fade_b * score
            dsplit = split_heads(dmixed, head_dim)
            dweights = low_dot(dsplit, values * stepe, ((1,), (1,)))
            dweights_a, dweights_b = dweights[:LANES], dweights[LANES:]
            dscore_ref[rows, :] += dweights_a * fade_a + dweights_b * fade_b
            spread_a, spread_b = dweights_a * weights_a, dweights_b * weights_b
            lane = iota((LANES, LANES), 1)
            rowsum_ref[rows, :] += jnp.where(
                lane == 2 * pair,
                jnp.sum(spread_a, axis=1, keepdims=True),
                jnp.where(lane == 2 * pair + 1, jnp.sum(spread_b, axis=1, keepdims=True), 0.0),
            )
            colsum_ref[pair, 0:1, rows] = jnp.sum(spread_a, axis=0, keepdims=True)
            colsum_ref[pair, 1:2, rows] = jnp.sum(spread_b, axis=0, keepdims=True)
            weights = jnp.concatenate([weights_a, weights_b], axis=0)
            dscaled = low_dot(weights, dsplit, ((0,), (0,)))
            dact_ref[rows, lanes] = dscaled * stepe + skip * dmixed
            dstep_ref[rows, :] += exact_dot(dscaled * values, collect)
        small_ref[5:6, lanes] = dgain
        dskip_ref[0:1, lanes] = dskip
        return 0

    lax.fori_loop(0, inner // LANES, scan, 0)
    for pair in range(inner // LANES):
        turned_ref[2 * pair : 2 * pair + 2, :] = colsum_ref[pair, 0:2, :]
    upper = (iota((LANES, LANES), 0) <= iota((LANES, LANES), 1)).astype(f32)
    rate = jnp.exp(heads_ref[1:2, :])
    ddt = jnp.zeros((1, LANES), f32)
    dalog = jnp.zeros((1, LANES), f32)
    for seq in range(seqs):
        rows = slice(seq * LANES, (seq + 1) * LANES)
        keys = act_ref[rows, inner : inner + LANES]
        queries = act_ref[rows, inner + LANES :]
        dscore = dscore_ref[rows, :]
        dact_ref[rows, inner : inner + LANES] = exact_dot(dscore, queries, ((0,), (0,)))
        dact_ref[rows, inner + LANES :] = exact_dot(dscore, keys)
        dcumul = rowsum_ref[rows, :] - turned_ref[:, rows].T
        ddecay = exact_dot(upper, dcumul)
        dalog = dalog + jnp.sum(ddecay * decay[rows], axis=0, keepdims=True)
        dstep = dstep_ref[rows, :] - ddecay * rate
        draw = dstep / (1.0 + jnp.exp(-raw[rows]))
        ddt = ddt + jnp.sum(draw, axis=0, keepdims=True)
        dproj_ref[rows, width - LANES :] = draw.astype(bf16)
    gather = (
        iota((inner, LANES), 0) // head_dim == iota((inner, LANES), 1)
    ).astype(f32)
    dskip_heads = exact_dot(dskip_ref[...], gather)
    small_ref[6:7, 0:LANES] = ddt
    small_ref[6:7, LANES : 2 * LANES] = dalog
    small_ref[6:7, 2 * LANES : 3 * LANES] = dskip_heads[0:1]

    def convolve_back(at, _):
        lanes = pl.ds(pl.multiple_of(at * LANES, LANES), LANES)
        signal, mixed = conv_block(proj_ref, masks_ref, cw_ref, cb_ref, inner, at)
        sig, _unused = silu_parts(mixed)
        dmixed = dact_ref[:, lanes] * (sig * (1.0 + mixed * (1.0 - sig)))
        taps = cw_ref.shape[0]
        small_ref[taps : taps + 1, lanes] = jnp.sum(dmixed, axis=0, keepdims=True)
        small_ref[taps - 1 : taps, lanes] = jnp.sum(dmixed * signal, axis=0, keepdims=True)
        dsignal = cw_ref[taps - 1 : taps, lanes] * dmixed
        for offset in range(1, taps):
            masked = dmixed * masks_ref[offset - 1]
            place = taps - 1 - offset
            small_ref[place : place + 1, lanes] = jnp.sum(
                masked * pltpu.roll(signal, offset, 0), axis=0, keepdims=True
            )
            dsignal = dsignal + cw_ref[place : place + 1, lanes] * pltpu.roll(
                masked, tokens - offset, 0
            )
        dproj_ref[:, pl.ds(pl.multiple_of(inner + at * LANES, LANES), LANES)] = dsignal.astype(bf16)
        return 0

    lax.fori_loop(0, act_ref.shape[1] // LANES, convolve_back, 0)
    for start in range(0, width, 512):
        lanes = slice(start, min(start + 512, width))
        grad_ref[:, lanes] = low_dot(normed_ref[...], dproj_ref[:, lanes], ((0,), (0,))).astype(bf16)
    copies = chunk_copies(pos_ref, chunks, grad_ref, sems, False)
    for copy in copies:
        copy.start()
    for copy in copies:
        copy.wait()


def dnormed_kernel(chunk_count, pos_ref, dproj_ref, *rest):
    chunks = rest[:chunk_count]
    dnormed_ref, w_ref, sems = rest[chunk_count:]
    copies = chunk_copies(pos_ref, chunks, w_ref, sems, True)
    for copy in copies:
        copy.start()
    for copy in copies:
        copy.wait()
    for start in range(0, w_ref.shape[0], 256):
        lanes = slice(start, start + 256)
        dnormed_ref[:, lanes] = low_dot(dproj_ref[...], w_ref[lanes, :], ((1,), (1,)))


def tail_kernel(tok_ref, cot_ref, gain_ref, mine_ref, other_ref, dtok_ref, dgain_ref):
    hidden = tok_ref[...].astype(f32)
    factor = lax.rsqrt(jnp.mean(hidden * hidden, axis=-1, keepdims=True) + epsilon)
    dnormed = mine_ref[...] + other_ref[...]
    dgain_ref[...] = jnp.broadcast_to(
        jnp.sum(dnormed * hidden * factor, axis=0, keepdims=True), dgain_ref.shape
    )
    scaled = dnormed * gain_ref[...]
    pull = jnp.mean(scaled * hidden, axis=-1, keepdims=True) * factor * factor * factor
    dtok_ref[...] = cot_ref[...].astype(f32) + scaled * factor - hidden * pull


class Links:
    first, second = (1, 2), (2, 1)

    def __init__(self, reps, chips):
        self.reps, self.chips = reps, chips
        self.paired = reps == 2 and chips == 16
        self.rep = lax.axis_index("rep")
        self.chip = lax.axis_index("fsdp")

    def exchange(self, x, masks):
        pairs = [
            (core * self.chips + chip, core * self.chips + (chip ^ masks[core]))
            for core in range(self.reps)
            for chip in range(self.chips)
        ]
        return lax.ppermute(x, BOTH, pairs)

    def sources(self):
        if not self.paired:
            return None
        one = jnp.where(self.rep == 0, self.first[0], self.first[1])
        two = jnp.where(self.rep == 0, self.second[0], self.second[1])
        places = [0 * one, one, two, 0 * one + 3]
        return jnp.stack([self.chip ^ (4 * slot) ^ place for slot in range(4) for place in places])

    def gather_rows(self, x):
        if not self.paired:
            return [lax.all_gather(x, "fsdp", axis=0, tiled=True)]
        chunks = []
        for slot in range(4):
            block = self.exchange(x, (4 * slot, 4 * slot)) if slot else x
            near = self.exchange(block, self.first)
            side = self.exchange(block, self.second)
            far = self.exchange(near, self.second)
            chunks += [block, near, side, far]
        return chunks

    def grad_shapes(self, rows, width):
        if not self.paired:
            return [jax.ShapeDtypeStruct((rows, width), bf16)]
        return [jax.ShapeDtypeStruct((rows // self.chips, width), bf16)] * self.chips

    def scatter_rows(self, chunks):
        if not self.paired:
            return lax.psum_scatter(chunks[0], "fsdp", scatter_dimension=0, tiled=True).astype(f32)
        total = None
        for slot in (3, 2, 1, 0):
            own, near, side, far = chunks[4 * slot : 4 * slot + 4]
            near = near.astype(f32) + self.exchange(far, self.second).astype(f32)
            own = own.astype(f32) + self.exchange(side, self.second).astype(f32)
            own = own + self.exchange(near.astype(bf16), self.first).astype(f32)
            if slot:
                own = self.exchange(own.astype(bf16), (4 * slot, 4 * slot)).astype(f32)
            total = own if total is None else total + own
        return total

    def swap(self, x):
        return lax.ppermute(x, "rep", [(0, 1), (1, 0)])

    def from_reps(self, x):
        if self.reps == 2:
            other = self.swap(x)
            return [jnp.where(self.rep == 0, x, other), jnp.where(self.rep == 0, other, x)]
        whole = lax.all_gather(x, "rep", axis=0)
        return [whole[at] for at in range(self.reps)]

    def sum_reps(self, x):
        return x + self.swap(x) if self.reps == 2 else lax.psum(x, "rep")

    def own_rows(self, x):
        rows = x.shape[0] // self.reps
        if self.reps == 2:
            mine = lax.dynamic_slice_in_dim(x, self.rep * rows, rows, 0)
            theirs = lax.dynamic_slice_in_dim(x, (1 - self.rep) * rows, rows, 0)
            return mine, self.swap(theirs)
        mine = lax.psum_scatter(x, "rep", scatter_dimension=0, tiled=True)
        return mine, jnp.zeros_like(mine)

    def sum_chips(self, x):
        if not self.paired:
            return lax.psum(x, "fsdp")
        for step in (1, 4):
            one, two, three = (self.exchange(x, (at * step, at * step)) for at in (1, 2, 3))
            x = (x + one) + (two + three)
        return x


def per_device(
    reps, chips,
    tokens, segment_ids, norm_gain, in_weight, conv_weight, conv_bias, dt_bias, a_log, skip_gain,
    gate_gain, out_weight, cotangent,
):
    links = Links(reps, chips)
    rep, chip = links.rep, links.chip
    full_inner, full_heads = gate_gain.shape[0], dt_bias.shape[0]
    conv_dim, taps = conv_bias.shape[0], conv_weight.shape[0]
    model = norm_gain.shape[0]
    state = (conv_dim - full_inner) // 2
    inner, heads = full_inner // reps, full_heads // reps
    head_dim = full_inner // full_heads
    rows_in, rows_out = in_weight.shape[0], out_weight.shape[0]
    conv_local = inner + 2 * state
    width = inner + conv_local + LANES
    own_tokens = tokens.shape[0]
    total = own_tokens * reps

    def columns(x, start, size):
        return lax.dynamic_slice_in_dim(x, start, size, x.ndim - 1)

    own_in = jnp.concatenate(
        [
            columns(in_weight, rep * inner, inner),
            columns(in_weight, full_inner + rep * inner, inner),
            in_weight[:, 2 * full_inner : full_inner + conv_dim],
            columns(in_weight, full_inner + conv_dim + rep * heads, heads),
            jnp.zeros((rows_in, LANES - heads), bf16),
        ],
        axis=1,
    )
    in_chunks = links.gather_rows(own_in)
    sources = links.sources()
    if links.paired:
        half = rows_out // 2
        away = lax.dynamic_slice_in_dim(out_weight, (1 - rep) * half, half, 0)
        kept = lax.dynamic_slice_in_dim(out_weight, rep * half, half, 0)
        moves = [(at, at + 8) for at in range(8)] + [(chips + at + 8, chips + at) for at in range(8)]
        came = lax.ppermute(away, BOTH, moves)
        holds = (rep == 0) == (chip < 8)
        own_out = jnp.where(holds, kept, came)
        in_pos = (sources * rows_in).astype(jnp.int32)
        out_pos = ((2 * (sources % 8) + sources // 8) * half).astype(jnp.int32)
        out_chunks = links.gather_rows(own_out)
    else:
        in_pos = out_pos = jnp.zeros((1,), jnp.int32)
        out_full = lax.all_gather(out_weight, "fsdp", axis=0, tiled=True)
        out_chunks = [lax.dynamic_slice_in_dim(out_full, rep * inner, inner, 0)]
    count = len(in_chunks)

    chip_tokens = jnp.concatenate(links.from_reps(tokens), axis=0)
    chip_cot = jnp.concatenate(links.from_reps(cotangent), axis=0)
    segments = jnp.concatenate(links.from_reps(segment_ids), axis=0)
    seq_count, seq_len = segments.shape
    masks = []
    for offset in range(1, taps):
        earlier = jnp.pad(segments, ((0, 0), (offset, 0)), constant_values=-1)[:, :seq_len]
        same = (earlier == segments).astype(f32).reshape(total, 1)
        masks.append(jnp.broadcast_to(same, (total, LANES)))
    masks = jnp.stack(masks)
    places = jnp.arange(seq_len)
    visible = (
        (places[:, None] >= places[None, :])[None] & (segments[:, :, None] == segments[:, None, :])
    ).astype(f32).reshape(total, seq_len)

    def local_conv(x):
        return jnp.concatenate([columns(x, rep * inner, inner), x[..., full_inner:]], axis=-1)

    conv_w, conv_b = local_conv(conv_weight), local_conv(conv_bias[None])

    def lane_row(x):
        return jnp.pad(columns(x, rep * heads, heads), (0, LANES - heads))

    head_rows = jnp.pad(jnp.stack([lane_row(dt_bias), lane_row(a_log)]), ((0, 6), (0, 0)))
    skip = jnp.repeat(columns(skip_gain, rep * heads, heads), head_dim)[None]
    gate_g = columns(gate_gain, rep * inner, inner)[None]
    norm_g = norm_gain[None]

    def arr(*shape, dtype=f32):
        return jax.ShapeDtypeStruct(shape, dtype)

    def vmem(*shape, dtype=f32):
        return pltpu.VMEM(shape, dtype)

    sems = pltpu.SemaphoreType.DMA((count,))
    normed, projected, mixed, squares = pl.pallas_call(
        functools.partial(forward_kernel, count, inner, head_dim),
        out_shape=[arr(total, model, dtype=bf16), arr(total, width), arr(total, inner), arr(total, LANES)],
        in_specs=in_smem(1) + in_vmem(8) + anywhere(count),
        out_specs=in_vmem(4),
        scratch_shapes=[
            vmem(model, width, dtype=bf16), vmem(total, conv_local), vmem(total, inner),
            vmem(total, inner), vmem(inner // LANES, 8, total), vmem(total, LANES), sems,
        ],
        compiler_params=params(),
        name="forward",
    )(in_pos, chip_tokens, norm_g, masks, visible, conv_w, conv_b, head_rows, skip, *in_chunks)
    squares = links.sum_reps(squares)
    out_shapes = links.grad_shapes(inner, model)
    gated, *out_grads = pl.pallas_call(
        functools.partial(gated_kernel, count, inner, full_inner),
        out_shape=[arr(total, inner, dtype=bf16)] + out_shapes,
        in_specs=in_smem(1) + in_vmem(5),
        out_specs=in_vmem(1) + anywhere(count),
        scratch_shapes=[vmem(inner, model, dtype=bf16), sems],
        compiler_params=params(),
        name="gated",
    )(out_pos, projected, mixed, squares, gate_g, chip_cot)
    d_gated, cross, block_part = pl.pallas_call(
        functools.partial(out_kernel, count, inner),
        out_shape=[arr(total, inner), arr(total, LANES), arr(total, model)],
        in_specs=in_smem(1) + in_vmem(5) + anywhere(count),
        out_specs=in_vmem(3),
        scratch_shapes=[vmem(inner, model, dtype=bf16), sems],
        compiler_params=params(),
        name="out",
    )(out_pos, projected, mixed, gate_g, chip_cot, gated, *out_chunks)
    cross = links.sum_reps(cross)
    in_shapes = links.grad_shapes(model, width)
    d_proj, small, *in_grads = pl.pallas_call(
        functools.partial(backward_kernel, count, inner, head_dim, full_inner),
        out_shape=[arr(total, width, dtype=bf16), arr(8, conv_local)] + in_shapes,
        in_specs=in_smem(1) + in_vmem(13),
        out_specs=in_vmem(2) + anywhere(count),
        scratch_shapes=[
            vmem(total, conv_local), vmem(total, inner), vmem(total, inner), vmem(inner // LANES, 8, total),
            vmem(total, LANES), vmem(total, LANES), vmem(total, conv_local), vmem(total, LANES),
            vmem(total, LANES), vmem(inner // LANES, 8, total), vmem(LANES, total), vmem(8, inner), vmem(model, width, dtype=bf16), sems,
        ],
        compiler_params=params(),
        name="backward",
    )(in_pos, normed, projected, mixed, d_gated, squares, cross, gate_g, masks, visible, conv_w, conv_b,
      head_rows, skip)

    out_sum = links.scatter_rows(out_grads)
    in_sum = links.scatter_rows(in_grads)
    d_normed = pl.pallas_call(
        functools.partial(dnormed_kernel, count),
        out_shape=arr(total, model),
        in_specs=in_smem(1) + in_vmem(1) + anywhere(count),
        out_specs=in_vmem(1)[0],
        scratch_shapes=[vmem(model, width, dtype=bf16), sems],
        compiler_params=params(),
        name="dnormed",
    )(in_pos, d_proj, *in_chunks)
    d_normed_a, d_normed_b = links.own_rows(d_normed)
    d_tokens, d_gain = pl.pallas_call(
        tail_kernel,
        out_shape=[arr(own_tokens, model), arr(8, model)],
        in_specs=in_vmem(5),
        out_specs=in_vmem(2),
        compiler_params=params(),
        name="tail",
    )(tokens, cotangent, norm_g, d_normed_a, d_normed_b)
    block_a, block_b = links.own_rows(block_part)
    block_out = (tokens.astype(f32) + (block_a + block_b)).astype(bf16)

    small = links.sum_chips(small)
    d_norm_gain = links.sum_chips(links.sum_reps(d_gain))[0]
    smalls = links.from_reps(small)

    def join(start, end, row=slice(None)):
        return jnp.concatenate([part[row, start:end] for part in smalls], axis=1)

    shared = sum(part[:, inner:] for part in smalls[1:]) + smalls[0][:, inner:]
    d_conv = jnp.concatenate([join(0, inner), shared], axis=1)
    d_conv_weight, d_conv_bias = d_conv[:taps], d_conv[taps]
    d_gate_gain = join(0, inner)[5]
    d_dt_bias = join(0, heads)[6]
    d_a_log = join(LANES, LANES + heads)[6]
    d_skip_gain = join(2 * LANES, 2 * LANES + heads)[6]

    in_parts = links.from_reps(in_sum)
    mid = inner + inner
    d_in_weight = jnp.concatenate(
        [part[:, :inner] for part in in_parts]
        + [part[:, inner:mid] for part in in_parts]
        + [sum(part[:, mid : mid + 2 * state] for part in in_parts[1:]) + in_parts[0][:, mid : mid + 2 * state]]
        + [part[:, mid + 2 * state : mid + 2 * state + heads] for part in in_parts],
        axis=1,
    )
    if links.paired:
        back = lax.ppermute(out_sum, BOTH, [(target, source) for source, target in moves])
        halves = jnp.where(rep == 0, jnp.concatenate([out_sum, back]), jnp.concatenate([back, out_sum]))
        other = links.swap(halves)
        d_out_weight = jnp.where(holds, halves, other)
    else:
        held = lax.all_gather(out_sum, "fsdp", axis=0, tiled=True)
        whole = lax.all_gather(held, "rep", axis=0, tiled=True)
        d_out_weight = lax.dynamic_slice_in_dim(whole, chip * rows_out, rows_out, 0)
    return (
        block_out, d_tokens, d_norm_gain, d_in_weight, d_conv_weight, d_conv_bias, d_dt_bias, d_a_log,
        d_skip_gain, d_gate_gain, d_out_weight,
    )


def solution(mesh):
    rows = P(("rep", "fsdp"), None)
    in_specs = (
        rows, rows, P(), P("fsdp", None), P(), P(), P(), P(), P(), P(), P("fsdp", None), rows,
    )
    out_specs = (
        rows, rows, P(), P("fsdp", None), P(), P(), P(), P(), P(), P(), P("fsdp", None),
    )
    reps, chips = mesh.shape["rep"], mesh.shape["fsdp"]
    return jax.shard_map(
        functools.partial(per_device, reps, chips),
        mesh=mesh, in_specs=in_specs, out_specs=out_specs, check_vma=False,
    )
```

```python
import functools

import jax
import jax.numpy as jnp
from jax import lax
from jax.experimental import pallas as pl
from jax.experimental.pallas import tpu as pltpu
from jax.sharding import PartitionSpec as P

epsilon = 1e-05
highest = lax.Precision.HIGHEST
f32 = jnp.float32
bf16 = jnp.bfloat16
LANES = 128
MIB = 1024 * 1024
BOTH = ("rep", "fsdp")


def exact_dot(a, b, dims=((1,), (0,))):
    return lax.dot_general(a, b, (dims, ((), ())), precision=highest, preferred_element_type=f32)


def low_dot(a, b, dims=((1,), (0,))):
    return lax.dot_general(
        a.astype(bf16), b.astype(bf16), (dims, ((), ())), preferred_element_type=f32
    )


def iota(shape, dim):
    return lax.broadcasted_iota(jnp.int32, shape, dim)


def cost(microseconds):
    return pl.CostEstimate(flops=0, transcendentals=0, bytes_accessed=microseconds * 3500000)


def params():
    return pltpu.CompilerParams(vmem_limit_bytes=56 * MIB)


def in_vmem(n):
    return [pl.BlockSpec(memory_space=pltpu.VMEM)] * n


def in_smem(n):
    return [pl.BlockSpec(memory_space=pltpu.SMEM)] * n


def in_hbm(n):
    return [pl.BlockSpec(memory_space=pltpu.HBM)] * n


def source_chip(rank_ref, slot, place):
    first = jnp.where(rank_ref[1] == 0, 1, 2)
    step = (0, first, 3 - first, 3)[place]
    return rank_ref[2] ^ (4 * slot) ^ step


def in_rows(rank_ref, slot, place, rows):
    return pl.ds(pl.multiple_of(source_chip(rank_ref, slot, place) * rows, 16), rows)


def out_rows(rank_ref, slot, place, rows):
    chip = source_chip(rank_ref, slot, place)
    return pl.ds(pl.multiple_of((4 * (chip // 8) + chip % 4) * rows, 16), rows)


def in_copies(rank_ref, chunks, whole, sems):
    copies = []
    for at, chunk in enumerate(chunks):
        part = chunk.at[:, pl.ds(0, whole.shape[1])]
        if len(chunks) > 1:
            target = whole.at[in_rows(rank_ref, at // 4, at % 4, chunk.shape[0])]
        else:
            target = whole
        copies.append(pltpu.make_async_copy(part, target, sems.at[at]))
    return copies


def out_copies(rank_ref, chunks, whole, sems):
    copies = []
    width = whole.shape[1]
    for at, chunk in enumerate(chunks):
        part = chunk.at[:, pl.ds(chunk.shape[1] - width, width)]
        if len(chunks) > 1:
            target = whole.at[out_rows(rank_ref, at // 4 * 2, at % 4, chunk.shape[0])]
        else:
            target = whole
        copies.append(pltpu.make_async_copy(part, target, sems.at[at]))
    return copies


def in_grad_copies(rank_ref, chunks, whole, sems):
    if len(chunks) == 1:
        return [pltpu.make_async_copy(whole, chunks[0], sems.at[0])]
    copies = []
    width = whole.shape[1]
    rows = chunks[0].shape[0]
    for group, first_slot in enumerate((2, 0)):
        for side in range(2):
            for place in range(4):
                chunk = chunks[3 * group + min(place, 2)]
                held = chunk.at[pl.ds(rows * (place == 3), rows), pl.ds(side * width, width)]
                part = whole.at[in_rows(rank_ref, first_slot + side, place, rows)]
                copies.append(pltpu.make_async_copy(part, held, sems.at[len(copies)]))
    return copies


def out_grad_copies(rank_ref, chunks, whole, sems):
    if len(chunks) == 1:
        return [pltpu.make_async_copy(whole, chunks[0], sems.at[0])]
    copies = []
    rows = chunks[0].shape[0] // 2
    for place, chunk in enumerate(chunks):
        for at in range(2):
            part = whole.at[out_rows(rank_ref, 2 * at, place, rows)]
            copies.append(pltpu.make_async_copy(part, chunk.at[pl.ds(at * rows, rows)], sems.at[len(copies)]))
    return copies


def started(source, target, sem):
    copy = pltpu.make_async_copy(source, target, sem)
    copy.start()
    return copy


def token_copies(places, refs, target, start, rows, sems, first=0):
    width = target.shape[1]
    return [
        started(
            refs[ref].at[pl.ds(row + start, rows), pl.ds(0, width)],
            target.at[pl.ds(at * rows, rows)],
            sems.at[first + at],
        )
        for at, (ref, row) in enumerate(places)
    ]


def spread_marks(seg_ref, masks_ref, vis_ref):
    row, col = iota((LANES, LANES), 0), iota((LANES, LANES), 1)
    for seq in range(seg_ref.shape[0] // 16):
        rows = slice(seq * LANES, (seq + 1) * LANES)
        across = jnp.broadcast_to(seg_ref[16 * seq : 16 * seq + 1, :].astype(f32), (LANES, LANES))
        down = across.T
        vis_ref[rows, :] = ((across == down) & (row >= col)).astype(f32)
        for offset in range(1, masks_ref.shape[0] + 1):
            same = (pltpu.roll(down, offset, 0) == down) & (row >= offset)
            masks_ref[offset - 1, rows, :] = same.astype(f32)


def halves(core, even, odd):
    lane = iota(even.shape, 1)
    low = jnp.where(lane < LANES // 2, even, pltpu.roll(odd, LANES // 2, 1))
    high = jnp.where(lane < LANES // 2, pltpu.roll(even, LANES // 2, 1), odd)
    return jnp.where(core == 0, low, high)


def head_blocks(inner, group, at, side):
    start = 4 * inner * group + LANES * (8 * (at // 2) + 2 * (at % 2))
    first = pl.multiple_of(start + 4 * LANES * side, LANES)
    return pl.ds(first, LANES), pl.ds(pl.multiple_of(first + LANES, LANES), LANES)


def head_number(local, side, core):
    return 16 * (local // 4) + 8 * side + 2 * (local % 4) + core


def pack_kernel(inner, state, heads, rank_ref, in_ref, out_ref, keep_ref, give_ref):
    side, core = rank_ref[0], rank_ref[1]
    shared = 2 * state
    for target, of_side in ((keep_ref, side), (give_ref, 1 - side)):
        for group in range(2):
            for at in range(inner // LANES):
                even, odd = head_blocks(inner, group, at, of_side)
                lanes = slice(inner * group + LANES * at, inner * group + LANES * (at + 1))
                target[:, lanes] = halves(
                    core, in_ref[:, even].astype(f32), in_ref[:, odd].astype(f32)
                ).astype(bf16)
        target[:, 2 * inner : 2 * inner + shared] = in_ref[:, 8 * inner : 8 * inner + shared]
        shape = (4 * heads, LANES)
        local = iota(shape, 1)
        pick = (local < heads) & (iota(shape, 0) == head_number(local, of_side, core))
        steps = low_dot(in_ref[:, 8 * inner + shared :], pick.astype(f32))
        target[:, 2 * inner + shared : 2 * inner + shared + LANES] = steps.astype(bf16)
    rows = keep_ref.shape[0]
    lower, upper = out_ref[:rows].astype(f32), out_ref[rows:].astype(f32)
    keep_ref[:, 2 * inner + shared + LANES :] = jnp.where(core == 0, lower, upper).astype(bf16)


def prepare_kernel(
    inner, state, heads, head_dim,
    rank_ref, cw_in, cb_in, gate_in, norm_in, dt_in, alog_in, skip_in,
    cw_ref, cb_ref, gate_ref, norm_ref, heads_ref, skip_ref,
):
    side, core = rank_ref[0], rank_ref[1]

    def chosen(get):
        low, high = (halves(core, get(4 * of_side), get(4 * of_side + 1)) for of_side in range(2))
        return jnp.where(side == 0, low, high)

    for at in range(inner // LANES):
        first = 8 * (at // 2) + 2 * (at % 2)
        lanes = slice(LANES * at, LANES * (at + 1))
        cw_ref[:, lanes] = chosen(lambda b: cw_in[:, LANES * (first + b) : LANES * (first + b + 1)])
        cb_ref[:, lanes] = chosen(lambda b: cb_in[first + b : first + b + 1, :])
        gate_ref[:, lanes] = chosen(lambda b: gate_in[first + b : first + b + 1, :])
    cw_ref[:, inner:] = cw_in[:, 4 * inner :]
    for at in range(2 * state // LANES):
        row = 4 * inner // LANES + at
        cb_ref[:, inner + LANES * at : inner + LANES * (at + 1)] = cb_in[row : row + 1, :]
    for row in range(norm_in.shape[0]):
        norm_ref[:, LANES * row : LANES * (row + 1)] = norm_in[row : row + 1, :]
    shape = (4 * heads, LANES)
    local = iota(shape, 1)
    pick = ((local < heads) & (iota(shape, 0) == head_number(local, side, core))).astype(f32)
    rows = jnp.concatenate([dt_in[...], alog_in[...], skip_in[...], jnp.zeros((5, 4 * heads), f32)], axis=0)
    own = exact_dot(rows, pick)
    heads_ref[...] = own
    spread = (iota((LANES, inner), 1) // head_dim == iota((LANES, inner), 0)).astype(f32)
    skip_ref[...] = exact_dot(own, spread)[2:3]


def unpack_kernel(
    inner, state, heads, model, taps,
    rank_ref, mine_ref, other_ref, small_mine_ref, small_other_ref,
    in_ref, out_ref, conv_ref, bias_ref, gate_ref, gain_ref, *head_refs,
):
    side, core = rank_ref[0], rank_ref[1]
    width = 2 * inner + 2 * state + LANES
    shared = 2 * state

    def both(start, end):
        mine, other = mine_ref[:, start:end], other_ref[:, start:end]
        return jnp.where(core == 0, mine, other), jnp.where(core == 0, other, mine)

    tails = [None, None]
    for offset, of_side in ((0, side), (width + model, 1 - side)):
        for group in range(2):
            for at in range(inner // LANES):
                start = offset + inner * group + LANES * at
                first, second = both(start, start + LANES)
                even, odd = head_blocks(inner, group, at, of_side)
                in_ref[:, even] = halves(0, first, second)
                in_ref[:, odd] = halves(1, first, second)
        start = offset + 2 * inner
        first, second = both(start, start + shared)
        keys = first + second
        start += shared
        first, second = both(start, start + LANES)
        row, col = iota((LANES, LANES), 0), iota((LANES, LANES), 1)
        steps = exact_dot(
            first, ((row < heads) & (col == head_number(row, of_side, 0))).astype(f32)
        ) + exact_dot(second, ((row < heads) & (col == head_number(row, of_side, 1))).astype(f32))
        tails[0 if offset == 0 else 1] = (keys, steps)
    in_ref[:, 8 * inner : 8 * inner + shared] = tails[0][0] + tails[1][0]
    in_ref[:, 8 * inner + shared :] = (tails[0][1] + tails[1][1])[:, : 4 * heads]
    rows = mine_ref.shape[0]
    first, second = both(width, width + model)
    out_ref[:rows, :] = first
    out_ref[rows:, :] = second

    def small_both(start, end):
        mine, other = small_mine_ref[:, start:end], small_other_ref[:, start:end]
        return jnp.where(core == 0, mine, other), jnp.where(core == 0, other, mine)

    row, col = iota((LANES, LANES), 0), iota((LANES, LANES), 1)
    small_width = small_mine_ref.shape[1] // 2
    for of_side in range(2):
        offset = small_width * jnp.where(side == of_side, 0, 1)
        for at in range(inner // LANES):
            lanes = pl.ds(pl.multiple_of(offset + LANES * at, LANES), LANES)
            mine, other = small_mine_ref[:, lanes], small_other_ref[:, lanes]
            first, second = jnp.where(core == 0, mine, other), jnp.where(core == 0, other, mine)
            place = 8 * (at // 2) + 4 * of_side + 2 * (at % 2)
            for step in range(2):
                block = halves(step, first, second)
                conv_ref[:, LANES * (place + step) : LANES * (place + step + 1)] = block[:taps]
                bias_ref[place + step : place + step + 1, :] = block[taps : taps + 1]
                gate_ref[place + step : place + step + 1, :] = block[taps + 1 : taps + 2]
    shared_blocks = []
    for at in range(inner // LANES, small_width // LANES):
        sides = []
        for of_side in range(2):
            start = small_width * of_side + LANES * at
            first, second = small_both(start, start + LANES)
            sides.append(first + second)
        shared_blocks.append(sides[0] + sides[1])
    for at, block in enumerate(shared_blocks[: shared // LANES]):
        place = 4 * inner // LANES + at
        conv_ref[:, LANES * place : LANES * (place + 1)] = block[:taps]
        bias_ref[place : place + 1, :] = block[taps : taps + 1]
    gain_ref[...] = shared_blocks[shared // LANES]
    scatter_sides = (side, 1 - side)
    for kind in range(3):
        total = jnp.zeros((8, LANES), f32)
        for at, of_side in enumerate(scatter_sides):
            start = small_width * at + LANES * kind
            first, second = small_both(start, start + LANES)
            for of_core, part in enumerate((first, second)):
                pick = (row < heads) & (col == head_number(row, of_side, of_core))
                total = total + exact_dot(part, pick.astype(f32))
        head_refs[kind][...] = total[taps + 2 : taps + 3, : 4 * heads]


def silu_parts(v):
    sig = 1.0 / (1.0 + jnp.exp(-v))
    return sig, v * sig


def conv_block(proj_ref, masks_ref, cw_ref, cb_ref, inner, at):
    signal = proj_ref[:, pl.ds(pl.multiple_of(inner + at * LANES, LANES), LANES)]
    lanes = pl.ds(pl.multiple_of(at * LANES, LANES), LANES)
    taps = cw_ref.shape[0]
    mixed = cb_ref[:, lanes] + cw_ref[taps - 1 : taps, lanes] * signal
    for offset in range(1, taps):
        earlier = pltpu.roll(signal, offset, 0) * masks_ref[offset - 1]
        mixed = mixed + cw_ref[taps - 1 - offset : taps - offset, lanes] * earlier
    return signal, mixed


def decay_prep(proj_ref, heads_ref, inner, head_dim, stepe_ref, cume_ref, cumt_ref):
    tokens, width = proj_ref.shape
    raw = proj_ref[:, width - LANES :] + heads_ref[0:1, :]
    step = jnp.maximum(raw, 0.0) + jnp.log1p(jnp.exp(-jnp.abs(raw)))
    decay = -step * jnp.exp(heads_ref[1:2, :])
    lower = (iota((LANES, LANES), 0) >= iota((LANES, LANES), 1)).astype(f32)
    spread = (
        iota((LANES, inner), 1) // head_dim == iota((LANES, inner), 0)
    ).astype(f32)
    stepe_ref[...] = exact_dot(step, spread)
    for seq in range(tokens // LANES):
        rows = slice(seq * LANES, (seq + 1) * LANES)
        cumul = exact_dot(lower, decay[rows])
        cume_ref[rows, :] = exact_dot(cumul, spread)
        turned = cumul.T
        for pair in range(inner // LANES):
            cumt_ref[pair, 0:2, rows] = turned[2 * pair : 2 * pair + 2]
    return raw, step, decay


def pair_weights(cume_ref, cumt_ref, vis_ref, rows, lanes, pair, half):
    cols = cume_ref[rows, lanes]
    seen = vis_ref[rows, :] > 0.5
    first, second = cumt_ref[pair, 0:1, rows], cumt_ref[pair, 1:2, rows]
    fade_a = jnp.exp(jnp.where(seen, cols[:, 0:1] - first, -1e30))
    fade_b = jnp.exp(jnp.where(seen, cols[:, half : half + 1] - second, -1e30))
    return fade_a, fade_b


def split_heads(block, half):
    lane = iota(block.shape, 1)
    return jnp.concatenate(
        [jnp.where(lane < half, block, 0.0), jnp.where(lane >= half, block, 0.0)], axis=0
    )


def forward_kernel(
    places, in_count, out_count, inner, head_dim,
    rank_ref, gain_ref, gate_gain_ref, cw_ref, cb_ref, heads_ref, skip_ref, *rest,
):
    token_count = 1 + max(ref for ref, _ in places)
    token_rows, rest = rest[:token_count], rest[token_count:]
    in_chunks, out_chunks = rest[:in_count], rest[in_count : in_count + out_count]
    (sums_ref, normed_out, proj_out, mixer_out, dgated_out,
     normed_ref, proj_ref, mixer_ref, dgated_ref, w_ref, w_out_ref, act_ref, stepe_ref, cume_ref,
     cumt_ref, score_ref, sq_ref, cross_ref, masks_ref, vis_ref, tok_ref, cot_ref, seg_ref,
     in_sems, out_sems, store_sems, token_sems) = (
        rest[in_count + out_count :]
    )
    count = len(places)
    tokens_in = token_copies(places, token_rows, tok_ref, 0, LANES, token_sems)
    tokens_in += token_copies(places, token_rows, seg_ref, 2 * LANES, 16, token_sems, count)
    cot_in = token_copies(places, token_rows, cot_ref, LANES, LANES, token_sems, 2 * count)
    copies = in_copies(rank_ref, in_chunks, w_ref, in_sems)
    copies += out_copies(rank_ref, out_chunks, w_out_ref, out_sems)
    for copy in copies:
        copy.start()
    for copy in tokens_in:
        copy.wait()
    hidden = tok_ref[...].astype(f32)
    factor = lax.rsqrt(jnp.mean(hidden * hidden, axis=-1, keepdims=True) + epsilon)
    normed_ref[...] = (hidden * factor * gain_ref[...]).astype(bf16)
    stores = [started(normed_ref, normed_out, store_sems.at[0])]
    spread_marks(seg_ref, masks_ref, vis_ref)
    for copy in copies + cot_in:
        copy.wait()
    tokens, width = proj_ref.shape
    for start in range(0, width, 512):
        end = min(start + 512, width)
        proj_ref[:, start:end] = jnp.dot(
            normed_ref[...], w_ref[:, start:end], preferred_element_type=f32
        )
    for start in range(0, inner, 256):
        lanes = slice(start, start + 256)
        dgated_ref[:, lanes] = low_dot(cot_ref[...], w_out_ref[lanes, :], ((1,), (1,)))
    stores.append(started(proj_ref, proj_out, store_sems.at[1]))
    stores.append(started(dgated_ref, dgated_out, store_sems.at[2]))
    decay_prep(proj_ref, heads_ref, inner, head_dim, stepe_ref, cume_ref, cumt_ref)

    def convolve(at, _):
        signal, mixed = conv_block(proj_ref, masks_ref, cw_ref, cb_ref, inner, at)
        act_ref[:, pl.ds(pl.multiple_of(at * LANES, LANES), LANES)] = silu_parts(mixed)[1]
        return 0

    lax.fori_loop(0, act_ref.shape[1] // LANES, convolve, 0)
    seqs = tokens // LANES
    for seq in range(seqs):
        rows = slice(seq * LANES, (seq + 1) * LANES)
        keys = act_ref[rows, inner : inner + LANES]
        queries = act_ref[rows, inner + LANES :]
        score_ref[rows, :] = exact_dot(queries, keys, ((1,), (1,)))
    sq_ref[...] = jnp.zeros_like(sq_ref)
    cross_ref[...] = jnp.zeros_like(cross_ref)

    def scan(pair, _):
        lanes = pl.ds(pl.multiple_of(pair * LANES, LANES), LANES)
        skip = skip_ref[:, lanes]
        for seq in range(seqs):
            rows = slice(seq * LANES, (seq + 1) * LANES)
            fade_a, fade_b = pair_weights(cume_ref, cumt_ref, vis_ref, rows, lanes, pair, head_dim)
            score = score_ref[rows, :]
            weights = jnp.concatenate([fade_a * score, fade_b * score], axis=1)
            values = act_ref[rows, lanes]
            scaled = split_heads(values * stepe_ref[rows, lanes], head_dim)
            mixed = low_dot(weights, scaled) + skip * values
            mixer_ref[rows, lanes] = mixed
            product = mixed * silu_parts(proj_ref[rows, lanes])[1]
            sq_ref[rows, :] += product * product
            cross_ref[rows, :] += product * gate_gain_ref[:, lanes] * dgated_ref[rows, lanes]
        return 0

    lax.fori_loop(0, inner // LANES, scan, 0)
    stores.append(started(mixer_ref, mixer_out, store_sems.at[3]))
    for seq in range(seqs):
        rows = slice(seq * LANES, (seq + 1) * LANES)
        sums_ref[seq : seq + 1, :] = jnp.sum(sq_ref[rows, :].T, axis=0, keepdims=True)
        at = seqs + seq
        sums_ref[at : at + 1, :] = jnp.sum(cross_ref[rows, :].T, axis=0, keepdims=True)
    for copy in stores:
        copy.wait()


def gated_kernel(
    places, chunk_count, grad_count, inner, full_inner,
    rank_ref, sums_ref, gain_ref, proj_in, mixer_in, *rest,
):
    token_count = 1 + max(ref for ref, _ in places)
    token_rows, rest = rest[:token_count], rest[token_count:]
    chunks = rest[:chunk_count]
    block_ref = rest[chunk_count]
    grads = rest[chunk_count + 1 : chunk_count + 1 + grad_count]
    (proj_ref, mixer_ref, gated_ref, factor_ref, w_out_ref, grad_ref, cot_ref, sems, grad_sems, load_sems,
     token_sems) = (
        rest[chunk_count + 1 + grad_count :]
    )
    loads = [
        started(proj_in.at[:, pl.ds(0, inner)], proj_ref, load_sems.at[0]),
        started(mixer_in, mixer_ref, load_sems.at[1]),
    ]
    loads += token_copies(places, token_rows, cot_ref, LANES, LANES, token_sems)
    weights = out_copies(rank_ref, chunks, w_out_ref, sems)
    for copy in weights:
        copy.start()
    tokens = proj_ref.shape[0]
    seqs = tokens // LANES
    for seq in range(seqs):
        row = lax.rsqrt(sums_ref[seq : seq + 1, :] / full_inner + epsilon)
        factor_ref[seq * LANES : (seq + 1) * LANES, :] = jnp.broadcast_to(row, (LANES, LANES)).T
    for copy in loads:
        copy.wait()
    for start in range(0, inner, LANES):
        lanes = slice(start, start + LANES)
        product = mixer_ref[:, lanes] * silu_parts(proj_ref[:, lanes])[1]
        gated_ref[:, lanes] = (product * factor_ref[...] * gain_ref[:, lanes]).astype(bf16)
    for start in range(0, inner, 256):
        lanes = slice(start, start + 256)
        grad_ref[lanes, :] = low_dot(gated_ref[:, lanes], cot_ref[...], ((0,), (0,))).astype(bf16)
    copies = out_grad_copies(rank_ref, grads, grad_ref, grad_sems)
    for copy in copies:
        copy.start()
    for copy in weights:
        copy.wait()
    block_ref[...] = jnp.dot(gated_ref[...], w_out_ref[...], preferred_element_type=f32)
    for copy in copies:
        copy.wait()


def backward_kernel(
    places, weight_count, chunk_count, inner, head_dim, full_inner,
    rank_ref, sums_ref, gain_ref, cw_ref, cb_ref, heads_ref, skip_ref,
    normed_in, proj_in, mixer_in, dgated_in, *rest,
):
    token_count = 1 + max(ref for ref, _ in places)
    token_rows, rest = rest[:token_count], rest[token_count:]
    weight_chunks = rest[:weight_count]
    rest = rest[weight_count:]
    dnormed_ref, small_ref = rest[:2]
    chunks = rest[2 : 2 + chunk_count]
    (normed_ref, proj_ref, mixer_ref, dgated_ref, masks_ref, vis_ref, dact_ref,
     act_ref, stepe_ref, cume_ref, cumt_ref, score_ref, dscore_ref, dstep_ref,
     rowsum_ref, colsum_ref, turned_ref, dskip_ref, factor_ref, pull_ref, turned_normed_ref, grad_ref,
     w_ref, dproj_ref, tok_ref, seg_ref, weight_sems, sems, load_sems, token_sems) = (
        rest[2 + chunk_count :]
    )
    seg_in = token_copies(places, token_rows, seg_ref, 2 * LANES, 16, token_sems)
    loads = [
        started(source, target, load_sems.at[at])
        for at, (source, target) in enumerate(
            ((proj_in, proj_ref), (mixer_in, mixer_ref), (dgated_in, dgated_ref), (normed_in, normed_ref))
        )
    ]
    weights = in_copies(rank_ref, weight_chunks, w_ref, weight_sems)
    for copy in weights:
        copy.start()
    weights += token_copies(places, token_rows, tok_ref, 0, LANES, token_sems, len(places))
    for copy in seg_in:
        copy.wait()
    spread_marks(seg_ref, masks_ref, vis_ref)
    loads[0].wait()
    tokens, width = proj_ref.shape
    seqs = tokens // LANES
    raw, step, decay = decay_prep(
        proj_ref, heads_ref, inner, head_dim, stepe_ref, cume_ref, cumt_ref
    )
    small_ref[...] = jnp.zeros_like(small_ref)

    def convolve(at, _):
        signal, mixed = conv_block(proj_ref, masks_ref, cw_ref, cb_ref, inner, at)
        act_ref[:, pl.ds(pl.multiple_of(at * LANES, LANES), LANES)] = silu_parts(mixed)[1]
        return 0

    lax.fori_loop(0, act_ref.shape[1] // LANES, convolve, 0)
    for seq in range(seqs):
        rows = slice(seq * LANES, (seq + 1) * LANES)
        keys = act_ref[rows, inner : inner + LANES]
        queries = act_ref[rows, inner + LANES :]
        score_ref[rows, :] = exact_dot(queries, keys, ((1,), (1,)))
    dscore_ref[...] = jnp.zeros_like(dscore_ref)
    dstep_ref[...] = jnp.zeros_like(dstep_ref)
    rowsum_ref[...] = jnp.zeros_like(rowsum_ref)
    turned_ref[...] = jnp.zeros_like(turned_ref)
    dskip_ref[...] = jnp.zeros_like(dskip_ref)
    for seq in range(seqs):
        rows = slice(seq * LANES, (seq + 1) * LANES)
        row = lax.rsqrt(sums_ref[seq : seq + 1, :] / full_inner + epsilon)
        pulled = row * row * row * sums_ref[seqs + seq : seqs + seq + 1, :] / full_inner
        factor_ref[rows, :] = jnp.broadcast_to(row, (LANES, LANES)).T
        pull_ref[rows, :] = jnp.broadcast_to(pulled, (LANES, LANES)).T

    def scan(pair, _):
        lanes = pl.ds(pl.multiple_of(pair * LANES, LANES), LANES)
        skip = skip_ref[:, lanes]
        gain = gain_ref[:, lanes]
        collect = (
            iota((LANES, LANES), 0) // head_dim + 2 * pair == iota((LANES, LANES), 1)
        ).astype(f32)
        dgain = jnp.zeros((1, LANES), f32)
        dskip = jnp.zeros((1, LANES), f32)
        for seq in range(seqs):
            rows = slice(seq * LANES, (seq + 1) * LANES)
            gate = proj_ref[rows, lanes]
            sig, gate_act = silu_parts(gate)
            mixed = mixer_ref[rows, lanes]
            product = mixed * gate_act
            dgated = dgated_ref[rows, lanes]
            factor = factor_ref[rows, :]
            dproduct = factor * gain * dgated - product * pull_ref[rows, :]
            dgain = dgain + jnp.sum(dgated * product * factor, axis=0, keepdims=True)
            dgate = dproduct * mixed * (sig * (1.0 + gate * (1.0 - sig)))
            dproj_ref[rows, lanes] = dgate.astype(bf16)
            dmixed = dproduct * gate_act
            values = act_ref[rows, lanes]
            stepe = stepe_ref[rows, lanes]
            dskip = dskip + jnp.sum(dmixed * values, axis=0, keepdims=True)
            fade_a, fade_b = pair_weights(cume_ref, cumt_ref, vis_ref, rows, lanes, pair, head_dim)
            score = score_ref[rows, :]
            weights_a, weights_b = fade_a * score, fade_b * score
            dsplit = split_heads(dmixed, head_dim)
            dweights = low_dot(dsplit, values * stepe, ((1,), (1,)))
            dweights_a, dweights_b = dweights[:LANES], dweights[LANES:]
            dscore_ref[rows, :] += dweights_a * fade_a + dweights_b * fade_b
            spread_a, spread_b = dweights_a * weights_a, dweights_b * weights_b
            lane = iota((LANES, LANES), 1)
            rowsum_ref[rows, :] += jnp.where(
                lane == 2 * pair,
                jnp.sum(spread_a, axis=1, keepdims=True),
                jnp.where(lane == 2 * pair + 1, jnp.sum(spread_b, axis=1, keepdims=True), 0.0),
            )
            colsum_ref[pair, 0:1, rows] = jnp.sum(spread_a, axis=0, keepdims=True)
            colsum_ref[pair, 1:2, rows] = jnp.sum(spread_b, axis=0, keepdims=True)
            weights = jnp.concatenate([weights_a, weights_b], axis=0)
            dscaled = low_dot(weights, dsplit, ((0,), (0,)))
            dact_ref[rows, lanes] = dscaled * stepe + skip * dmixed
            dstep_ref[rows, :] += exact_dot(dscaled * values, collect)
        small_ref[5:6, lanes] = dgain
        dskip_ref[0:1, lanes] = dskip
        return 0

    for copy in loads[1:]:
        copy.wait()
    lax.fori_loop(0, inner // LANES, scan, 0)
    for pair in range(inner // LANES):
        turned_ref[2 * pair : 2 * pair + 2, :] = colsum_ref[pair, 0:2, :]
    upper = (iota((LANES, LANES), 0) <= iota((LANES, LANES), 1)).astype(f32)
    rate = jnp.exp(heads_ref[1:2, :])
    ddt = jnp.zeros((1, LANES), f32)
    dalog = jnp.zeros((1, LANES), f32)
    for seq in range(seqs):
        rows = slice(seq * LANES, (seq + 1) * LANES)
        keys = act_ref[rows, inner : inner + LANES]
        queries = act_ref[rows, inner + LANES :]
        dscore = dscore_ref[rows, :]
        dact_ref[rows, inner : inner + LANES] = exact_dot(dscore, queries, ((0,), (0,)))
        dact_ref[rows, inner + LANES :] = exact_dot(dscore, keys)
        dcumul = rowsum_ref[rows, :] - turned_ref[:, rows].T
        ddecay = exact_dot(upper, dcumul)
        dalog = dalog + jnp.sum(ddecay * decay[rows], axis=0, keepdims=True)
        dstep = dstep_ref[rows, :] - ddecay * rate
        draw = dstep / (1.0 + jnp.exp(-raw[rows]))
        ddt = ddt + jnp.sum(draw, axis=0, keepdims=True)
        dproj_ref[rows, width - LANES :] = draw.astype(bf16)
    gather = (
        iota((inner, LANES), 0) // head_dim == iota((inner, LANES), 1)
    ).astype(f32)
    dskip_heads = exact_dot(dskip_ref[...], gather)
    small_ref[6:7, 0:LANES] = ddt
    small_ref[6:7, LANES : 2 * LANES] = dalog
    small_ref[6:7, 2 * LANES : 3 * LANES] = dskip_heads[0:1]

    def convolve_back(at, _):
        lanes = pl.ds(pl.multiple_of(at * LANES, LANES), LANES)
        signal, mixed = conv_block(proj_ref, masks_ref, cw_ref, cb_ref, inner, at)
        sig, _unused = silu_parts(mixed)
        dmixed = dact_ref[:, lanes] * (sig * (1.0 + mixed * (1.0 - sig)))
        taps = cw_ref.shape[0]
        small_ref[taps : taps + 1, lanes] = jnp.sum(dmixed, axis=0, keepdims=True)
        small_ref[taps - 1 : taps, lanes] = jnp.sum(dmixed * signal, axis=0, keepdims=True)
        dsignal = cw_ref[taps - 1 : taps, lanes] * dmixed
        for offset in range(1, taps):
            masked = dmixed * masks_ref[offset - 1]
            place = taps - 1 - offset
            small_ref[place : place + 1, lanes] = jnp.sum(
                masked * pltpu.roll(signal, offset, 0), axis=0, keepdims=True
            )
            dsignal = dsignal + cw_ref[place : place + 1, lanes] * pltpu.roll(
                masked, tokens - offset, 0
            )
        dproj_ref[:, pl.ds(pl.multiple_of(inner + at * LANES, LANES), LANES)] = dsignal.astype(bf16)
        return 0

    lax.fori_loop(0, dact_ref.shape[1] // LANES, convolve_back, 0)
    for seq in range(seqs):
        rows = slice(seq * LANES, (seq + 1) * LANES)
        turned_normed_ref[:, rows] = normed_ref[rows, :].astype(f32).T.astype(bf16)
    for start in range(0, width, 512):
        lanes = slice(start, min(start + 512, width))
        grad_ref[:, lanes] = low_dot(turned_normed_ref[...], dproj_ref[:, lanes]).astype(bf16)
    copies = in_grad_copies(rank_ref, chunks, grad_ref, sems)
    for copy in copies:
        copy.start()
    for copy in weights:
        copy.wait()
    model = w_ref.shape[0]
    hidden = tok_ref[...].astype(f32)
    token_factor = lax.rsqrt(jnp.mean(hidden * hidden, axis=-1, keepdims=True) + epsilon)
    conv_width = dact_ref.shape[1]
    part = model // 8
    for start in range(0, model, 256):
        lanes = slice(start, start + 256)
        dnormed = low_dot(dproj_ref[...], w_ref[lanes, :], ((1,), (1,)))
        dnormed_ref[:, lanes] = dnormed
        dgain = jnp.sum(dnormed * hidden[:, lanes] * token_factor, axis=0, keepdims=True)
        for at in range(0, 256, part):
            row = (start + at) // part
            small_ref[row : row + 1, conv_width:] = dgain[:, at : at + part]
    for copy in copies:
        copy.wait()


def tail_kernel(tok_ref, cot_ref, gain_ref, mine_ref, other_ref, dtok_ref):
    hidden = tok_ref[...].astype(f32)
    factor = lax.rsqrt(jnp.mean(hidden * hidden, axis=-1, keepdims=True) + epsilon)
    dnormed = mine_ref[...] + other_ref[...]
    scaled = dnormed * gain_ref[...]
    pull = jnp.mean(scaled * hidden, axis=-1, keepdims=True) * factor * factor * factor
    dtok_ref[...] = cot_ref[...].astype(f32) + scaled * factor - hidden * pull


def after(x, *others):
    return lax.optimization_barrier((x, *others))[0]


class Links:
    first, second = (1, 2), (2, 1)
    slots = (0, 4, 8, 12)

    def __init__(self, reps, chips, paired):
        self.reps, self.chips, self.paired = reps, chips, paired
        self.rep = lax.axis_index("rep")
        self.chip = lax.axis_index("fsdp")
        self.side = self.chip // 4 % 2

    def exchange(self, x, masks):
        if isinstance(masks, int):
            masks = (masks, masks)
        pairs = [
            (core * self.chips + chip, core * self.chips + (chip ^ masks[core]))
            for core in range(self.reps)
            for chip in range(self.chips)
        ]
        return lax.ppermute(x, BOTH, pairs)

    def swap(self, x):
        return lax.ppermute(x, "rep", [(0, 1), (1, 0)])

    def spread(self, block):
        near = self.exchange(block, self.first)
        side = self.exchange(block, self.second)
        return [block, near, side, self.exchange(near, self.second)]

    def gather(self, keep, give):
        across = self.exchange(keep, self.slots[2])
        own = self.spread(keep)
        beside = self.exchange(give, self.slots[1])
        far = self.exchange(after(give, beside), self.slots[3])
        return [own, self.spread(beside), self.spread(across), self.spread(far)]

    def square(self, own, near, send):
        rows = own.shape[0]
        came = self.exchange(send, self.second)
        near = (near.astype(f32) + came[rows:].astype(f32)).astype(bf16)
        last = self.exchange(near, self.first)
        return own.astype(f32) + came[:rows].astype(f32) + last.astype(f32), came, last

    def square_at_once(self, own, near, side, far):
        moved = [self.exchange(near, self.first), self.exchange(side, self.second), self.exchange(far, 3)]
        return sum((x.astype(f32) for x in moved), own.astype(f32)), moved

    def across(self, x):
        return self.exchange(x.astype(bf16), self.slots[2]).astype(f32)

    def beside(self, x):
        return self.exchange(x.astype(bf16), self.slots[1]).astype(f32)

    def scatter(self, chunks, far, out, after_first, meanwhile):
        width = chunks[0].shape[1] // 2
        close, _, _ = self.square(*chunks[:2], after(chunks[2], after_first, out[1]))
        other = self.beside(after(close[:, width:] + far[:, width:], *meanwhile))
        return jnp.concatenate([close[:, :width] + far[:, :width], out[0] + out[1], other], axis=1)

    def sum_chips(self, x):
        for step in (1, 2, 8):
            x = x + self.exchange(x, step)
        return jnp.concatenate([x, self.exchange(x, 4)], axis=1)

    def group_rows(self, x, others):
        other = after(self.exchange(x, self.slots[1]), *others)
        return [x, self.swap(jnp.concatenate([x, other])), other]

    def from_reps(self, x):
        whole = lax.all_gather(x, "rep", axis=0)
        return [whole[at] for at in range(self.reps)]

    def sum_group(self, x):
        if not self.paired:
            return lax.psum(x, "rep")

        def reordered(y, bit):
            return jnp.concatenate([y[at ^ bit : (at ^ bit) + 1] for at in range(y.shape[0])])

        x = x + reordered(self.exchange(x, self.slots[1]), 2)
        return x + reordered(self.swap(x), 1)

    def from_side(self, x):
        return self.exchange(x[x.shape[0] // 2 :].astype(bf16), self.slots[1])

    def own_rows(self, x, came):
        rows = x.shape[0] // 4
        came = came.astype(f32)
        return x[:rows] + came[:rows], self.swap(x[rows : 2 * rows] + came[rows:])

    def scattered(self, x):
        mine = lax.psum_scatter(x, "rep", scatter_dimension=0, tiled=True)
        return mine, jnp.zeros_like(mine)


def per_device(
    reps, chips,
    tokens, segment_ids, norm_gain, in_weight, conv_weight, conv_bias, dt_bias, a_log, skip_gain,
    gate_gain, out_weight, cotangent,
):
    full_inner, full_heads = gate_gain.shape[0], dt_bias.shape[0]
    conv_dim, taps = conv_bias.shape[0], conv_weight.shape[0]
    model = norm_gain.shape[0]
    state = (conv_dim - full_inner) // 2
    head_dim = full_inner // full_heads
    rows_in, rows_out = in_weight.shape[0], out_weight.shape[0]
    paired = (reps, chips, full_heads) == (2, 16, 32) and rows_out == 2 * rows_in == 2 * head_dim
    ranks = 4 if paired else reps
    inner, heads = full_inner // ranks, full_heads // ranks
    links = Links(reps, chips, paired)
    rep, chip = links.rep, links.chip
    conv_local = inner + 2 * state
    width = inner + conv_local + LANES
    own_tokens = tokens.shape[0]
    total = own_tokens * ranks

    def arr(*shape, dtype=f32):
        return jax.ShapeDtypeStruct(shape, dtype)

    def vmem(*shape, dtype=f32):
        return pltpu.VMEM(shape, dtype)

    def own_heads(x, size):
        lead = x.shape[:-1]
        if paired:
            split = x.reshape(lead + (2, 2, 4, 2, size))
            split = lax.dynamic_index_in_dim(split, links.side, split.ndim - 4, False)
        else:
            split = x.reshape(lead + (heads, reps, size))
        split = lax.dynamic_index_in_dim(split, rep, split.ndim - 2, False)
        return split.reshape(lead + (heads * size,))

    def all_heads(parts, size):
        lead = parts[0].shape[:-1]
        if paired:
            split = [part.reshape(lead + (2, 1, 4, 1, size)) for part in parts]
            sides = [jnp.concatenate(split[at : at + 2], axis=-2) for at in (0, 2)]
            whole = jnp.concatenate(sides, axis=-4)
        else:
            whole = jnp.concatenate([part.reshape(lead + (heads, 1, size)) for part in parts], axis=-2)
        return whole.reshape(lead + (full_heads * size,))

    rank = jnp.stack([links.side, rep, chip]).astype(jnp.int32)
    if paired:
        keep, give = pl.pallas_call(
            functools.partial(pack_kernel, inner, state, heads),
            out_shape=[arr(rows_in, width + model, dtype=bf16), arr(rows_in, width, dtype=bf16)],
            in_specs=in_smem(1) + in_vmem(2),
            out_specs=in_vmem(2),
            compiler_params=params(),
            name="pack",
        )(rank, in_weight, out_weight)
        slots = links.gather(keep, give)
        first_rows = slots[1][0]
        conv_w, conv_b, gate_g, norm_g, head_rows, skip = pl.pallas_call(
            functools.partial(prepare_kernel, inner, state, heads, head_dim),
            out_shape=[
                arr(taps, conv_local), arr(1, conv_local), arr(1, inner), arr(1, model), arr(8, LANES),
                arr(1, inner),
            ],
            in_specs=in_smem(1) + in_vmem(7),
            out_specs=in_vmem(6),
            compiler_params=params(),
            name="prepare",
        )(rank, conv_weight, conv_bias.reshape(-1, LANES), gate_gain.reshape(-1, LANES),
          norm_gain.reshape(-1, LANES), dt_bias[None], a_log[None], skip_gain[None])
        in_chunks, out_chunks = sum(slots, []), slots[0] + slots[2]
        in_shapes = [(rows_in, 2 * width), (rows_in, 2 * width), (2 * rows_in, 2 * width)] * 2
        out_shapes = [(2 * rows_in, model)] * 4
    else:
        in_full = lax.all_gather(in_weight, "fsdp", axis=0, tiled=True)
        out_full = lax.all_gather(out_weight, "fsdp", axis=0, tiled=True)
        ends = [full_inner, 2 * full_inner, full_inner + conv_dim]
        gates, signals, shared, step_cols = jnp.split(in_full, ends, axis=1)
        in_chunks = [
            jnp.concatenate(
                [own_heads(gates, head_dim), own_heads(signals, head_dim), shared, own_heads(step_cols, 1),
                 jnp.zeros((model, LANES - heads), bf16)],
                axis=1,
            )
        ]
        out_chunks = [own_heads(out_full.T, head_dim).T]
        def local_conv(x):
            return jnp.concatenate([own_heads(x[:, :full_inner], head_dim), x[:, full_inner:]], axis=1)

        conv_w, conv_b = local_conv(conv_weight), local_conv(conv_bias[None])

        def lane_row(x):
            return jnp.pad(own_heads(x, 1), (0, LANES - heads))

        head_rows = jnp.pad(jnp.stack([lane_row(dt_bias), lane_row(a_log)]), ((0, 6), (0, 0)))
        skip = jnp.repeat(own_heads(skip_gain, 1), head_dim)[None]
        gate_g = own_heads(gate_gain, head_dim)[None]
        norm_g = norm_gain[None]
        in_shapes, out_shapes = [(model, width)], [(inner, model)]
    extra = jnp.pad(segment_ids.astype(bf16), ((0, 15), (0, model - segment_ids.shape[1])))
    own_rows = jnp.concatenate([tokens, cotangent, extra])
    held = own_rows.shape[0]
    if paired:
        own_rows = after(own_rows, first_rows)
        waits = slots[0][3:] + slots[1][1:3] + slots[2][1:3] + slots[3][:1]
        token_rows = links.group_rows(own_rows, waits)
        places = ((0, 0), (1, 0), (2, 0), (1, held))
    else:
        token_rows = links.from_reps(own_rows)
        places = tuple((at, 0) for at in range(reps))
    in_shapes = [arr(*shape, dtype=bf16) for shape in in_shapes]
    out_shapes = [arr(*shape, dtype=bf16) for shape in out_shapes]
    in_count, out_count = len(in_chunks), len(out_chunks)

    w_in, w_out = vmem(model, width, dtype=bf16), vmem(inner, model, dtype=bf16)
    in_sems, out_sems = (pltpu.SemaphoreType.DMA((n,)) for n in (in_count, out_count))
    def sems(n):
        return pltpu.SemaphoreType.DMA((n,))

    kept = [vmem(total, model, dtype=bf16), vmem(total, width), vmem(total, inner), vmem(total, inner)]
    tok, segs = vmem(total, model, dtype=bf16), vmem(16 * len(places), LANES, dtype=bf16)
    conv_masks = [vmem(taps - 1, total, LANES), vmem(total, LANES)]
    sums, normed, projected, mixed, d_gated = pl.pallas_call(
        functools.partial(forward_kernel, places, in_count, out_count, inner, head_dim),
        out_shape=[
            arr(2 * total // LANES, LANES), arr(total, model, dtype=bf16), arr(total, width),
            arr(total, inner), arr(total, inner),
        ],
        in_specs=in_smem(1) + in_vmem(6) + in_hbm(len(token_rows) + in_count + out_count),
        out_specs=in_vmem(1) + in_hbm(4),
        scratch_shapes=kept + [
            w_in, w_out,
            vmem(total, conv_local), vmem(total, inner), vmem(total, inner), vmem(inner // LANES, 8, total),
            vmem(total, LANES), vmem(total, LANES), vmem(total, LANES), *conv_masks,
            tok, tok, segs, in_sems, out_sems, sems(4), sems(3 * len(places)),
        ],
        compiler_params=params(),
        cost_estimate=cost(14),
        name="forward",
    )(rank, norm_g, gate_g, conv_w, conv_b, head_rows, skip, *token_rows, *in_chunks, *out_chunks)
    sums = links.sum_group(sums)
    block_part, *out_grads = pl.pallas_call(
        functools.partial(gated_kernel, places, out_count, len(out_shapes), inner, full_inner),
        out_shape=[arr(total, model)] + out_shapes,
        in_specs=in_smem(1) + in_vmem(2) + in_hbm(2 + len(token_rows) + out_count),
        out_specs=in_vmem(1) + in_hbm(len(out_shapes)),
        scratch_shapes=[
            vmem(total, inner), vmem(total, inner), vmem(total, inner, dtype=bf16), vmem(total, LANES), w_out,
            vmem(inner, model, dtype=bf16), tok, out_sems, out_sems, sems(2), sems(len(places)),
        ],
        compiler_params=params(),
        cost_estimate=cost(6),
        name="gated",
    )(rank, sums, gate_g, projected, mixed, *token_rows, *out_chunks)
    if paired:
        out_sums, moved = links.square_at_once(*out_grads)
        sums = after(sums, out_grads[2])
        block_came = links.from_side(block_part)
    d_normed, small, *in_grads = pl.pallas_call(
        functools.partial(backward_kernel, places, in_count, len(in_shapes), inner, head_dim, full_inner),
        out_shape=[arr(total, model), arr(8, conv_local + model // 8)] + in_shapes,
        in_specs=in_smem(1) + in_vmem(6) + in_hbm(4 + len(token_rows) + in_count),
        out_specs=in_vmem(2) + in_hbm(len(in_shapes)),
        scratch_shapes=kept + conv_masks + [
            vmem(total, conv_local),
            vmem(total, conv_local), vmem(total, inner), vmem(total, inner), vmem(inner // LANES, 8, total),
            vmem(total, LANES), vmem(total, LANES), vmem(total, LANES),
            vmem(total, LANES), vmem(inner // LANES, 8, total), vmem(LANES, total), vmem(8, inner),
            vmem(total, LANES), vmem(total, LANES), vmem(model, total, dtype=bf16), w_in, w_in,
            vmem(total, width, dtype=bf16), tok, segs, in_sems, in_sems, sems(4),
            sems(2 * len(places)),
        ],
        compiler_params=params(),
        cost_estimate=cost(24),
        name="backward",
    )(rank, sums, gate_g, conv_w, conv_b, head_rows, skip, normed, projected, mixed, d_gated, *token_rows,
      *in_chunks)

    if paired:
        far, came, last = links.square(*in_grads[:2], after(in_grads[2], block_came, *moved))
        far = links.across(far)
        out_parts = out_sums[:rows_in], links.across(out_sums[rows_in:])
        small = links.sum_chips(after(small, last))
        small_other = links.swap(small)
        d_normed_parts = links.own_rows(d_normed, after(links.from_side(d_normed), last))
        block_parts = links.own_rows(block_part, block_came)
    else:
        out_sum, in_sum = (
            lax.psum_scatter(grads[0], "fsdp", scatter_dimension=0, tiled=True).astype(f32)
            for grads in (out_grads, in_grads)
        )
        smalls = links.from_reps(lax.psum(small, "fsdp"))
        d_normed_parts, block_parts = links.scattered(d_normed), links.scattered(block_part)
    d_tokens = pl.pallas_call(
        tail_kernel,
        out_shape=arr(own_tokens, model),
        in_specs=in_vmem(5),
        out_specs=in_vmem(1)[0],
        compiler_params=params(),
        cost_estimate=cost(2),
        name="tail",
    )(tokens, cotangent, norm_g, *d_normed_parts)
    block_out = (tokens.astype(f32) + (block_parts[0] + block_parts[1])).astype(bf16)

    if paired:
        grad_sum = links.scatter(
            in_grads[3:], far, out_parts, came, [d_tokens, block_out, small_other]
        )
        d_in_weight, d_out_weight, d_conv_weight, d_conv_bias, d_gate_gain, d_norm_gain, *by_head = pl.pallas_call(
            functools.partial(unpack_kernel, inner, state, heads, model, taps),
            out_shape=[
                arr(*in_weight.shape), arr(*out_weight.shape), arr(taps, conv_dim), arr(conv_dim // LANES, LANES),
                arr(full_inner // LANES, LANES), arr(8, model // 8), *[arr(1, full_heads)] * 3,
            ],
            in_specs=in_smem(1) + in_vmem(4),
            out_specs=in_vmem(9),
            compiler_params=params(),
            name="unpack",
        )(rank, grad_sum, links.swap(grad_sum), small, small_other)
        d_conv_bias, d_gate_gain, d_norm_gain = (x.reshape(-1) for x in (d_conv_bias, d_gate_gain, d_norm_gain))
        d_dt_bias, d_a_log, d_skip_gain = (x.reshape(-1) for x in by_head)
    else:
        parts = [part[:, :inner] for part in smalls]
        shared = sum(part[:, inner:] for part in smalls)
        d_norm_gain = shared[:, 2 * state :].reshape(-1)
        d_conv = jnp.concatenate([all_heads(parts, head_dim), shared[:, : 2 * state]], axis=1)
        d_conv_weight, d_conv_bias = d_conv[:taps], d_conv[taps]
        d_gate_gain = d_conv[taps + 1, :full_inner]
        d_dt_bias, d_a_log, d_skip_gain = (
            all_heads([part[taps + 2, at * LANES : at * LANES + heads] for part in parts], 1) for at in range(3)
        )
        in_parts = links.from_reps(in_sum)
        mid = 2 * inner
        end = mid + 2 * state
        d_in_weight = jnp.concatenate(
            [
                all_heads([part[:, :inner] for part in in_parts], head_dim),
                all_heads([part[:, inner:mid] for part in in_parts], head_dim),
                sum(part[:, mid:end] for part in in_parts),
                all_heads([part[:, end : end + heads] for part in in_parts], 1),
            ],
            axis=1,
        )
        held = links.from_reps(lax.all_gather(out_sum, "fsdp", axis=0, tiled=True))
        whole = all_heads([part.T for part in held], head_dim).T
        d_out_weight = lax.dynamic_slice_in_dim(whole, chip * rows_out, rows_out, 0)
    return (
        block_out, d_tokens, d_norm_gain, d_in_weight, d_conv_weight, d_conv_bias, d_dt_bias, d_a_log,
        d_skip_gain, d_gate_gain, d_out_weight,
    )


def solution(mesh):
    rows = P(("rep", "fsdp"), None)
    in_specs = (
        rows, rows, P(), P("fsdp", None), P(), P(), P(), P(), P(), P(), P("fsdp", None), rows,
    )
    out_specs = (
        rows, rows, P(), P("fsdp", None), P(), P(), P(), P(), P(), P(), P("fsdp", None),
    )
    reps, chips = mesh.shape["rep"], mesh.shape["fsdp"]
    return jax.shard_map(
        functools.partial(per_device, reps, chips),
        mesh=mesh, in_specs=in_specs, out_specs=out_specs, check_vma=False,
    )
```

```python
import functools

import jax
import jax.numpy as jnp
from jax import lax
from jax.experimental import pallas as pl
from jax.experimental.pallas import tpu as pltpu
from jax.sharding import PartitionSpec as P

epsilon = 1e-05
highest = lax.Precision.HIGHEST
f32 = jnp.float32
bf16 = jnp.bfloat16
LANES = 128
MIB = 1024 * 1024
BOTH = ("rep", "fsdp")


def exact_dot(a, b, dims=((1,), (0,))):
    return lax.dot_general(a, b, (dims, ((), ())), precision=highest, preferred_element_type=f32)


def low_dot(a, b, dims=((1,), (0,))):
    return lax.dot_general(
        a.astype(bf16), b.astype(bf16), (dims, ((), ())), preferred_element_type=f32
    )


def iota(shape, dim):
    return lax.broadcasted_iota(jnp.int32, shape, dim)


def cost(microseconds):
    return pl.CostEstimate(flops=0, transcendentals=0, bytes_accessed=microseconds * 3500000)


def params():
    return pltpu.CompilerParams(vmem_limit_bytes=56 * MIB)


def in_vmem(n):
    return [pl.BlockSpec(memory_space=pltpu.VMEM)] * n


def in_smem(n):
    return [pl.BlockSpec(memory_space=pltpu.SMEM)] * n


def in_hbm(n):
    return [pl.BlockSpec(memory_space=pltpu.HBM)] * n


def source_chip(rank_ref, slot, place):
    first = jnp.where(rank_ref[1] == 0, 1, 2)
    step = (0, first, 3 - first, 3)[place]
    return rank_ref[2] ^ (4 * slot) ^ step


def in_rows(rank_ref, slot, place, rows):
    return pl.ds(pl.multiple_of(source_chip(rank_ref, slot, place) * rows, 16), rows)


def out_rows(rank_ref, slot, place, rows):
    chip = source_chip(rank_ref, slot, place)
    return pl.ds(pl.multiple_of((4 * (chip // 8) + chip % 4) * rows, 16), rows)


def in_copies(rank_ref, chunks, whole, sems):
    copies = []
    for at, chunk in enumerate(chunks):
        part = chunk.at[:, pl.ds(0, whole.shape[1])]
        if len(chunks) > 1:
            target = whole.at[in_rows(rank_ref, at // 4, at % 4, chunk.shape[0])]
        else:
            target = whole
        copies.append(pltpu.make_async_copy(part, target, sems.at[at]))
    return copies


def out_copies(rank_ref, chunks, whole, sems):
    copies = []
    width = whole.shape[1]
    for at, chunk in enumerate(chunks):
        part = chunk.at[:, pl.ds(chunk.shape[1] - width, width)]
        if len(chunks) > 1:
            target = whole.at[out_rows(rank_ref, at // 4 * 2, at % 4, chunk.shape[0])]
        else:
            target = whole
        copies.append(pltpu.make_async_copy(part, target, sems.at[at]))
    return copies


def in_grad_copies(rank_ref, chunks, whole, sems):
    if len(chunks) == 1:
        return [pltpu.make_async_copy(whole, chunks[0], sems.at[0])]
    copies = []
    width = whole.shape[1]
    rows = chunks[0].shape[0]
    for group, first_slot in enumerate((2, 0)):
        for side in range(2):
            for place in range(4):
                chunk = chunks[3 * group + min(place, 2)]
                held = chunk.at[pl.ds(rows * (place == 3), rows), pl.ds(side * width, width)]
                part = whole.at[in_rows(rank_ref, first_slot + side, place, rows)]
                copies.append(pltpu.make_async_copy(part, held, sems.at[len(copies)]))
    return copies


def out_grad_copies(rank_ref, chunks, whole, sems):
    if len(chunks) == 1:
        return [pltpu.make_async_copy(whole, chunks[0], sems.at[0])]
    copies = []
    rows = chunks[0].shape[0] // 2
    for place, chunk in enumerate(chunks):
        for at in range(2):
            part = whole.at[out_rows(rank_ref, 2 * at, place, rows)]
            copies.append(pltpu.make_async_copy(part, chunk.at[pl.ds(at * rows, rows)], sems.at[len(copies)]))
    return copies


def started(source, target, sem):
    copy = pltpu.make_async_copy(source, target, sem)
    copy.start()
    return copy


def token_copies(places, refs, target, start, rows, sems, first=0):
    width = target.shape[1]
    return [
        started(
            refs[ref].at[pl.ds(row + start, rows), pl.ds(0, width)],
            target.at[pl.ds(at * rows, rows)],
            sems.at[first + at],
        )
        for at, (ref, row) in enumerate(places)
    ]


def spread_marks(seg_ref, masks_ref, vis_ref):
    row, col = iota((LANES, LANES), 0), iota((LANES, LANES), 1)
    for seq in range(seg_ref.shape[0] // 16):
        rows = slice(seq * LANES, (seq + 1) * LANES)
        across = jnp.broadcast_to(seg_ref[16 * seq : 16 * seq + 1, :].astype(f32), (LANES, LANES))
        down = across.T
        vis_ref[rows, :] = ((across == down) & (row >= col)).astype(f32)
        for offset in range(1, masks_ref.shape[0] + 1):
            same = (pltpu.roll(down, offset, 0) == down) & (row >= offset)
            masks_ref[offset - 1, rows, :] = same.astype(f32)


def halves(core, even, odd):
    lane = iota(even.shape, 1)
    low = jnp.where(lane < LANES // 2, even, pltpu.roll(odd, LANES // 2, 1))
    high = jnp.where(lane < LANES // 2, pltpu.roll(even, LANES // 2, 1), odd)
    return jnp.where(core == 0, low, high)


def head_blocks(inner, group, at, side):
    start = 4 * inner * group + LANES * (8 * (at // 2) + 2 * (at % 2))
    first = pl.multiple_of(start + 4 * LANES * side, LANES)
    return pl.ds(first, LANES), pl.ds(pl.multiple_of(first + LANES, LANES), LANES)


def head_number(local, side, core):
    return 16 * (local // 4) + 8 * side + 2 * (local % 4) + core


def pack_kernel(inner, state, heads, rank_ref, in_ref, out_ref, keep_ref, give_ref):
    side, core = rank_ref[0], rank_ref[1]
    shared = 2 * state
    for target, of_side in ((keep_ref, side), (give_ref, 1 - side)):
        for group in range(2):
            for at in range(inner // LANES):
                even, odd = head_blocks(inner, group, at, of_side)
                lanes = slice(inner * group + LANES * at, inner * group + LANES * (at + 1))
                target[:, lanes] = halves(
                    core, in_ref[:, even].astype(f32), in_ref[:, odd].astype(f32)
                ).astype(bf16)
        target[:, 2 * inner : 2 * inner + shared] = in_ref[:, 8 * inner : 8 * inner + shared]
        shape = (4 * heads, LANES)
        local = iota(shape, 1)
        pick = (local < heads) & (iota(shape, 0) == head_number(local, of_side, core))
        steps = low_dot(in_ref[:, 8 * inner + shared :], pick.astype(f32))
        target[:, 2 * inner + shared : 2 * inner + shared + LANES] = steps.astype(bf16)
    rows = keep_ref.shape[0]
    lower, upper = out_ref[:rows].astype(f32), out_ref[rows:].astype(f32)
    keep_ref[:, 2 * inner + shared + LANES :] = jnp.where(core == 0, lower, upper).astype(bf16)


def prepare_kernel(
    inner, state, heads, head_dim,
    rank_ref, cw_in, cb_in, gate_in, norm_in, dt_in, alog_in, skip_in,
    cw_ref, cb_ref, gate_ref, norm_ref, heads_ref, skip_ref,
):
    side, core = rank_ref[0], rank_ref[1]

    def chosen(get):
        low, high = (halves(core, get(4 * of_side), get(4 * of_side + 1)) for of_side in range(2))
        return jnp.where(side == 0, low, high)

    for at in range(inner // LANES):
        first = 8 * (at // 2) + 2 * (at % 2)
        lanes = slice(LANES * at, LANES * (at + 1))
        cw_ref[:, lanes] = chosen(lambda b: cw_in[:, LANES * (first + b) : LANES * (first + b + 1)])
        cb_ref[:, lanes] = chosen(lambda b: cb_in[first + b : first + b + 1, :])
        gate_ref[:, lanes] = chosen(lambda b: gate_in[first + b : first + b + 1, :])
    cw_ref[:, inner:] = cw_in[:, 4 * inner :]
    for at in range(2 * state // LANES):
        row = 4 * inner // LANES + at
        cb_ref[:, inner + LANES * at : inner + LANES * (at + 1)] = cb_in[row : row + 1, :]
    for row in range(norm_in.shape[0]):
        norm_ref[:, LANES * row : LANES * (row + 1)] = norm_in[row : row + 1, :]
    shape = (4 * heads, LANES)
    local = iota(shape, 1)
    pick = ((local < heads) & (iota(shape, 0) == head_number(local, side, core))).astype(f32)
    rows = jnp.concatenate([dt_in[...], alog_in[...], skip_in[...], jnp.zeros((5, 4 * heads), f32)], axis=0)
    own = exact_dot(rows, pick)
    heads_ref[...] = own
    spread = (iota((LANES, inner), 1) // head_dim == iota((LANES, inner), 0)).astype(f32)
    skip_ref[...] = exact_dot(own, spread)[2:3]


def unpack_kernel(
    inner, state, heads, model, taps,
    rank_ref, mine_ref, other_ref, small_mine_ref, small_other_ref,
    in_ref, out_ref, conv_ref, bias_ref, gate_ref, gain_ref, *head_refs,
):
    side, core = rank_ref[0], rank_ref[1]
    width = 2 * inner + 2 * state + LANES
    shared = 2 * state

    def both(start, end):
        mine, other = mine_ref[:, start:end], other_ref[:, start:end]
        return jnp.where(core == 0, mine, other), jnp.where(core == 0, other, mine)

    tails = [None, None]
    for offset, of_side in ((0, side), (width + model, 1 - side)):
        for group in range(2):
            for at in range(inner // LANES):
                start = offset + inner * group + LANES * at
                first, second = both(start, start + LANES)
                even, odd = head_blocks(inner, group, at, of_side)
                in_ref[:, even] = halves(0, first, second)
                in_ref[:, odd] = halves(1, first, second)
        start = offset + 2 * inner
        first, second = both(start, start + shared)
        keys = first + second
        start += shared
        first, second = both(start, start + LANES)
        row, col = iota((LANES, LANES), 0), iota((LANES, LANES), 1)
        steps = exact_dot(
            first, ((row < heads) & (col == head_number(row, of_side, 0))).astype(f32)
        ) + exact_dot(second, ((row < heads) & (col == head_number(row, of_side, 1))).astype(f32))
        tails[0 if offset == 0 else 1] = (keys, steps)
    in_ref[:, 8 * inner : 8 * inner + shared] = tails[0][0] + tails[1][0]
    in_ref[:, 8 * inner + shared :] = (tails[0][1] + tails[1][1])[:, : 4 * heads]
    rows = mine_ref.shape[0]
    first, second = both(width, width + model)
    out_ref[:rows, :] = first
    out_ref[rows:, :] = second

    def small_both(start, end):
        mine, other = small_mine_ref[:, start:end], small_other_ref[:, start:end]
        return jnp.where(core == 0, mine, other), jnp.where(core == 0, other, mine)

    row, col = iota((LANES, LANES), 0), iota((LANES, LANES), 1)
    small_width = small_mine_ref.shape[1] // 2
    for of_side in range(2):
        offset = small_width * jnp.where(side == of_side, 0, 1)
        for at in range(inner // LANES):
            lanes = pl.ds(pl.multiple_of(offset + LANES * at, LANES), LANES)
            mine, other = small_mine_ref[:, lanes], small_other_ref[:, lanes]
            first, second = jnp.where(core == 0, mine, other), jnp.where(core == 0, other, mine)
            place = 8 * (at // 2) + 4 * of_side + 2 * (at % 2)
            for step in range(2):
                block = halves(step, first, second)
                conv_ref[:, LANES * (place + step) : LANES * (place + step + 1)] = block[:taps]
                bias_ref[place + step : place + step + 1, :] = block[taps : taps + 1]
                gate_ref[place + step : place + step + 1, :] = block[taps + 1 : taps + 2]
    shared_blocks = []
    for at in range(inner // LANES, small_width // LANES):
        sides = []
        for of_side in range(2):
            start = small_width * of_side + LANES * at
            first, second = small_both(start, start + LANES)
            sides.append(first + second)
        shared_blocks.append(sides[0] + sides[1])
    for at, block in enumerate(shared_blocks[: shared // LANES]):
        place = 4 * inner // LANES + at
        conv_ref[:, LANES * place : LANES * (place + 1)] = block[:taps]
        bias_ref[place : place + 1, :] = block[taps : taps + 1]
    gain_ref[...] = shared_blocks[shared // LANES]
    scatter_sides = (side, 1 - side)
    for kind in range(3):
        total = jnp.zeros((8, LANES), f32)
        for at, of_side in enumerate(scatter_sides):
            start = small_width * at + LANES * kind
            first, second = small_both(start, start + LANES)
            for of_core, part in enumerate((first, second)):
                pick = (row < heads) & (col == head_number(row, of_side, of_core))
                total = total + exact_dot(part, pick.astype(f32))
        head_refs[kind][...] = total[taps + 2 : taps + 3, : 4 * heads]


def silu_parts(v):
    sig = 1.0 / (1.0 + jnp.exp(-v))
    return sig, v * sig


def conv_block(proj_ref, masks_ref, cw_ref, cb_ref, inner, at):
    signal = proj_ref[:, pl.ds(pl.multiple_of(inner + at * LANES, LANES), LANES)]
    lanes = pl.ds(pl.multiple_of(at * LANES, LANES), LANES)
    taps = cw_ref.shape[0]
    mixed = cb_ref[:, lanes] + cw_ref[taps - 1 : taps, lanes] * signal
    for offset in range(1, taps):
        earlier = pltpu.roll(signal, offset, 0) * masks_ref[offset - 1]
        mixed = mixed + cw_ref[taps - 1 - offset : taps - offset, lanes] * earlier
    return signal, mixed


def decay_prep(proj_ref, heads_ref, inner, head_dim, stepe_ref, cume_ref, cumt_ref):
    tokens, width = proj_ref.shape
    raw = proj_ref[:, width - LANES :] + heads_ref[0:1, :]
    step = jnp.maximum(raw, 0.0) + jnp.log1p(jnp.exp(-jnp.abs(raw)))
    decay = -step * jnp.exp(heads_ref[1:2, :])
    lower = (iota((LANES, LANES), 0) >= iota((LANES, LANES), 1)).astype(f32)
    spread = (
        iota((LANES, inner), 1) // head_dim == iota((LANES, inner), 0)
    ).astype(f32)
    stepe_ref[...] = exact_dot(step, spread)
    for seq in range(tokens // LANES):
        rows = slice(seq * LANES, (seq + 1) * LANES)
        cumul = exact_dot(lower, decay[rows])
        cume_ref[rows, :] = exact_dot(cumul, spread)
        turned = cumul.T
        for pair in range(inner // LANES):
            cumt_ref[pair, 0:2, rows] = turned[2 * pair : 2 * pair + 2]
    return raw, step, decay


def pair_weights(cume_ref, cumt_ref, vis_ref, rows, lanes, pair, half):
    cols = cume_ref[rows, lanes]
    seen = vis_ref[rows, :] > 0.5
    first, second = cumt_ref[pair, 0:1, rows], cumt_ref[pair, 1:2, rows]
    fade_a = jnp.exp(jnp.where(seen, cols[:, 0:1] - first, -1e30))
    fade_b = jnp.exp(jnp.where(seen, cols[:, half : half + 1] - second, -1e30))
    return fade_a, fade_b


def split_heads(block, half):
    lane = iota(block.shape, 1)
    return jnp.concatenate(
        [jnp.where(lane < half, block, 0.0), jnp.where(lane >= half, block, 0.0)], axis=0
    )


def forward_kernel(
    places, in_count, out_count, inner, head_dim,
    rank_ref, gain_ref, gate_gain_ref, cw_ref, cb_ref, heads_ref, skip_ref, *rest,
):
    token_count = 1 + max(ref for ref, _ in places)
    token_rows, rest = rest[:token_count], rest[token_count:]
    in_chunks, out_chunks = rest[:in_count], rest[in_count : in_count + out_count]
    (sums_ref, normed_out, proj_out, mixer_out, dgated_out,
     normed_ref, proj_ref, mixer_ref, dgated_ref, w_ref, w_out_ref, act_ref, stepe_ref, cume_ref,
     cumt_ref, score_ref, sq_ref, cross_ref, masks_ref, vis_ref, tok_ref, cot_ref, seg_ref,
     in_sems, out_sems, store_sems, token_sems) = (
        rest[in_count + out_count :]
    )
    count = len(places)
    tokens_in = token_copies(places, token_rows, tok_ref, 0, LANES, token_sems)
    tokens_in += token_copies(places, token_rows, seg_ref, 2 * LANES, 16, token_sems, count)
    cot_in = token_copies(places, token_rows, cot_ref, LANES, LANES, token_sems, 2 * count)
    copies = in_copies(rank_ref, in_chunks, w_ref, in_sems)
    copies += out_copies(rank_ref, out_chunks, w_out_ref, out_sems)
    for copy in copies:
        copy.start()
    for copy in tokens_in:
        copy.wait()
    hidden = tok_ref[...].astype(f32)
    factor = lax.rsqrt(jnp.mean(hidden * hidden, axis=-1, keepdims=True) + epsilon)
    normed_ref[...] = (hidden * factor * gain_ref[...]).astype(bf16)
    stores = [started(normed_ref, normed_out, store_sems.at[0])]
    spread_marks(seg_ref, masks_ref, vis_ref)
    for copy in copies + cot_in:
        copy.wait()
    tokens, width = proj_ref.shape
    for start in range(0, width, 512):
        end = min(start + 512, width)
        proj_ref[:, start:end] = jnp.dot(
            normed_ref[...], w_ref[:, start:end], preferred_element_type=f32
        )
    for start in range(0, inner, 256):
        lanes = slice(start, start + 256)
        dgated_ref[:, lanes] = low_dot(cot_ref[...], w_out_ref[lanes, :], ((1,), (1,)))
    stores.append(started(proj_ref, proj_out, store_sems.at[1]))
    stores.append(started(dgated_ref, dgated_out, store_sems.at[2]))
    decay_prep(proj_ref, heads_ref, inner, head_dim, stepe_ref, cume_ref, cumt_ref)

    def convolve(at, _):
        signal, mixed = conv_block(proj_ref, masks_ref, cw_ref, cb_ref, inner, at)
        act_ref[:, pl.ds(pl.multiple_of(at * LANES, LANES), LANES)] = silu_parts(mixed)[1]
        return 0

    lax.fori_loop(0, act_ref.shape[1] // LANES, convolve, 0)
    seqs = tokens // LANES
    for seq in range(seqs):
        rows = slice(seq * LANES, (seq + 1) * LANES)
        keys = act_ref[rows, inner : inner + LANES]
        queries = act_ref[rows, inner + LANES :]
        score_ref[rows, :] = exact_dot(queries, keys, ((1,), (1,)))
    sq_ref[...] = jnp.zeros_like(sq_ref)
    cross_ref[...] = jnp.zeros_like(cross_ref)

    def scan(pair, _):
        lanes = pl.ds(pl.multiple_of(pair * LANES, LANES), LANES)
        skip = skip_ref[:, lanes]
        for seq in range(seqs):
            rows = slice(seq * LANES, (seq + 1) * LANES)
            fade_a, fade_b = pair_weights(cume_ref, cumt_ref, vis_ref, rows, lanes, pair, head_dim)
            score = score_ref[rows, :]
            weights = jnp.concatenate([fade_a * score, fade_b * score], axis=1)
            values = act_ref[rows, lanes]
            scaled = split_heads(values * stepe_ref[rows, lanes], head_dim)
            mixed = low_dot(weights, scaled) + skip * values
            mixer_ref[rows, lanes] = mixed
            product = mixed * silu_parts(proj_ref[rows, lanes])[1]
            sq_ref[rows, :] += product * product
            cross_ref[rows, :] += product * gate_gain_ref[:, lanes] * dgated_ref[rows, lanes]
        return 0

    lax.fori_loop(0, inner // LANES, scan, 0)
    stores.append(started(mixer_ref, mixer_out, store_sems.at[3]))
    for seq in range(seqs):
        rows = slice(seq * LANES, (seq + 1) * LANES)
        sums_ref[seq : seq + 1, :] = jnp.sum(sq_ref[rows, :].T, axis=0, keepdims=True)
        at = seqs + seq
        sums_ref[at : at + 1, :] = jnp.sum(cross_ref[rows, :].T, axis=0, keepdims=True)
    for copy in stores:
        copy.wait()


def gated_kernel(
    places, chunk_count, grad_count, inner, full_inner,
    rank_ref, sums_ref, gain_ref, proj_in, mixer_in, *rest,
):
    token_count = 1 + max(ref for ref, _ in places)
    token_rows, rest = rest[:token_count], rest[token_count:]
    chunks = rest[:chunk_count]
    close_ref, away_ref = rest[chunk_count : chunk_count + 2]
    grads = rest[chunk_count + 2 : chunk_count + 2 + grad_count]
    (proj_ref, mixer_ref, gated_ref, factor_ref, w_out_ref, grad_ref, cot_ref, sems, grad_sems, load_sems,
     token_sems) = (
        rest[chunk_count + 2 + grad_count :]
    )
    loads = [
        started(proj_in.at[:, pl.ds(0, inner)], proj_ref, load_sems.at[0]),
        started(mixer_in, mixer_ref, load_sems.at[1]),
    ]
    loads += token_copies(places, token_rows, cot_ref, LANES, LANES, token_sems)
    weights = out_copies(rank_ref, chunks, w_out_ref, sems)
    for copy in weights:
        copy.start()
    tokens = proj_ref.shape[0]
    seqs = tokens // LANES
    for seq in range(seqs):
        row = lax.rsqrt(sums_ref[seq : seq + 1, :] / full_inner + epsilon)
        factor_ref[seq * LANES : (seq + 1) * LANES, :] = jnp.broadcast_to(row, (LANES, LANES)).T
    for copy in loads:
        copy.wait()
    for start in range(0, inner, LANES):
        lanes = slice(start, start + LANES)
        product = mixer_ref[:, lanes] * silu_parts(proj_ref[:, lanes])[1]
        gated_ref[:, lanes] = (product * factor_ref[...] * gain_ref[:, lanes]).astype(bf16)
    for start in range(0, inner, 256):
        lanes = slice(start, start + 256)
        grad_ref[lanes, :] = low_dot(gated_ref[:, lanes], cot_ref[...], ((0,), (0,))).astype(bf16)
    copies = out_grad_copies(rank_ref, grads, grad_ref, grad_sems)
    for copy in copies:
        copy.start()
    for copy in weights:
        copy.wait()
    half = tokens // 2
    close_ref[...] = jnp.dot(gated_ref[:half, :], w_out_ref[...], preferred_element_type=f32)
    away = jnp.dot(gated_ref[half:, :], w_out_ref[...], preferred_element_type=f32)
    away_ref[...] = away.astype(bf16)
    for copy in copies:
        copy.wait()


def backward_kernel(
    places, weight_count, chunk_count, inner, head_dim, full_inner,
    rank_ref, sums_ref, gain_ref, cw_ref, cb_ref, heads_ref, skip_ref,
    normed_in, proj_in, mixer_in, dgated_in, *rest,
):
    token_count = 1 + max(ref for ref, _ in places)
    token_rows, rest = rest[:token_count], rest[token_count:]
    weight_chunks = rest[:weight_count]
    rest = rest[weight_count:]
    close_ref, away_ref, small_ref, coded_ref = rest[:4]
    chunks = rest[4 : 4 + chunk_count]
    (normed_ref, proj_ref, mixer_ref, dgated_ref, masks_ref, vis_ref, dact_ref,
     act_ref, stepe_ref, cume_ref, cumt_ref, score_ref, dscore_ref, dstep_ref,
     rowsum_ref, colsum_ref, turned_ref, dskip_ref, factor_ref, pull_ref, turned_normed_ref, grad_ref,
     w_ref, dproj_ref, tok_ref, seg_ref, carried_ref, weight_sems, sems, load_sems, token_sems) = (
        rest[4 + chunk_count :]
    )
    seg_in = token_copies(places, token_rows, seg_ref, 2 * LANES, 16, token_sems)
    loads = [
        started(source, target, load_sems.at[at])
        for at, (source, target) in enumerate(
            ((proj_in, proj_ref), (mixer_in, mixer_ref), (dgated_in, dgated_ref), (normed_in, normed_ref))
        )
    ]
    weights = in_copies(rank_ref, weight_chunks, w_ref, weight_sems)
    for copy in weights:
        copy.start()
    weights += token_copies(places, token_rows, tok_ref, 0, LANES, token_sems, len(places))
    for copy in seg_in:
        copy.wait()
    spread_marks(seg_ref, masks_ref, vis_ref)
    loads[0].wait()
    tokens, width = proj_ref.shape
    seqs = tokens // LANES
    raw, step, decay = decay_prep(
        proj_ref, heads_ref, inner, head_dim, stepe_ref, cume_ref, cumt_ref
    )
    small_ref[...] = jnp.zeros_like(small_ref)

    def convolve(at, _):
        signal, mixed = conv_block(proj_ref, masks_ref, cw_ref, cb_ref, inner, at)
        act_ref[:, pl.ds(pl.multiple_of(at * LANES, LANES), LANES)] = silu_parts(mixed)[1]
        return 0

    lax.fori_loop(0, act_ref.shape[1] // LANES, convolve, 0)
    for seq in range(seqs):
        rows = slice(seq * LANES, (seq + 1) * LANES)
        keys = act_ref[rows, inner : inner + LANES]
        queries = act_ref[rows, inner + LANES :]
        score_ref[rows, :] = exact_dot(queries, keys, ((1,), (1,)))
    dscore_ref[...] = jnp.zeros_like(dscore_ref)
    dstep_ref[...] = jnp.zeros_like(dstep_ref)
    rowsum_ref[...] = jnp.zeros_like(rowsum_ref)
    turned_ref[...] = jnp.zeros_like(turned_ref)
    dskip_ref[...] = jnp.zeros_like(dskip_ref)
    for seq in range(seqs):
        rows = slice(seq * LANES, (seq + 1) * LANES)
        row = lax.rsqrt(sums_ref[seq : seq + 1, :] / full_inner + epsilon)
        pulled = row * row * row * sums_ref[seqs + seq : seqs + seq + 1, :] / full_inner
        factor_ref[rows, :] = jnp.broadcast_to(row, (LANES, LANES)).T
        pull_ref[rows, :] = jnp.broadcast_to(pulled, (LANES, LANES)).T

    def scan(pair, _):
        lanes = pl.ds(pl.multiple_of(pair * LANES, LANES), LANES)
        skip = skip_ref[:, lanes]
        gain = gain_ref[:, lanes]
        collect = (
            iota((LANES, LANES), 0) // head_dim + 2 * pair == iota((LANES, LANES), 1)
        ).astype(f32)
        dgain = jnp.zeros((1, LANES), f32)
        dskip = jnp.zeros((1, LANES), f32)
        for seq in range(seqs):
            rows = slice(seq * LANES, (seq + 1) * LANES)
            gate = proj_ref[rows, lanes]
            sig, gate_act = silu_parts(gate)
            mixed = mixer_ref[rows, lanes]
            product = mixed * gate_act
            dgated = dgated_ref[rows, lanes]
            factor = factor_ref[rows, :]
            dproduct = factor * gain * dgated - product * pull_ref[rows, :]
            dgain = dgain + jnp.sum(dgated * product * factor, axis=0, keepdims=True)
            dgate = dproduct * mixed * (sig * (1.0 + gate * (1.0 - sig)))
            dproj_ref[rows, lanes] = dgate.astype(bf16)
            dmixed = dproduct * gate_act
            values = act_ref[rows, lanes]
            stepe = stepe_ref[rows, lanes]
            dskip = dskip + jnp.sum(dmixed * values, axis=0, keepdims=True)
            fade_a, fade_b = pair_weights(cume_ref, cumt_ref, vis_ref, rows, lanes, pair, head_dim)
            score = score_ref[rows, :]
            weights_a, weights_b = fade_a * score, fade_b * score
            dsplit = split_heads(dmixed, head_dim)
            dweights = low_dot(dsplit, values * stepe, ((1,), (1,)))
            dweights_a, dweights_b = dweights[:LANES], dweights[LANES:]
            dscore_ref[rows, :] += dweights_a * fade_a + dweights_b * fade_b
            spread_a, spread_b = dweights_a * weights_a, dweights_b * weights_b
            lane = iota((LANES, LANES), 1)
            rowsum_ref[rows, :] += jnp.where(
                lane == 2 * pair,
                jnp.sum(spread_a, axis=1, keepdims=True),
                jnp.where(lane == 2 * pair + 1, jnp.sum(spread_b, axis=1, keepdims=True), 0.0),
            )
            colsum_ref[pair, 0:1, rows] = jnp.sum(spread_a, axis=0, keepdims=True)
            colsum_ref[pair, 1:2, rows] = jnp.sum(spread_b, axis=0, keepdims=True)
            weights = jnp.concatenate([weights_a, weights_b], axis=0)
            dscaled = low_dot(weights, dsplit, ((0,), (0,)))
            dact_ref[rows, lanes] = dscaled * stepe + skip * dmixed
            dstep_ref[rows, :] += exact_dot(dscaled * values, collect)
        small_ref[5:6, lanes] = dgain
        dskip_ref[0:1, lanes] = dskip
        return 0

    for copy in loads[1:]:
        copy.wait()
    lax.fori_loop(0, inner // LANES, scan, 0)
    for pair in range(inner // LANES):
        turned_ref[2 * pair : 2 * pair + 2, :] = colsum_ref[pair, 0:2, :]
    upper = (iota((LANES, LANES), 0) <= iota((LANES, LANES), 1)).astype(f32)
    rate = jnp.exp(heads_ref[1:2, :])
    ddt = jnp.zeros((1, LANES), f32)
    dalog = jnp.zeros((1, LANES), f32)
    for seq in range(seqs):
        rows = slice(seq * LANES, (seq + 1) * LANES)
        keys = act_ref[rows, inner : inner + LANES]
        queries = act_ref[rows, inner + LANES :]
        dscore = dscore_ref[rows, :]
        dact_ref[rows, inner : inner + LANES] = exact_dot(dscore, queries, ((0,), (0,)))
        dact_ref[rows, inner + LANES :] = exact_dot(dscore, keys)
        dcumul = rowsum_ref[rows, :] - turned_ref[:, rows].T
        ddecay = exact_dot(upper, dcumul)
        dalog = dalog + jnp.sum(ddecay * decay[rows], axis=0, keepdims=True)
        dstep = dstep_ref[rows, :] - ddecay * rate
        draw = dstep / (1.0 + jnp.exp(-raw[rows]))
        ddt = ddt + jnp.sum(draw, axis=0, keepdims=True)
        dproj_ref[rows, width - LANES :] = draw.astype(bf16)
    gather = (
        iota((inner, LANES), 0) // head_dim == iota((inner, LANES), 1)
    ).astype(f32)
    dskip_heads = exact_dot(dskip_ref[...], gather)
    small_ref[6:7, 0:LANES] = ddt
    small_ref[6:7, LANES : 2 * LANES] = dalog
    small_ref[6:7, 2 * LANES : 3 * LANES] = dskip_heads[0:1]

    def convolve_back(at, _):
        lanes = pl.ds(pl.multiple_of(at * LANES, LANES), LANES)
        signal, mixed = conv_block(proj_ref, masks_ref, cw_ref, cb_ref, inner, at)
        sig, _unused = silu_parts(mixed)
        dmixed = dact_ref[:, lanes] * (sig * (1.0 + mixed * (1.0 - sig)))
        taps = cw_ref.shape[0]
        small_ref[taps : taps + 1, lanes] = jnp.sum(dmixed, axis=0, keepdims=True)
        small_ref[taps - 1 : taps, lanes] = jnp.sum(dmixed * signal, axis=0, keepdims=True)
        dsignal = cw_ref[taps - 1 : taps, lanes] * dmixed
        for offset in range(1, taps):
            masked = dmixed * masks_ref[offset - 1]
            place = taps - 1 - offset
            small_ref[place : place + 1, lanes] = jnp.sum(
                masked * pltpu.roll(signal, offset, 0), axis=0, keepdims=True
            )
            dsignal = dsignal + cw_ref[place : place + 1, lanes] * pltpu.roll(
                masked, tokens - offset, 0
            )
        dproj_ref[:, pl.ds(pl.multiple_of(inner + at * LANES, LANES), LANES)] = dsignal.astype(bf16)
        return 0

    lax.fori_loop(0, dact_ref.shape[1] // LANES, convolve_back, 0)
    for seq in range(seqs):
        rows = slice(seq * LANES, (seq + 1) * LANES)
        turned_normed_ref[:, rows] = normed_ref[rows, :].astype(f32).T.astype(bf16)
    for start in range(0, width, 512):
        lanes = slice(start, min(start + 512, width))
        grad_ref[:, lanes] = low_dot(turned_normed_ref[...], dproj_ref[:, lanes]).astype(bf16)
    copies = in_grad_copies(rank_ref, chunks, grad_ref, sems)
    for copy in copies:
        copy.start()
    for copy in weights:
        copy.wait()
    model = w_ref.shape[0]
    hidden = tok_ref[...].astype(f32)
    token_factor = lax.rsqrt(jnp.mean(hidden * hidden, axis=-1, keepdims=True) + epsilon)
    conv_width = dact_ref.shape[1]
    part = model // 8
    for start in range(0, model, 256):
        lanes = slice(start, start + 256)
        dnormed = low_dot(dproj_ref[...], w_ref[lanes, :], ((1,), (1,)))
        half = tokens // 2
        close_ref[:, lanes] = dnormed[:half]
        away_ref[:, lanes] = dnormed[half:].astype(bf16)
        dgain = jnp.sum(dnormed * hidden[:, lanes] * token_factor, axis=0, keepdims=True)
        for at in range(0, 256, part):
            row = (start + at) // part
            small_ref[row : row + 1, conv_width:] = dgain[:, at : at + part]
    high = small_ref[...].astype(bf16)
    low = small_ref[...] - high.astype(f32)
    coded_ref[...] = jnp.concatenate([high.astype(f32), low], axis=0).astype(bf16)
    if chunk_count > 1:
        carried_ref[...] = jnp.zeros_like(carried_ref)
        carried_ref[:, : coded_ref.shape[1]] = coded_ref[...]
        held = chunks[2].at[pl.ds(chunks[2].shape[0] - 16, 16)]
        copies.append(started(carried_ref, held, token_sems.at[2 * len(places)]))
    for copy in copies:
        copy.wait()


def tail_kernel(tok_ref, cot_ref, gain_ref, mine_ref, other_ref, dtok_ref):
    hidden = tok_ref[...].astype(f32)
    factor = lax.rsqrt(jnp.mean(hidden * hidden, axis=-1, keepdims=True) + epsilon)
    dnormed = mine_ref[...] + other_ref[...]
    scaled = dnormed * gain_ref[...]
    pull = jnp.mean(scaled * hidden, axis=-1, keepdims=True) * factor * factor * factor
    dtok_ref[...] = cot_ref[...].astype(f32) + scaled * factor - hidden * pull


def after(x, *others):
    return lax.optimization_barrier((x, *others))[0]


class Links:
    first, second = (1, 2), (2, 1)
    slots = (0, 4, 8, 12)

    def __init__(self, reps, chips, paired):
        self.reps, self.chips, self.paired = reps, chips, paired
        self.rep = lax.axis_index("rep")
        self.chip = lax.axis_index("fsdp")
        self.side = self.chip // 4 % 2

    def exchange(self, x, masks):
        if isinstance(masks, int):
            masks = (masks, masks)
        pairs = [
            (core * self.chips + chip, core * self.chips + (chip ^ masks[core]))
            for core in range(self.reps)
            for chip in range(self.chips)
        ]
        return lax.ppermute(x, BOTH, pairs)

    def swap(self, x):
        return lax.ppermute(x, "rep", [(0, 1), (1, 0)])

    def spread(self, block):
        near = self.exchange(block, self.first)
        side = self.exchange(block, self.second)
        return [block, near, side, self.exchange(near, self.second)]

    def gather(self, keep, give):
        beside, across = self.exchange(give, self.slots[1]), self.exchange(keep, self.slots[2])
        own, near = self.spread(keep), self.spread(beside)
        far = self.exchange(after(give, beside), self.slots[3])
        return [own, near, self.spread(after(across, *own[2:], near[2])), self.spread(after(far, near[3]))]

    def square_with(self, own, near, send, small, earlier):
        rows, width = own.shape
        count = small.shape[0] // 2

        def decoded(x):
            x = x[-2 * count :, : small.shape[1]].astype(f32)
            return x[:count] + x[count:]

        came = self.exchange(send, self.second)
        near = (near.astype(f32) + came[rows : 2 * rows].astype(f32)).astype(bf16)
        near = after(near, earlier)
        total = decoded(small) + decoded(came)
        high = lax.reduce_precision(total, 8, 7)
        coded = jnp.concatenate([high, total - high]).astype(bf16)
        ride = jnp.pad(coded, ((0, 0), (0, width - small.shape[1])))
        last = self.exchange(jnp.concatenate([near, ride]), self.first)
        total = decoded(coded) + decoded(last)
        return own.astype(f32) + came[:rows].astype(f32) + last[:rows].astype(f32), total, came

    def square_at_once(self, own, near, side, far):
        moved = [self.exchange(near, self.first), self.exchange(side, self.second), self.exchange(far, 3)]
        return sum((x.astype(f32) for x in moved), own.astype(f32)), moved

    def across(self, x):
        return self.exchange(x.astype(bf16), self.slots[2])

    def beside(self, x):
        return self.exchange(x.astype(bf16), self.slots[1]).astype(f32)

    def square_second(self, own, near, came, meanwhile):
        rows = own.shape[0]
        near = (near.astype(f32) + came[rows:].astype(f32)).astype(bf16)
        near = self.exchange(after(near, *meanwhile), self.first)
        return own.astype(f32) + came[:rows].astype(f32) + near.astype(f32)

    def sum_lines(self, x):
        same, beside, other = (self.exchange(x, slot) for slot in (8, 4, 12))
        return jnp.concatenate([x + same, beside + other], axis=1)

    def group_rows(self, x, others):
        other = after(self.exchange(x, self.slots[1]), *others)
        return [x, self.swap(jnp.concatenate([x, other])), other]

    def from_reps(self, x):
        whole = lax.all_gather(x, "rep", axis=0)
        return [whole[at] for at in range(self.reps)]

    def sum_group(self, x):
        if not self.paired:
            return lax.psum(x, "rep")

        def reordered(y, bit):
            return jnp.concatenate([y[at ^ bit : (at ^ bit) + 1] for at in range(y.shape[0])])

        x = x + reordered(self.exchange(x, self.slots[1]), 2)
        return x + reordered(self.swap(x), 1)

    def from_side(self, x):
        return self.exchange(x, self.slots[1])

    def own_rows(self, x, came):
        rows = x.shape[0] // 2
        came = came.astype(f32)
        return x[:rows] + came[:rows], self.swap(x[rows:] + came[rows:])

    def scattered(self, close, away):
        x = jnp.concatenate([close, away.astype(f32)])
        mine = lax.psum_scatter(x, "rep", scatter_dimension=0, tiled=True)
        return mine, jnp.zeros_like(mine)


def per_device(
    reps, chips,
    tokens, segment_ids, norm_gain, in_weight, conv_weight, conv_bias, dt_bias, a_log, skip_gain,
    gate_gain, out_weight, cotangent,
):
    full_inner, full_heads = gate_gain.shape[0], dt_bias.shape[0]
    conv_dim, taps = conv_bias.shape[0], conv_weight.shape[0]
    model = norm_gain.shape[0]
    state = (conv_dim - full_inner) // 2
    head_dim = full_inner // full_heads
    rows_in, rows_out = in_weight.shape[0], out_weight.shape[0]
    paired = (reps, chips, full_heads) == (2, 16, 32) and rows_out == 2 * rows_in == 2 * head_dim
    ranks = 4 if paired else reps
    inner, heads = full_inner // ranks, full_heads // ranks
    links = Links(reps, chips, paired)
    rep, chip = links.rep, links.chip
    conv_local = inner + 2 * state
    width = inner + conv_local + LANES
    own_tokens = tokens.shape[0]
    total = own_tokens * ranks

    def arr(*shape, dtype=f32):
        return jax.ShapeDtypeStruct(shape, dtype)

    def vmem(*shape, dtype=f32):
        return pltpu.VMEM(shape, dtype)

    def own_heads(x, size):
        lead = x.shape[:-1]
        if paired:
            split = x.reshape(lead + (2, 2, 4, 2, size))
            split = lax.dynamic_index_in_dim(split, links.side, split.ndim - 4, False)
        else:
            split = x.reshape(lead + (heads, reps, size))
        split = lax.dynamic_index_in_dim(split, rep, split.ndim - 2, False)
        return split.reshape(lead + (heads * size,))

    def all_heads(parts, size):
        lead = parts[0].shape[:-1]
        if paired:
            split = [part.reshape(lead + (2, 1, 4, 1, size)) for part in parts]
            sides = [jnp.concatenate(split[at : at + 2], axis=-2) for at in (0, 2)]
            whole = jnp.concatenate(sides, axis=-4)
        else:
            whole = jnp.concatenate([part.reshape(lead + (heads, 1, size)) for part in parts], axis=-2)
        return whole.reshape(lead + (full_heads * size,))

    rank = jnp.stack([links.side, rep, chip]).astype(jnp.int32)
    if paired:
        keep, give = pl.pallas_call(
            functools.partial(pack_kernel, inner, state, heads),
            out_shape=[arr(rows_in, width + model, dtype=bf16), arr(rows_in, width, dtype=bf16)],
            in_specs=in_smem(1) + in_vmem(2),
            out_specs=in_vmem(2),
            compiler_params=params(),
            name="pack",
        )(rank, in_weight, out_weight)
        slots = links.gather(keep, give)
        first_rows = slots[1][0]
        conv_w, conv_b, gate_g, norm_g, head_rows, skip = pl.pallas_call(
            functools.partial(prepare_kernel, inner, state, heads, head_dim),
            out_shape=[
                arr(taps, conv_local), arr(1, conv_local), arr(1, inner), arr(1, model), arr(8, LANES),
                arr(1, inner),
            ],
            in_specs=in_smem(1) + in_vmem(7),
            out_specs=in_vmem(6),
            compiler_params=params(),
            name="prepare",
        )(rank, conv_weight, conv_bias.reshape(-1, LANES), gate_gain.reshape(-1, LANES),
          norm_gain.reshape(-1, LANES), dt_bias[None], a_log[None], skip_gain[None])
        in_chunks, out_chunks = sum(slots, []), slots[0] + slots[2]
        in_shapes = [(rows_in, 2 * width), (rows_in, 2 * width), (2 * rows_in, 2 * width)] * 2
        in_shapes[2] = (2 * rows_in + 16, 2 * width)
        out_shapes = [(2 * rows_in, model)] * 4
    else:
        in_full = lax.all_gather(in_weight, "fsdp", axis=0, tiled=True)
        out_full = lax.all_gather(out_weight, "fsdp", axis=0, tiled=True)
        ends = [full_inner, 2 * full_inner, full_inner + conv_dim]
        gates, signals, shared, step_cols = jnp.split(in_full, ends, axis=1)
        in_chunks = [
            jnp.concatenate(
                [own_heads(gates, head_dim), own_heads(signals, head_dim), shared, own_heads(step_cols, 1),
                 jnp.zeros((model, LANES - heads), bf16)],
                axis=1,
            )
        ]
        out_chunks = [own_heads(out_full.T, head_dim).T]
        def local_conv(x):
            return jnp.concatenate([own_heads(x[:, :full_inner], head_dim), x[:, full_inner:]], axis=1)

        conv_w, conv_b = local_conv(conv_weight), local_conv(conv_bias[None])

        def lane_row(x):
            return jnp.pad(own_heads(x, 1), (0, LANES - heads))

        head_rows = jnp.pad(jnp.stack([lane_row(dt_bias), lane_row(a_log)]), ((0, 6), (0, 0)))
        skip = jnp.repeat(own_heads(skip_gain, 1), head_dim)[None]
        gate_g = own_heads(gate_gain, head_dim)[None]
        norm_g = norm_gain[None]
        in_shapes, out_shapes = [(model, width)], [(inner, model)]
    extra = jnp.pad(segment_ids.astype(bf16), ((0, 15), (0, model - segment_ids.shape[1])))
    own_rows = jnp.concatenate([tokens, cotangent, extra])
    held = own_rows.shape[0]
    if paired:
        own_rows = after(own_rows, first_rows)
        waits = slots[0][3:] + slots[1][1:3] + slots[2][1:3] + slots[3][:1]
        token_rows = links.group_rows(own_rows, waits)
        places = ((0, 0), (1, 0), (2, 0), (1, held))
    else:
        token_rows = links.from_reps(own_rows)
        places = tuple((at, 0) for at in range(reps))
    in_shapes = [arr(*shape, dtype=bf16) for shape in in_shapes]
    out_shapes = [arr(*shape, dtype=bf16) for shape in out_shapes]
    in_count, out_count = len(in_chunks), len(out_chunks)

    w_in, w_out = vmem(model, width, dtype=bf16), vmem(inner, model, dtype=bf16)
    in_sems, out_sems = (pltpu.SemaphoreType.DMA((n,)) for n in (in_count, out_count))
    def sems(n):
        return pltpu.SemaphoreType.DMA((n,))

    kept = [vmem(total, model, dtype=bf16), vmem(total, width), vmem(total, inner), vmem(total, inner)]
    tok, segs = vmem(total, model, dtype=bf16), vmem(16 * len(places), LANES, dtype=bf16)
    conv_masks = [vmem(taps - 1, total, LANES), vmem(total, LANES)]
    sums, normed, projected, mixed, d_gated = pl.pallas_call(
        functools.partial(forward_kernel, places, in_count, out_count, inner, head_dim),
        out_shape=[
            arr(2 * total // LANES, LANES), arr(total, model, dtype=bf16), arr(total, width),
            arr(total, inner), arr(total, inner),
        ],
        in_specs=in_smem(1) + in_vmem(6) + in_hbm(len(token_rows) + in_count + out_count),
        out_specs=in_vmem(1) + in_hbm(4),
        scratch_shapes=kept + [
            w_in, w_out,
            vmem(total, conv_local), vmem(total, inner), vmem(total, inner), vmem(inner // LANES, 8, total),
            vmem(total, LANES), vmem(total, LANES), vmem(total, LANES), *conv_masks,
            tok, tok, segs, in_sems, out_sems, sems(4), sems(3 * len(places)),
        ],
        compiler_params=params(),
        cost_estimate=cost(14),
        name="forward",
    )(rank, norm_g, gate_g, conv_w, conv_b, head_rows, skip, *token_rows, *in_chunks, *out_chunks)
    sums = links.sum_group(sums)
    block_close, block_away, *out_grads = pl.pallas_call(
        functools.partial(gated_kernel, places, out_count, len(out_shapes), inner, full_inner),
        out_shape=[arr(total // 2, model), arr(total // 2, model, dtype=bf16)] + out_shapes,
        in_specs=in_smem(1) + in_vmem(2) + in_hbm(2 + len(token_rows) + out_count),
        out_specs=in_vmem(2) + in_hbm(len(out_shapes)),
        scratch_shapes=[
            vmem(total, inner), vmem(total, inner), vmem(total, inner, dtype=bf16), vmem(total, LANES), w_out,
            vmem(inner, model, dtype=bf16), tok, out_sems, out_sems, sems(2), sems(len(places)),
        ],
        compiler_params=params(),
        cost_estimate=cost(6),
        name="gated",
    )(rank, sums, gate_g, projected, mixed, *token_rows, *out_chunks)
    if paired:
        out_sums, moved = links.square_at_once(*out_grads)
        sums = after(sums, out_grads[2])
        block_came = links.from_side(block_away)
    d_normed_close, d_normed_away, small, coded, *in_grads = pl.pallas_call(
        functools.partial(backward_kernel, places, in_count, len(in_shapes), inner, head_dim, full_inner),
        out_shape=[
            arr(total // 2, model), arr(total // 2, model, dtype=bf16),
            arr(8, conv_local + model // 8), arr(16, conv_local + model // 8, dtype=bf16),
        ] + in_shapes,
        in_specs=in_smem(1) + in_vmem(6) + in_hbm(4 + len(token_rows) + in_count),
        out_specs=in_vmem(4) + in_hbm(len(in_shapes)),
        scratch_shapes=kept + conv_masks + [
            vmem(total, conv_local),
            vmem(total, conv_local), vmem(total, inner), vmem(total, inner), vmem(inner // LANES, 8, total),
            vmem(total, LANES), vmem(total, LANES), vmem(total, LANES),
            vmem(total, LANES), vmem(inner // LANES, 8, total), vmem(LANES, total), vmem(8, inner),
            vmem(total, LANES), vmem(total, LANES), vmem(model, total, dtype=bf16), w_in, w_in,
            vmem(total, width, dtype=bf16), tok, segs, vmem(16, 2 * width, dtype=bf16), in_sems, in_sems, sems(4),
            sems(2 * len(places) + 1),
        ],
        compiler_params=params(),
        cost_estimate=cost(24),
        name="backward",
    )(rank, sums, gate_g, conv_w, conv_b, head_rows, skip, normed, projected, mixed, d_gated, *token_rows,
      *in_chunks)

    if paired:
        out_across = links.across(out_sums[rows_in:])
        far, small, came = links.square_with(
            *in_grads[:2], after(in_grads[2], block_came, *moved), coded, out_across
        )
        came = links.exchange(after(in_grads[5], came), links.second)
        far = links.across(far).astype(f32)
        small = links.sum_lines(after(small, came))
        small_other = links.swap(small)
        d_normed_parts = links.own_rows(d_normed_close, after(links.from_side(d_normed_away), came))
        block_parts = links.own_rows(block_close, block_came)
    else:
        out_sum, in_sum = (
            lax.psum_scatter(grads[0], "fsdp", scatter_dimension=0, tiled=True).astype(f32)
            for grads in (out_grads, in_grads)
        )
        smalls = links.from_reps(lax.psum(small, "fsdp"))
        d_normed_parts = links.scattered(d_normed_close, d_normed_away)
        block_parts = links.scattered(block_close, block_away)
    d_tokens = pl.pallas_call(
        tail_kernel,
        out_shape=arr(own_tokens, model),
        in_specs=in_vmem(5),
        out_specs=in_vmem(1)[0],
        compiler_params=params(),
        cost_estimate=cost(2),
        name="tail",
    )(tokens, cotangent, norm_g, *d_normed_parts)
    block_out = (tokens.astype(f32) + (block_parts[0] + block_parts[1])).astype(bf16)

    if paired:
        close = links.square_second(*in_grads[3:5], came, [d_tokens, block_out])
        other = links.beside(after(close[:, width:] + far[:, width:], small_other))
        out_sum = out_sums[:rows_in] + out_across.astype(f32)
        grad_sum = jnp.concatenate([close[:, :width] + far[:, :width], out_sum, other], axis=1)
        d_in_weight, d_out_weight, d_conv_weight, d_conv_bias, d_gate_gain, d_norm_gain, *by_head = pl.pallas_call(
            functools.partial(unpack_kernel, inner, state, heads, model, taps),
            out_shape=[
                arr(*in_weight.shape), arr(*out_weight.shape), arr(taps, conv_dim), arr(conv_dim // LANES, LANES),
                arr(full_inner // LANES, LANES), arr(8, model // 8), *[arr(1, full_heads)] * 3,
            ],
            in_specs=in_smem(1) + in_vmem(4),
            out_specs=in_vmem(9),
            compiler_params=params(),
            name="unpack",
        )(rank, grad_sum, links.swap(grad_sum), small, small_other)
        d_conv_bias, d_gate_gain, d_norm_gain = (x.reshape(-1) for x in (d_conv_bias, d_gate_gain, d_norm_gain))
        d_dt_bias, d_a_log, d_skip_gain = (x.reshape(-1) for x in by_head)
    else:
        parts = [part[:, :inner] for part in smalls]
        shared = sum(part[:, inner:] for part in smalls)
        d_norm_gain = shared[:, 2 * state :].reshape(-1)
        d_conv = jnp.concatenate([all_heads(parts, head_dim), shared[:, : 2 * state]], axis=1)
        d_conv_weight, d_conv_bias = d_conv[:taps], d_conv[taps]
        d_gate_gain = d_conv[taps + 1, :full_inner]
        d_dt_bias, d_a_log, d_skip_gain = (
            all_heads([part[taps + 2, at * LANES : at * LANES + heads] for part in parts], 1) for at in range(3)
        )
        in_parts = links.from_reps(in_sum)
        mid = 2 * inner
        end = mid + 2 * state
        d_in_weight = jnp.concatenate(
            [
                all_heads([part[:, :inner] for part in in_parts], head_dim),
                all_heads([part[:, inner:mid] for part in in_parts], head_dim),
                sum(part[:, mid:end] for part in in_parts),
                all_heads([part[:, end : end + heads] for part in in_parts], 1),
            ],
            axis=1,
        )
        held = links.from_reps(lax.all_gather(out_sum, "fsdp", axis=0, tiled=True))
        whole = all_heads([part.T for part in held], head_dim).T
        d_out_weight = lax.dynamic_slice_in_dim(whole, chip * rows_out, rows_out, 0)
    return (
        block_out, d_tokens, d_norm_gain, d_in_weight, d_conv_weight, d_conv_bias, d_dt_bias, d_a_log,
        d_skip_gain, d_gate_gain, d_out_weight,
    )


def solution(mesh):
    rows = P(("rep", "fsdp"), None)
    in_specs = (
        rows, rows, P(), P("fsdp", None), P(), P(), P(), P(), P(), P(), P("fsdp", None), rows,
    )
    out_specs = (
        rows, rows, P(), P("fsdp", None), P(), P(), P(), P(), P(), P(), P("fsdp", None),
    )
    reps, chips = mesh.shape["rep"], mesh.shape["fsdp"]
    return jax.shard_map(
        functools.partial(per_device, reps, chips),
        mesh=mesh, in_specs=in_specs, out_specs=out_specs, check_vma=False,
    )
```

```python
import functools

import jax
import jax.numpy as jnp
from jax import lax
from jax.experimental import pallas as pl
from jax.experimental.pallas import tpu as pltpu
from jax.sharding import PartitionSpec as P

epsilon = 1e-05
highest = lax.Precision.HIGHEST
f32 = jnp.float32
bf16 = jnp.bfloat16
LANES = 128
MIB = 1024 * 1024
BOTH = ("rep", "fsdp")


def exact_dot(a, b, dims=((1,), (0,))):
    return lax.dot_general(a, b, (dims, ((), ())), precision=highest, preferred_element_type=f32)


def low_dot(a, b, dims=((1,), (0,))):
    return lax.dot_general(
        a.astype(bf16), b.astype(bf16), (dims, ((), ())), preferred_element_type=f32
    )


def iota(shape, dim):
    return lax.broadcasted_iota(jnp.int32, shape, dim)


def cost(microseconds):
    return pl.CostEstimate(flops=0, transcendentals=0, bytes_accessed=microseconds * 3500000)


def params(mebibytes=56):
    return pltpu.CompilerParams(vmem_limit_bytes=mebibytes * MIB)


def in_vmem(n):
    return [pl.BlockSpec(memory_space=pltpu.VMEM)] * n


def in_smem(n):
    return [pl.BlockSpec(memory_space=pltpu.SMEM)] * n


def in_hbm(n):
    return [pl.BlockSpec(memory_space=pltpu.HBM)] * n


def source_chip(rank_ref, slot, place):
    first = jnp.where(rank_ref[1] == 0, 1, 2)
    step = (0, first, 3 - first, 3)[place]
    return rank_ref[2] ^ (4 * slot) ^ step


def in_rows(rank_ref, slot, place, rows):
    return pl.ds(pl.multiple_of(source_chip(rank_ref, slot, place) * rows, 16), rows)


def out_rows(rank_ref, slot, place, rows):
    chip = source_chip(rank_ref, slot, place)
    return pl.ds(pl.multiple_of((4 * (chip // 8) + chip % 4) * rows, 16), rows)


def in_copies(rank_ref, chunks, whole, sems):
    copies = []
    for at, chunk in enumerate(chunks):
        part = chunk.at[:, pl.ds(0, whole.shape[1])]
        if len(chunks) > 1:
            target = whole.at[in_rows(rank_ref, at // 4, at % 4, chunk.shape[0])]
        else:
            target = whole
        copies.append(pltpu.make_async_copy(part, target, sems.at[at]))
    return copies


def out_copies(rank_ref, chunks, whole, sems):
    copies = []
    width = whole.shape[1]
    for at, chunk in enumerate(chunks):
        part = chunk.at[:, pl.ds(chunk.shape[1] - width, width)]
        if len(chunks) > 1:
            target = whole.at[out_rows(rank_ref, at // 4 * 2, at % 4, chunk.shape[0])]
        else:
            target = whole
        copies.append(pltpu.make_async_copy(part, target, sems.at[at]))
    return copies


def in_grad_copies(rank_ref, chunks, whole, sems):
    if len(chunks) == 1:
        return [pltpu.make_async_copy(whole, chunks[0], sems.at[0])]
    copies = []
    width = whole.shape[1]
    rows = chunks[0].shape[0]
    for group, first_slot in enumerate((2, 0)):
        for side in range(2):
            for place in range(4):
                chunk = chunks[3 * group + min(place, 2)]
                held = chunk.at[pl.ds(rows * (place == 3), rows), pl.ds(side * width, width)]
                part = whole.at[in_rows(rank_ref, first_slot + side, place, rows)]
                copies.append(pltpu.make_async_copy(part, held, sems.at[len(copies)]))
    return copies


def out_grad_copies(rank_ref, chunks, whole, sems):
    if len(chunks) == 1:
        return [pltpu.make_async_copy(whole, chunks[0], sems.at[0])]
    copies = []
    rows = chunks[0].shape[0] // 2
    for place, chunk in enumerate(chunks):
        for at in range(2):
            part = whole.at[out_rows(rank_ref, 2 * at, place, rows)]
            copies.append(pltpu.make_async_copy(part, chunk.at[pl.ds(at * rows, rows)], sems.at[len(copies)]))
    return copies


def started(source, target, sem):
    copy = pltpu.make_async_copy(source, target, sem)
    copy.start()
    return copy


def token_copies(places, refs, target, start, rows, sems, first=0):
    width = target.shape[1]
    return [
        started(
            refs[ref].at[pl.ds(row + start, rows), pl.ds(0, width)],
            target.at[pl.ds(at * rows, rows)],
            sems.at[first + at],
        )
        for at, (ref, row) in enumerate(places)
    ]


def spread_marks(seg_ref, masks_ref, vis_ref):
    row, col = iota((LANES, LANES), 0), iota((LANES, LANES), 1)
    for seq in range(seg_ref.shape[0] // 16):
        rows = slice(seq * LANES, (seq + 1) * LANES)
        across = jnp.broadcast_to(seg_ref[16 * seq : 16 * seq + 1, :].astype(f32), (LANES, LANES))
        down = across.T
        vis_ref[rows, :] = ((across == down) & (row >= col)).astype(f32)
        for offset in range(1, masks_ref.shape[0] + 1):
            same = (pltpu.roll(down, offset, 0) == down) & (row >= offset)
            masks_ref[offset - 1, rows, :] = same.astype(f32)


def halves(core, even, odd):
    lane = iota(even.shape, 1)
    low = jnp.where(lane < LANES // 2, even, pltpu.roll(odd, LANES // 2, 1))
    high = jnp.where(lane < LANES // 2, pltpu.roll(even, LANES // 2, 1), odd)
    return jnp.where(core == 0, low, high)


def head_blocks(inner, group, at, side):
    start = 4 * inner * group + LANES * (8 * (at // 2) + 2 * (at % 2))
    first = pl.multiple_of(start + 4 * LANES * side, LANES)
    return pl.ds(first, LANES), pl.ds(pl.multiple_of(first + LANES, LANES), LANES)


def head_number(local, side, core):
    return 16 * (local // 4) + 8 * side + 2 * (local % 4) + core


def pack_kernel(inner, state, heads, rank_ref, in_ref, out_ref, keep_ref, give_ref):
    side, core = rank_ref[0], rank_ref[1]
    shared = 2 * state
    for target, of_side in ((keep_ref, side), (give_ref, 1 - side)):
        for group in range(2):
            for at in range(inner // LANES):
                even, odd = head_blocks(inner, group, at, of_side)
                lanes = slice(inner * group + LANES * at, inner * group + LANES * (at + 1))
                target[:, lanes] = halves(
                    core, in_ref[:, even].astype(f32), in_ref[:, odd].astype(f32)
                ).astype(bf16)
        target[:, 2 * inner : 2 * inner + shared] = in_ref[:, 8 * inner : 8 * inner + shared]
        shape = (4 * heads, LANES)
        local = iota(shape, 1)
        pick = (local < heads) & (iota(shape, 0) == head_number(local, of_side, core))
        steps = low_dot(in_ref[:, 8 * inner + shared :], pick.astype(f32))
        target[:, 2 * inner + shared : 2 * inner + shared + LANES] = steps.astype(bf16)
    rows = keep_ref.shape[0]
    lower, upper = out_ref[:rows].astype(f32), out_ref[rows:].astype(f32)
    keep_ref[:, 2 * inner + shared + LANES :] = jnp.where(core == 0, lower, upper).astype(bf16)


def prepare_kernel(
    inner, state, heads, head_dim,
    rank_ref, cw_in, cb_in, gate_in, norm_in, dt_in, alog_in, skip_in,
    cw_ref, cb_ref, gate_ref, norm_ref, heads_ref, skip_ref,
):
    side, core = rank_ref[0], rank_ref[1]

    def chosen(get):
        low, high = (halves(core, get(4 * of_side), get(4 * of_side + 1)) for of_side in range(2))
        return jnp.where(side == 0, low, high)

    for at in range(inner // LANES):
        first = 8 * (at // 2) + 2 * (at % 2)
        lanes = slice(LANES * at, LANES * (at + 1))
        cw_ref[:, lanes] = chosen(lambda b: cw_in[:, LANES * (first + b) : LANES * (first + b + 1)])
        cb_ref[:, lanes] = chosen(lambda b: cb_in[first + b : first + b + 1, :])
        gate_ref[:, lanes] = chosen(lambda b: gate_in[first + b : first + b + 1, :])
    cw_ref[:, inner:] = cw_in[:, 4 * inner :]
    for at in range(2 * state // LANES):
        row = 4 * inner // LANES + at
        cb_ref[:, inner + LANES * at : inner + LANES * (at + 1)] = cb_in[row : row + 1, :]
    for row in range(norm_in.shape[0]):
        norm_ref[:, LANES * row : LANES * (row + 1)] = norm_in[row : row + 1, :]
    shape = (4 * heads, LANES)
    local = iota(shape, 1)
    pick = ((local < heads) & (iota(shape, 0) == head_number(local, side, core))).astype(f32)
    rows = jnp.concatenate([dt_in[...], alog_in[...], skip_in[...], jnp.zeros((5, 4 * heads), f32)], axis=0)
    own = exact_dot(rows, pick)
    heads_ref[...] = own
    spread = (iota((LANES, inner), 1) // head_dim == iota((LANES, inner), 0)).astype(f32)
    skip_ref[...] = exact_dot(own, spread)[2:3]


def unpack_kernel(
    inner, state, heads, model, taps,
    rank_ref, mine_ref, other_ref, small_mine_ref, small_other_ref,
    in_ref, out_ref, conv_ref, bias_ref, gate_ref, gain_ref, *head_refs,
):
    side, core = rank_ref[0], rank_ref[1]
    width = 2 * inner + 2 * state + LANES
    shared = 2 * state

    def both(start, end):
        mine, other = mine_ref[:, start:end], other_ref[:, start:end]
        return jnp.where(core == 0, mine, other), jnp.where(core == 0, other, mine)

    tails = [None, None]
    for offset, of_side in ((0, side), (width + model, 1 - side)):
        for group in range(2):
            for at in range(inner // LANES):
                start = offset + inner * group + LANES * at
                first, second = both(start, start + LANES)
                even, odd = head_blocks(inner, group, at, of_side)
                in_ref[:, even] = halves(0, first, second)
                in_ref[:, odd] = halves(1, first, second)
        start = offset + 2 * inner
        first, second = both(start, start + shared)
        keys = first + second
        start += shared
        first, second = both(start, start + LANES)
        row, col = iota((LANES, LANES), 0), iota((LANES, LANES), 1)
        steps = exact_dot(
            first, ((row < heads) & (col == head_number(row, of_side, 0))).astype(f32)
        ) + exact_dot(second, ((row < heads) & (col == head_number(row, of_side, 1))).astype(f32))
        tails[0 if offset == 0 else 1] = (keys, steps)
    in_ref[:, 8 * inner : 8 * inner + shared] = tails[0][0] + tails[1][0]
    in_ref[:, 8 * inner + shared :] = (tails[0][1] + tails[1][1])[:, : 4 * heads]
    rows = mine_ref.shape[0]
    first, second = both(width, width + model)
    out_ref[:rows, :] = first
    out_ref[rows:, :] = second

    def small_both(start, end):
        mine, other = small_mine_ref[:, start:end], small_other_ref[:, start:end]
        return jnp.where(core == 0, mine, other), jnp.where(core == 0, other, mine)

    row, col = iota((LANES, LANES), 0), iota((LANES, LANES), 1)
    small_width = small_mine_ref.shape[1] // 2
    for of_side in range(2):
        offset = small_width * jnp.where(side == of_side, 0, 1)
        for at in range(inner // LANES):
            lanes = pl.ds(pl.multiple_of(offset + LANES * at, LANES), LANES)
            mine, other = small_mine_ref[:, lanes], small_other_ref[:, lanes]
            first, second = jnp.where(core == 0, mine, other), jnp.where(core == 0, other, mine)
            place = 8 * (at // 2) + 4 * of_side + 2 * (at % 2)
            for step in range(2):
                block = halves(step, first, second)
                conv_ref[:, LANES * (place + step) : LANES * (place + step + 1)] = block[:taps]
                bias_ref[place + step : place + step + 1, :] = block[taps : taps + 1]
                gate_ref[place + step : place + step + 1, :] = block[taps + 1 : taps + 2]
    shared_blocks = []
    for at in range(inner // LANES, small_width // LANES):
        sides = []
        for of_side in range(2):
            start = small_width * of_side + LANES * at
            first, second = small_both(start, start + LANES)
            sides.append(first + second)
        shared_blocks.append(sides[0] + sides[1])
    for at, block in enumerate(shared_blocks[: shared // LANES]):
        place = 4 * inner // LANES + at
        conv_ref[:, LANES * place : LANES * (place + 1)] = block[:taps]
        bias_ref[place : place + 1, :] = block[taps : taps + 1]
    gain_ref[...] = shared_blocks[shared // LANES]
    scatter_sides = (side, 1 - side)
    for kind in range(3):
        total = jnp.zeros((8, LANES), f32)
        for at, of_side in enumerate(scatter_sides):
            start = small_width * at + LANES * kind
            first, second = small_both(start, start + LANES)
            for of_core, part in enumerate((first, second)):
                pick = (row < heads) & (col == head_number(row, of_side, of_core))
                total = total + exact_dot(part, pick.astype(f32))
        head_refs[kind][...] = total[taps + 2 : taps + 3, : 4 * heads]


def silu_parts(v):
    sig = 1.0 / (1.0 + jnp.exp(-v))
    return sig, v * sig


def conv_block(proj_ref, masks_ref, cw_ref, cb_ref, inner, at):
    signal = proj_ref[:, pl.ds(pl.multiple_of(inner + at * LANES, LANES), LANES)]
    lanes = pl.ds(pl.multiple_of(at * LANES, LANES), LANES)
    taps = cw_ref.shape[0]
    mixed = cb_ref[:, lanes] + cw_ref[taps - 1 : taps, lanes] * signal
    for offset in range(1, taps):
        earlier = pltpu.roll(signal, offset, 0) * masks_ref[offset - 1]
        mixed = mixed + cw_ref[taps - 1 - offset : taps - offset, lanes] * earlier
    return signal, mixed


def decay_prep(proj_ref, heads_ref, inner, head_dim, stepe_ref, cume_ref, cumt_ref):
    tokens, width = proj_ref.shape
    raw = proj_ref[:, width - LANES :] + heads_ref[0:1, :]
    step = jnp.maximum(raw, 0.0) + jnp.log1p(jnp.exp(-jnp.abs(raw)))
    decay = -step * jnp.exp(heads_ref[1:2, :])
    lower = (iota((LANES, LANES), 0) >= iota((LANES, LANES), 1)).astype(f32)
    spread = (
        iota((LANES, inner), 1) // head_dim == iota((LANES, inner), 0)
    ).astype(f32)
    stepe_ref[...] = exact_dot(step, spread)
    for seq in range(tokens // LANES):
        rows = slice(seq * LANES, (seq + 1) * LANES)
        cumul = exact_dot(lower, decay[rows])
        cume_ref[rows, :] = exact_dot(cumul, spread)
        turned = cumul.T
        for pair in range(inner // LANES):
            cumt_ref[pair, 0:2, rows] = turned[2 * pair : 2 * pair + 2]
    return raw, step, decay


def pair_weights(cume_ref, cumt_ref, vis_ref, rows, lanes, pair, half):
    cols = cume_ref[rows, lanes]
    seen = vis_ref[rows, :] > 0.5
    first, second = cumt_ref[pair, 0:1, rows], cumt_ref[pair, 1:2, rows]
    fade_a = jnp.exp(jnp.where(seen, cols[:, 0:1] - first, -1e30))
    fade_b = jnp.exp(jnp.where(seen, cols[:, half : half + 1] - second, -1e30))
    return fade_a, fade_b


def split_heads(block, half):
    lane = iota(block.shape, 1)
    return jnp.concatenate(
        [jnp.where(lane < half, block, 0.0), jnp.where(lane >= half, block, 0.0)], axis=0
    )


def forward_kernel(
    places, in_count, out_count, inner, head_dim,
    rank_ref, gain_ref, gate_gain_ref, cw_ref, cb_ref, heads_ref, skip_ref, *rest,
):
    token_count = 1 + max(ref for ref, _ in places)
    token_rows, rest = rest[:token_count], rest[token_count:]
    in_chunks, out_chunks = rest[:in_count], rest[in_count : in_count + out_count]
    (sums_ref, normed_out, proj_out, mixer_out, dgated_out,
     normed_ref, proj_ref, mixer_ref, dgated_ref, w_ref, w_out_ref, act_ref, stepe_ref, cume_ref,
     cumt_ref, score_ref, sq_ref, cross_ref, masks_ref, vis_ref, tok_ref, cot_ref, seg_ref,
     in_sems, out_sems, store_sems, token_sems) = (
        rest[in_count + out_count :]
    )
    count = len(places)
    tokens_in = token_copies(places, token_rows, tok_ref, 0, LANES, token_sems)
    tokens_in += token_copies(places, token_rows, seg_ref, 2 * LANES, 16, token_sems, count)
    cot_in = token_copies(places, token_rows, cot_ref, LANES, LANES, token_sems, 2 * count)
    copies = in_copies(rank_ref, in_chunks, w_ref, in_sems)
    copies += out_copies(rank_ref, out_chunks, w_out_ref, out_sems)
    for copy in copies:
        copy.start()
    for copy in tokens_in:
        copy.wait()
    hidden = tok_ref[...].astype(f32)
    factor = lax.rsqrt(jnp.mean(hidden * hidden, axis=-1, keepdims=True) + epsilon)
    normed_ref[...] = (hidden * factor * gain_ref[...]).astype(bf16)
    stores = [started(normed_ref, normed_out, store_sems.at[0])]
    spread_marks(seg_ref, masks_ref, vis_ref)
    for copy in copies + cot_in:
        copy.wait()
    tokens, width = proj_ref.shape
    for start in range(0, width, 512):
        end = min(start + 512, width)
        proj_ref[:, start:end] = jnp.dot(
            normed_ref[...], w_ref[:, start:end], preferred_element_type=f32
        )
    for start in range(0, inner, 256):
        lanes = slice(start, start + 256)
        dgated_ref[:, lanes] = low_dot(cot_ref[...], w_out_ref[lanes, :], ((1,), (1,)))
    stores.append(started(proj_ref, proj_out, store_sems.at[1]))
    stores.append(started(dgated_ref, dgated_out, store_sems.at[2]))
    decay_prep(proj_ref, heads_ref, inner, head_dim, stepe_ref, cume_ref, cumt_ref)

    def convolve(at, _):
        signal, mixed = conv_block(proj_ref, masks_ref, cw_ref, cb_ref, inner, at)
        act_ref[:, pl.ds(pl.multiple_of(at * LANES, LANES), LANES)] = silu_parts(mixed)[1]
        return 0

    lax.fori_loop(0, act_ref.shape[1] // LANES, convolve, 0)
    seqs = tokens // LANES
    for seq in range(seqs):
        rows = slice(seq * LANES, (seq + 1) * LANES)
        keys = act_ref[rows, inner : inner + LANES]
        queries = act_ref[rows, inner + LANES :]
        score_ref[rows, :] = exact_dot(queries, keys, ((1,), (1,)))
    sq_ref[...] = jnp.zeros_like(sq_ref)
    cross_ref[...] = jnp.zeros_like(cross_ref)

    def scan(pair, _):
        lanes = pl.ds(pl.multiple_of(pair * LANES, LANES), LANES)
        skip = skip_ref[:, lanes]
        for seq in range(seqs):
            rows = slice(seq * LANES, (seq + 1) * LANES)
            fade_a, fade_b = pair_weights(cume_ref, cumt_ref, vis_ref, rows, lanes, pair, head_dim)
            score = score_ref[rows, :]
            weights = jnp.concatenate([fade_a * score, fade_b * score], axis=1)
            values = act_ref[rows, lanes]
            scaled = split_heads(values * stepe_ref[rows, lanes], head_dim)
            mixed = low_dot(weights, scaled) + skip * values
            mixer_ref[rows, lanes] = mixed
            product = mixed * silu_parts(proj_ref[rows, lanes])[1]
            sq_ref[rows, :] += product * product
            cross_ref[rows, :] += product * gate_gain_ref[:, lanes] * dgated_ref[rows, lanes]
        return 0

    lax.fori_loop(0, inner // LANES, scan, 0)
    stores.append(started(mixer_ref, mixer_out, store_sems.at[3]))
    for seq in range(seqs):
        rows = slice(seq * LANES, (seq + 1) * LANES)
        sums_ref[seq : seq + 1, :] = jnp.sum(sq_ref[rows, :].T, axis=0, keepdims=True)
        at = seqs + seq
        sums_ref[at : at + 1, :] = jnp.sum(cross_ref[rows, :].T, axis=0, keepdims=True)
    for copy in stores:
        copy.wait()


def gated_kernel(
    places, chunk_count, grad_count, inner, full_inner,
    rank_ref, sums_ref, gain_ref, proj_in, mixer_in, *rest,
):
    token_count = 1 + max(ref for ref, _ in places)
    token_rows, rest = rest[:token_count], rest[token_count:]
    chunks = rest[:chunk_count]
    close_ref, away_ref = rest[chunk_count : chunk_count + 2]
    grads = rest[chunk_count + 2 : chunk_count + 2 + grad_count]
    (proj_ref, mixer_ref, gated_ref, factor_ref, w_out_ref, grad_ref, cot_ref, sems, grad_sems, load_sems,
     token_sems) = (
        rest[chunk_count + 2 + grad_count :]
    )
    loads = [
        started(proj_in.at[:, pl.ds(0, inner)], proj_ref, load_sems.at[0]),
        started(mixer_in, mixer_ref, load_sems.at[1]),
    ]
    loads += token_copies(places, token_rows, cot_ref, LANES, LANES, token_sems)
    weights = out_copies(rank_ref, chunks, w_out_ref, sems)
    for copy in weights:
        copy.start()
    tokens = proj_ref.shape[0]
    seqs = tokens // LANES
    for seq in range(seqs):
        row = lax.rsqrt(sums_ref[seq : seq + 1, :] / full_inner + epsilon)
        factor_ref[seq * LANES : (seq + 1) * LANES, :] = jnp.broadcast_to(row, (LANES, LANES)).T
    for copy in loads:
        copy.wait()
    for start in range(0, inner, LANES):
        lanes = slice(start, start + LANES)
        product = mixer_ref[:, lanes] * silu_parts(proj_ref[:, lanes])[1]
        gated_ref[:, lanes] = (product * factor_ref[...] * gain_ref[:, lanes]).astype(bf16)
    for start in range(0, inner, 256):
        lanes = slice(start, start + 256)
        grad_ref[lanes, :] = low_dot(gated_ref[:, lanes], cot_ref[...], ((0,), (0,))).astype(bf16)
    copies = out_grad_copies(rank_ref, grads, grad_ref, grad_sems)
    for copy in copies:
        copy.start()
    for copy in weights:
        copy.wait()
    half = tokens // 2
    close_ref[...] = jnp.dot(gated_ref[:half, :], w_out_ref[...], preferred_element_type=f32)
    away = jnp.dot(gated_ref[half:, :], w_out_ref[...], preferred_element_type=f32)
    away_ref[...] = away.astype(bf16)
    for copy in copies:
        copy.wait()


def backward_kernel(
    places, weight_count, chunk_count, inner, head_dim, full_inner,
    rank_ref, sums_ref, gain_ref, cw_ref, cb_ref, heads_ref, skip_ref,
    normed_in, proj_in, mixer_in, dgated_in, *rest,
):
    token_count = 1 + max(ref for ref, _ in places)
    token_rows, rest = rest[:token_count], rest[token_count:]
    weight_chunks = rest[:weight_count]
    rest = rest[weight_count:]
    close_ref, away_ref, small_ref, coded_ref = rest[:4]
    chunks = rest[4 : 4 + chunk_count]
    (normed_ref, proj_ref, mixer_ref, dgated_ref, masks_ref, vis_ref, dact_ref,
     act_ref, stepe_ref, cume_ref, cumt_ref, score_ref, dscore_ref, dstep_ref,
     rowsum_ref, colsum_ref, turned_ref, dskip_ref, factor_ref, pull_ref, turned_normed_ref, grad_ref,
     w_ref, dproj_ref, tok_ref, seg_ref, carried_ref, weight_sems, sems, load_sems, token_sems) = (
        rest[4 + chunk_count :]
    )
    seg_in = token_copies(places, token_rows, seg_ref, 2 * LANES, 16, token_sems)
    loads = [
        started(source, target, load_sems.at[at])
        for at, (source, target) in enumerate(
            ((proj_in, proj_ref), (mixer_in, mixer_ref), (dgated_in, dgated_ref), (normed_in, normed_ref))
        )
    ]
    weights = in_copies(rank_ref, weight_chunks, w_ref, weight_sems)
    for copy in weights:
        copy.start()
    weights += token_copies(places, token_rows, tok_ref, 0, LANES, token_sems, len(places))
    for copy in seg_in:
        copy.wait()
    spread_marks(seg_ref, masks_ref, vis_ref)
    loads[0].wait()
    tokens, width = proj_ref.shape
    seqs = tokens // LANES
    raw, step, decay = decay_prep(
        proj_ref, heads_ref, inner, head_dim, stepe_ref, cume_ref, cumt_ref
    )
    small_ref[...] = jnp.zeros_like(small_ref)

    def convolve(at, _):
        signal, mixed = conv_block(proj_ref, masks_ref, cw_ref, cb_ref, inner, at)
        act_ref[:, pl.ds(pl.multiple_of(at * LANES, LANES), LANES)] = silu_parts(mixed)[1]
        return 0

    lax.fori_loop(0, act_ref.shape[1] // LANES, convolve, 0)
    for seq in range(seqs):
        rows = slice(seq * LANES, (seq + 1) * LANES)
        keys = act_ref[rows, inner : inner + LANES]
        queries = act_ref[rows, inner + LANES :]
        score_ref[rows, :] = exact_dot(queries, keys, ((1,), (1,)))
    dscore_ref[...] = jnp.zeros_like(dscore_ref)
    dstep_ref[...] = jnp.zeros_like(dstep_ref)
    rowsum_ref[...] = jnp.zeros_like(rowsum_ref)
    turned_ref[...] = jnp.zeros_like(turned_ref)
    dskip_ref[...] = jnp.zeros_like(dskip_ref)
    for seq in range(seqs):
        rows = slice(seq * LANES, (seq + 1) * LANES)
        row = lax.rsqrt(sums_ref[seq : seq + 1, :] / full_inner + epsilon)
        pulled = row * row * row * sums_ref[seqs + seq : seqs + seq + 1, :] / full_inner
        factor_ref[rows, :] = jnp.broadcast_to(row, (LANES, LANES)).T
        pull_ref[rows, :] = jnp.broadcast_to(pulled, (LANES, LANES)).T

    def scan(pair, _):
        lanes = pl.ds(pl.multiple_of(pair * LANES, LANES), LANES)
        skip = skip_ref[:, lanes]
        gain = gain_ref[:, lanes]
        collect = (
            iota((LANES, LANES), 0) // head_dim + 2 * pair == iota((LANES, LANES), 1)
        ).astype(f32)
        dgain = jnp.zeros((1, LANES), f32)
        dskip = jnp.zeros((1, LANES), f32)
        for seq in range(seqs):
            rows = slice(seq * LANES, (seq + 1) * LANES)
            gate = proj_ref[rows, lanes]
            sig, gate_act = silu_parts(gate)
            mixed = mixer_ref[rows, lanes]
            product = mixed * gate_act
            dgated = dgated_ref[rows, lanes]
            factor = factor_ref[rows, :]
            dproduct = factor * gain * dgated - product * pull_ref[rows, :]
            dgain = dgain + jnp.sum(dgated * product * factor, axis=0, keepdims=True)
            dgate = dproduct * mixed * (sig * (1.0 + gate * (1.0 - sig)))
            dproj_ref[rows, lanes] = dgate.astype(bf16)
            dmixed = dproduct * gate_act
            values = act_ref[rows, lanes]
            stepe = stepe_ref[rows, lanes]
            dskip = dskip + jnp.sum(dmixed * values, axis=0, keepdims=True)
            fade_a, fade_b = pair_weights(cume_ref, cumt_ref, vis_ref, rows, lanes, pair, head_dim)
            score = score_ref[rows, :]
            weights_a, weights_b = fade_a * score, fade_b * score
            dsplit = split_heads(dmixed, head_dim)
            dweights = low_dot(dsplit, values * stepe, ((1,), (1,)))
            dweights_a, dweights_b = dweights[:LANES], dweights[LANES:]
            dscore_ref[rows, :] += dweights_a * fade_a + dweights_b * fade_b
            spread_a, spread_b = dweights_a * weights_a, dweights_b * weights_b
            lane = iota((LANES, LANES), 1)
            rowsum_ref[rows, :] += jnp.where(
                lane == 2 * pair,
                jnp.sum(spread_a, axis=1, keepdims=True),
                jnp.where(lane == 2 * pair + 1, jnp.sum(spread_b, axis=1, keepdims=True), 0.0),
            )
            colsum_ref[pair, 0:1, rows] = jnp.sum(spread_a, axis=0, keepdims=True)
            colsum_ref[pair, 1:2, rows] = jnp.sum(spread_b, axis=0, keepdims=True)
            weights = jnp.concatenate([weights_a, weights_b], axis=0)
            dscaled = low_dot(weights, dsplit, ((0,), (0,)))
            dact_ref[rows, lanes] = dscaled * stepe + skip * dmixed
            dstep_ref[rows, :] += exact_dot(dscaled * values, collect)
        small_ref[5:6, lanes] = dgain
        dskip_ref[0:1, lanes] = dskip
        return 0

    for copy in loads[1:]:
        copy.wait()
    lax.fori_loop(0, inner // LANES, scan, 0)
    for pair in range(inner // LANES):
        turned_ref[2 * pair : 2 * pair + 2, :] = colsum_ref[pair, 0:2, :]
    upper = (iota((LANES, LANES), 0) <= iota((LANES, LANES), 1)).astype(f32)
    rate = jnp.exp(heads_ref[1:2, :])
    ddt = jnp.zeros((1, LANES), f32)
    dalog = jnp.zeros((1, LANES), f32)
    for seq in range(seqs):
        rows = slice(seq * LANES, (seq + 1) * LANES)
        keys = act_ref[rows, inner : inner + LANES]
        queries = act_ref[rows, inner + LANES :]
        dscore = dscore_ref[rows, :]
        dact_ref[rows, inner : inner + LANES] = exact_dot(dscore, queries, ((0,), (0,)))
        dact_ref[rows, inner + LANES :] = exact_dot(dscore, keys)
        dcumul = rowsum_ref[rows, :] - turned_ref[:, rows].T
        ddecay = exact_dot(upper, dcumul)
        dalog = dalog + jnp.sum(ddecay * decay[rows], axis=0, keepdims=True)
        dstep = dstep_ref[rows, :] - ddecay * rate
        draw = dstep / (1.0 + jnp.exp(-raw[rows]))
        ddt = ddt + jnp.sum(draw, axis=0, keepdims=True)
        dproj_ref[rows, width - LANES :] = draw.astype(bf16)
    gather = (
        iota((inner, LANES), 0) // head_dim == iota((inner, LANES), 1)
    ).astype(f32)
    dskip_heads = exact_dot(dskip_ref[...], gather)
    small_ref[6:7, 0:LANES] = ddt
    small_ref[6:7, LANES : 2 * LANES] = dalog
    small_ref[6:7, 2 * LANES : 3 * LANES] = dskip_heads[0:1]

    def convolve_back(at, _):
        lanes = pl.ds(pl.multiple_of(at * LANES, LANES), LANES)
        signal, mixed = conv_block(proj_ref, masks_ref, cw_ref, cb_ref, inner, at)
        sig, _unused = silu_parts(mixed)
        dmixed = dact_ref[:, lanes] * (sig * (1.0 + mixed * (1.0 - sig)))
        taps = cw_ref.shape[0]
        small_ref[taps : taps + 1, lanes] = jnp.sum(dmixed, axis=0, keepdims=True)
        small_ref[taps - 1 : taps, lanes] = jnp.sum(dmixed * signal, axis=0, keepdims=True)
        dsignal = cw_ref[taps - 1 : taps, lanes] * dmixed
        for offset in range(1, taps):
            masked = dmixed * masks_ref[offset - 1]
            place = taps - 1 - offset
            small_ref[place : place + 1, lanes] = jnp.sum(
                masked * pltpu.roll(signal, offset, 0), axis=0, keepdims=True
            )
            dsignal = dsignal + cw_ref[place : place + 1, lanes] * pltpu.roll(
                masked, tokens - offset, 0
            )
        dproj_ref[:, pl.ds(pl.multiple_of(inner + at * LANES, LANES), LANES)] = dsignal.astype(bf16)
        return 0

    lax.fori_loop(0, dact_ref.shape[1] // LANES, convolve_back, 0)
    for seq in range(seqs):
        rows = slice(seq * LANES, (seq + 1) * LANES)
        turned_normed_ref[:, rows] = normed_ref[rows, :].astype(f32).T.astype(bf16)
    for start in range(0, width, 512):
        lanes = slice(start, min(start + 512, width))
        grad_ref[:, lanes] = low_dot(turned_normed_ref[...], dproj_ref[:, lanes]).astype(bf16)
    copies = in_grad_copies(rank_ref, chunks, grad_ref, sems)
    for copy in copies:
        copy.start()
    for copy in weights:
        copy.wait()
    model = w_ref.shape[0]
    hidden = tok_ref[...].astype(f32)
    token_factor = lax.rsqrt(jnp.mean(hidden * hidden, axis=-1, keepdims=True) + epsilon)
    conv_width = dact_ref.shape[1]
    part = model // 8
    for start in range(0, model, 256):
        lanes = slice(start, start + 256)
        dnormed = low_dot(dproj_ref[...], w_ref[lanes, :], ((1,), (1,)))
        half = tokens // 2
        close_ref[:, lanes] = dnormed[:half]
        away_ref[:, lanes] = dnormed[half:].astype(bf16)
        dgain = jnp.sum(dnormed * hidden[:, lanes] * token_factor, axis=0, keepdims=True)
        for at in range(0, 256, part):
            row = (start + at) // part
            small_ref[row : row + 1, conv_width:] = dgain[:, at : at + part]
    high = small_ref[...].astype(bf16)
    low = small_ref[...] - high.astype(f32)
    coded_ref[...] = jnp.concatenate([high.astype(f32), low], axis=0).astype(bf16)
    if chunk_count > 1:
        carried_ref[...] = jnp.zeros_like(carried_ref)
        carried_ref[:, : coded_ref.shape[1]] = coded_ref[...]
        held = chunks[2].at[pl.ds(chunks[2].shape[0] - 16, 16)]
        copies.append(started(carried_ref, held, token_sems.at[2 * len(places)]))
    for copy in copies:
        copy.wait()


def tail_kernel(tok_ref, cot_ref, gain_ref, mine_ref, other_ref, dtok_ref):
    hidden = tok_ref[...].astype(f32)
    factor = lax.rsqrt(jnp.mean(hidden * hidden, axis=-1, keepdims=True) + epsilon)
    dnormed = mine_ref[...] + other_ref[...]
    scaled = dnormed * gain_ref[...]
    pull = jnp.mean(scaled * hidden, axis=-1, keepdims=True) * factor * factor * factor
    dtok_ref[...] = cot_ref[...].astype(f32) + scaled * factor - hidden * pull


def after(x, *others):
    return lax.optimization_barrier((x, *others))[0]


class Links:
    first, second = (1, 2), (2, 1)
    slots = (0, 4, 8, 12)

    def __init__(self, reps, chips, paired):
        self.reps, self.chips, self.paired = reps, chips, paired
        self.rep = lax.axis_index("rep")
        self.chip = lax.axis_index("fsdp")
        self.side = self.chip // 4 % 2

    def exchange(self, x, masks):
        if isinstance(masks, int):
            masks = (masks, masks)
        pairs = [
            (core * self.chips + chip, core * self.chips + (chip ^ masks[core]))
            for core in range(self.reps)
            for chip in range(self.chips)
        ]
        return lax.ppermute(x, BOTH, pairs)

    def swap(self, x):
        return lax.ppermute(x, "rep", [(0, 1), (1, 0)])

    def spread(self, block):
        near = self.exchange(block, self.first)
        side = self.exchange(block, self.second)
        return [block, near, side, self.exchange(near, self.second)]

    def gather(self, keep, give):
        beside, across = self.exchange(give, self.slots[1]), self.exchange(keep, self.slots[2])
        own, near = self.spread(keep), self.spread(beside)
        far = self.exchange(after(give, beside), self.slots[3])
        return [own, near, self.spread(after(across, *own[2:], near[2])), self.spread(after(far, near[3]))]

    def square_with(self, own, near, send, small, earlier):
        rows, width = own.shape
        count = small.shape[0] // 2

        def decoded(x):
            x = x[-2 * count :, : small.shape[1]].astype(f32)
            return x[:count] + x[count:]

        came = self.exchange(send, self.second)
        near = (near.astype(f32) + came[rows : 2 * rows].astype(f32)).astype(bf16)
        near = after(near, earlier)
        total = decoded(small) + decoded(came)
        high = lax.reduce_precision(total, 8, 7)
        coded = jnp.concatenate([high, total - high]).astype(bf16)
        ride = jnp.pad(coded, ((0, 0), (0, width - small.shape[1])))
        last = self.exchange(jnp.concatenate([near, ride]), self.first)
        total = decoded(coded) + decoded(last)
        return own.astype(f32) + came[:rows].astype(f32) + last[:rows].astype(f32), total, came

    def square_at_once(self, own, near, side, far):
        moved = [self.exchange(near, self.first), self.exchange(side, self.second), self.exchange(far, 3)]
        return sum((x.astype(f32) for x in moved), own.astype(f32)), moved

    def across(self, x):
        return self.exchange(x.astype(bf16), self.slots[2])

    def beside(self, x):
        return self.exchange(x.astype(bf16), self.slots[1]).astype(f32)

    def square_second(self, own, near, came, meanwhile):
        rows = own.shape[0]
        near = (near.astype(f32) + came[rows:].astype(f32)).astype(bf16)
        near = self.exchange(after(near, *meanwhile), self.first)
        return own.astype(f32) + came[:rows].astype(f32) + near.astype(f32)

    def sum_lines(self, x):
        same, beside, other = (self.exchange(x, slot) for slot in (8, 4, 12))
        return jnp.concatenate([x + same, beside + other], axis=1)

    def group_rows(self, x, others):
        other = after(self.exchange(x, self.slots[1]), *others)
        return [x, self.swap(jnp.concatenate([x, other])), other]

    def from_reps(self, x):
        whole = lax.all_gather(x, "rep", axis=0)
        return [whole[at] for at in range(self.reps)]

    def sum_group(self, x):
        if not self.paired:
            return lax.psum(x, "rep")

        def reordered(y, bit):
            return jnp.concatenate([y[at ^ bit : (at ^ bit) + 1] for at in range(y.shape[0])])

        x = x + reordered(self.exchange(x, self.slots[1]), 2)
        return x + reordered(self.swap(x), 1)

    def from_side(self, x):
        return self.exchange(x, self.slots[1])

    def own_rows(self, x, came):
        rows = x.shape[0] // 2
        came = came.astype(f32)
        return x[:rows] + came[:rows], self.swap(x[rows:] + came[rows:])

    def scattered(self, close, away):
        x = jnp.concatenate([close, away.astype(f32)])
        mine = lax.psum_scatter(x, "rep", scatter_dimension=0, tiled=True)
        return mine, jnp.zeros_like(mine)


def per_device(
    reps, chips,
    tokens, segment_ids, norm_gain, in_weight, conv_weight, conv_bias, dt_bias, a_log, skip_gain,
    gate_gain, out_weight, cotangent,
):
    full_inner, full_heads = gate_gain.shape[0], dt_bias.shape[0]
    conv_dim, taps = conv_bias.shape[0], conv_weight.shape[0]
    model = norm_gain.shape[0]
    state = (conv_dim - full_inner) // 2
    head_dim = full_inner // full_heads
    rows_in, rows_out = in_weight.shape[0], out_weight.shape[0]
    paired = (reps, chips, full_heads) == (2, 16, 32) and rows_out == 2 * rows_in == 2 * head_dim
    ranks = 4 if paired else reps
    inner, heads = full_inner // ranks, full_heads // ranks
    links = Links(reps, chips, paired)
    rep, chip = links.rep, links.chip
    conv_local = inner + 2 * state
    width = inner + conv_local + LANES
    own_tokens = tokens.shape[0]
    total = own_tokens * ranks

    def arr(*shape, dtype=f32):
        return jax.ShapeDtypeStruct(shape, dtype)

    def vmem(*shape, dtype=f32):
        return pltpu.VMEM(shape, dtype)

    def own_heads(x, size):
        lead = x.shape[:-1]
        if paired:
            split = x.reshape(lead + (2, 2, 4, 2, size))
            split = lax.dynamic_index_in_dim(split, links.side, split.ndim - 4, False)
        else:
            split = x.reshape(lead + (heads, reps, size))
        split = lax.dynamic_index_in_dim(split, rep, split.ndim - 2, False)
        return split.reshape(lead + (heads * size,))

    def all_heads(parts, size):
        lead = parts[0].shape[:-1]
        if paired:
            split = [part.reshape(lead + (2, 1, 4, 1, size)) for part in parts]
            sides = [jnp.concatenate(split[at : at + 2], axis=-2) for at in (0, 2)]
            whole = jnp.concatenate(sides, axis=-4)
        else:
            whole = jnp.concatenate([part.reshape(lead + (heads, 1, size)) for part in parts], axis=-2)
        return whole.reshape(lead + (full_heads * size,))

    rank = jnp.stack([links.side, rep, chip]).astype(jnp.int32)
    if paired:
        keep, give = pl.pallas_call(
            functools.partial(pack_kernel, inner, state, heads),
            out_shape=[arr(rows_in, width + model, dtype=bf16), arr(rows_in, width, dtype=bf16)],
            in_specs=in_smem(1) + in_vmem(2),
            out_specs=in_vmem(2),
            compiler_params=params(),
            name="pack",
        )(rank, in_weight, out_weight)
        slots = links.gather(keep, give)
        first_rows = slots[1][0]
        conv_w, conv_b, gate_g, norm_g, head_rows, skip = pl.pallas_call(
            functools.partial(prepare_kernel, inner, state, heads, head_dim),
            out_shape=[
                arr(taps, conv_local), arr(1, conv_local), arr(1, inner), arr(1, model), arr(8, LANES),
                arr(1, inner),
            ],
            in_specs=in_smem(1) + in_vmem(7),
            out_specs=in_vmem(6),
            compiler_params=params(),
            name="prepare",
        )(rank, conv_weight, conv_bias.reshape(-1, LANES), gate_gain.reshape(-1, LANES),
          norm_gain.reshape(-1, LANES), dt_bias[None], a_log[None], skip_gain[None])
        in_chunks, out_chunks = sum(slots, []), slots[0] + slots[2]
        in_shapes = [(rows_in, 2 * width), (rows_in, 2 * width), (2 * rows_in, 2 * width)] * 2
        in_shapes[2] = (2 * rows_in + 16, 2 * width)
        out_shapes = [(2 * rows_in, model)] * 4
    else:
        in_full = lax.all_gather(in_weight, "fsdp", axis=0, tiled=True)
        out_full = lax.all_gather(out_weight, "fsdp", axis=0, tiled=True)
        ends = [full_inner, 2 * full_inner, full_inner + conv_dim]
        gates, signals, shared, step_cols = jnp.split(in_full, ends, axis=1)
        in_chunks = [
            jnp.concatenate(
                [own_heads(gates, head_dim), own_heads(signals, head_dim), shared, own_heads(step_cols, 1),
                 jnp.zeros((model, LANES - heads), bf16)],
                axis=1,
            )
        ]
        out_chunks = [own_heads(out_full.T, head_dim).T]
        def local_conv(x):
            return jnp.concatenate([own_heads(x[:, :full_inner], head_dim), x[:, full_inner:]], axis=1)

        conv_w, conv_b = local_conv(conv_weight), local_conv(conv_bias[None])

        def lane_row(x):
            return jnp.pad(own_heads(x, 1), (0, LANES - heads))

        head_rows = jnp.pad(jnp.stack([lane_row(dt_bias), lane_row(a_log)]), ((0, 6), (0, 0)))
        skip = jnp.repeat(own_heads(skip_gain, 1), head_dim)[None]
        gate_g = own_heads(gate_gain, head_dim)[None]
        norm_g = norm_gain[None]
        in_shapes, out_shapes = [(model, width)], [(inner, model)]
    extra = jnp.pad(segment_ids.astype(bf16), ((0, 15), (0, model - segment_ids.shape[1])))
    own_rows = jnp.concatenate([tokens, cotangent, extra])
    held = own_rows.shape[0]
    if paired:
        own_rows = after(own_rows, first_rows)
        waits = slots[0][3:] + slots[1][1:3] + slots[2][1:3] + slots[3][:1]
        token_rows = links.group_rows(own_rows, waits)
        places = ((0, 0), (1, 0), (2, 0), (1, held))
    else:
        token_rows = links.from_reps(own_rows)
        places = tuple((at, 0) for at in range(reps))
    in_shapes = [arr(*shape, dtype=bf16) for shape in in_shapes]
    out_shapes = [arr(*shape, dtype=bf16) for shape in out_shapes]
    in_count, out_count = len(in_chunks), len(out_chunks)

    w_in, w_out = vmem(model, width, dtype=bf16), vmem(inner, model, dtype=bf16)
    in_sems, out_sems = (pltpu.SemaphoreType.DMA((n,)) for n in (in_count, out_count))
    def sems(n):
        return pltpu.SemaphoreType.DMA((n,))

    kept = [vmem(total, model, dtype=bf16), vmem(total, width), vmem(total, inner), vmem(total, inner)]
    tok, segs = vmem(total, model, dtype=bf16), vmem(16 * len(places), LANES, dtype=bf16)
    conv_masks = [vmem(taps - 1, total, LANES), vmem(total, LANES)]
    sums, normed, projected, mixed, d_gated = pl.pallas_call(
        functools.partial(forward_kernel, places, in_count, out_count, inner, head_dim),
        out_shape=[
            arr(2 * total // LANES, LANES), arr(total, model, dtype=bf16), arr(total, width),
            arr(total, inner), arr(total, inner),
        ],
        in_specs=in_smem(1) + in_vmem(6) + in_hbm(len(token_rows) + in_count + out_count),
        out_specs=in_vmem(1) + in_hbm(4),
        scratch_shapes=kept + [
            w_in, w_out,
            vmem(total, conv_local), vmem(total, inner), vmem(total, inner), vmem(inner // LANES, 8, total),
            vmem(total, LANES), vmem(total, LANES), vmem(total, LANES), *conv_masks,
            tok, tok, segs, in_sems, out_sems, sems(4), sems(3 * len(places)),
        ],
        compiler_params=params(),
        cost_estimate=cost(14),
        name="forward",
    )(rank, norm_g, gate_g, conv_w, conv_b, head_rows, skip, *token_rows, *in_chunks, *out_chunks)
    sums = links.sum_group(sums)
    block_close, block_away, *out_grads = pl.pallas_call(
        functools.partial(gated_kernel, places, out_count, len(out_shapes), inner, full_inner),
        out_shape=[arr(total // 2, model), arr(total // 2, model, dtype=bf16)] + out_shapes,
        in_specs=in_smem(1) + in_vmem(2) + in_hbm(2 + len(token_rows) + out_count),
        out_specs=in_vmem(2) + in_hbm(len(out_shapes)),
        scratch_shapes=[
            vmem(total, inner), vmem(total, inner), vmem(total, inner, dtype=bf16), vmem(total, LANES), w_out,
            vmem(inner, model, dtype=bf16), tok, out_sems, out_sems, sems(2), sems(len(places)),
        ],
        compiler_params=params(),
        cost_estimate=cost(6),
        name="gated",
    )(rank, sums, gate_g, projected, mixed, *token_rows, *out_chunks)
    if paired:
        out_sums, moved = links.square_at_once(*out_grads)
        sums = after(sums, out_grads[2])
        block_came = links.from_side(block_away)
    d_normed_close, d_normed_away, small, coded, *in_grads = pl.pallas_call(
        functools.partial(backward_kernel, places, in_count, len(in_shapes), inner, head_dim, full_inner),
        out_shape=[
            arr(total // 2, model), arr(total // 2, model, dtype=bf16),
            arr(8, conv_local + model // 8), arr(16, conv_local + model // 8, dtype=bf16),
        ] + in_shapes,
        in_specs=in_smem(1) + in_vmem(6) + in_hbm(4 + len(token_rows) + in_count),
        out_specs=in_vmem(4) + in_hbm(len(in_shapes)),
        scratch_shapes=kept + conv_masks + [
            vmem(total, conv_local),
            vmem(total, conv_local), vmem(total, inner), vmem(total, inner), vmem(inner // LANES, 8, total),
            vmem(total, LANES), vmem(total, LANES), vmem(total, LANES),
            vmem(total, LANES), vmem(inner // LANES, 8, total), vmem(LANES, total), vmem(8, inner),
            vmem(total, LANES), vmem(total, LANES), vmem(model, total, dtype=bf16), w_in, w_in,
            vmem(total, width, dtype=bf16), tok, segs, vmem(16, 2 * width, dtype=bf16), in_sems, in_sems, sems(4),
            sems(2 * len(places) + 1),
        ],
        compiler_params=params(),
        cost_estimate=cost(24),
        name="backward",
    )(rank, sums, gate_g, conv_w, conv_b, head_rows, skip, normed, projected, mixed, d_gated, *token_rows,
      *in_chunks)

    if paired:
        out_across = links.across(out_sums[rows_in:])
        far, small, came = links.square_with(
            *in_grads[:2], after(in_grads[2], block_came, *moved), coded, out_across
        )
        came = links.exchange(after(in_grads[5], came), links.second)
        far = links.across(far).astype(f32)
        small = links.sum_lines(after(small, came))
        small_other = links.swap(small)
        d_normed_parts = links.own_rows(d_normed_close, after(links.from_side(d_normed_away), came))
        block_parts = links.own_rows(block_close, block_came)
    else:
        out_sum, in_sum = (
            lax.psum_scatter(grads[0], "fsdp", scatter_dimension=0, tiled=True).astype(f32)
            for grads in (out_grads, in_grads)
        )
        smalls = links.from_reps(lax.psum(small, "fsdp"))
        d_normed_parts = links.scattered(d_normed_close, d_normed_away)
        block_parts = links.scattered(block_close, block_away)
    d_tokens = pl.pallas_call(
        tail_kernel,
        out_shape=arr(own_tokens, model),
        in_specs=in_vmem(5),
        out_specs=in_vmem(1)[0],
        compiler_params=params(8),
        cost_estimate=cost(2),
        name="tail",
    )(tokens, cotangent, norm_g, *d_normed_parts)
    block_out = (tokens.astype(f32) + (block_parts[0] + block_parts[1])).astype(bf16)

    if paired:
        close = links.square_second(*in_grads[3:5], came, [d_tokens, block_out])
        other = links.beside(after(close[:, width:] + far[:, width:], small_other))
        out_sum = out_sums[:rows_in] + out_across.astype(f32)
        grad_sum = jnp.concatenate([close[:, :width] + far[:, :width], out_sum, other], axis=1)
        d_in_weight, d_out_weight, d_conv_weight, d_conv_bias, d_gate_gain, d_norm_gain, *by_head = pl.pallas_call(
            functools.partial(unpack_kernel, inner, state, heads, model, taps),
            out_shape=[
                arr(*in_weight.shape), arr(*out_weight.shape), arr(taps, conv_dim), arr(conv_dim // LANES, LANES),
                arr(full_inner // LANES, LANES), arr(8, model // 8), *[arr(1, full_heads)] * 3,
            ],
            in_specs=in_smem(1) + in_vmem(4),
            out_specs=in_vmem(9),
            compiler_params=params(8),
            name="unpack",
        )(rank, grad_sum, links.swap(grad_sum), small, small_other)
        d_conv_bias, d_gate_gain, d_norm_gain = (x.reshape(-1) for x in (d_conv_bias, d_gate_gain, d_norm_gain))
        d_dt_bias, d_a_log, d_skip_gain = (x.reshape(-1) for x in by_head)
    else:
        parts = [part[:, :inner] for part in smalls]
        shared = sum(part[:, inner:] for part in smalls)
        d_norm_gain = shared[:, 2 * state :].reshape(-1)
        d_conv = jnp.concatenate([all_heads(parts, head_dim), shared[:, : 2 * state]], axis=1)
        d_conv_weight, d_conv_bias = d_conv[:taps], d_conv[taps]
        d_gate_gain = d_conv[taps + 1, :full_inner]
        d_dt_bias, d_a_log, d_skip_gain = (
            all_heads([part[taps + 2, at * LANES : at * LANES + heads] for part in parts], 1) for at in range(3)
        )
        in_parts = links.from_reps(in_sum)
        mid = 2 * inner
        end = mid + 2 * state
        d_in_weight = jnp.concatenate(
            [
                all_heads([part[:, :inner] for part in in_parts], head_dim),
                all_heads([part[:, inner:mid] for part in in_parts], head_dim),
                sum(part[:, mid:end] for part in in_parts),
                all_heads([part[:, end : end + heads] for part in in_parts], 1),
            ],
            axis=1,
        )
        held = links.from_reps(lax.all_gather(out_sum, "fsdp", axis=0, tiled=True))
        whole = all_heads([part.T for part in held], head_dim).T
        d_out_weight = lax.dynamic_slice_in_dim(whole, chip * rows_out, rows_out, 0)
    return (
        block_out, d_tokens, d_norm_gain, d_in_weight, d_conv_weight, d_conv_bias, d_dt_bias, d_a_log,
        d_skip_gain, d_gate_gain, d_out_weight,
    )


def solution(mesh):
    rows = P(("rep", "fsdp"), None)
    in_specs = (
        rows, rows, P(), P("fsdp", None), P(), P(), P(), P(), P(), P(), P("fsdp", None), rows,
    )
    out_specs = (
        rows, rows, P(), P("fsdp", None), P(), P(), P(), P(), P(), P(), P("fsdp", None),
    )
    reps, chips = mesh.shape["rep"], mesh.shape["fsdp"]
    return jax.shard_map(
        functools.partial(per_device, reps, chips),
        mesh=mesh, in_specs=in_specs, out_specs=out_specs, check_vma=False,
    )
```
